256 devices in a mesh: tm: 8 (over x, core), clip: 32 (over z, y).
Axes of the slice: x: 4, y: 4, z: 8, core: 2. Of those that a mesh axis runs over, the one named last changes fastest.
Arguments:
- video: bfloat16 [16, 8192, 1152], P('tm', 'clip'), may hold values from -6 to 6
- cameras: int32 [32], P('clip'), may hold values from 4 to 8, as said below
- rays: float32 [6, 8192], P(None, 'clip'), may hold values from -6 to 6
- ray_weight: float32 [6, 1152], replicated, may hold values from -2.4 to 2.4
- modulation: bfloat16 [32, 6, 1152], P('clip'), may hold values from -3 to 3
- spatial_qkv: bfloat16 [1152, 3456], P('clip'), may hold values from -1 to 1
- spatial_out: bfloat16 [1152, 1152], P('clip'), may hold values from -0.1875 to 0.1875
- temporal_qkv: bfloat16 [1152, 3456], P('clip'), may hold values from -1 to 1
- temporal_out: bfloat16 [1152, 1152], P('clip'), may hold values from -0.1875 to 0.1875
Outputs:
- result: bfloat16 [16, 8192, 1152], P('tm', 'clip')
The draws below stay inside these ranges and needn't reach their ends.
Inputs may be any that keep to these rules, and one draw needn't show every extreme that they name: Clips 2k and 2k+1 hold 12 cameras together, for every k.
All inputs are finite; a program needn't handle non-finite values.
Results may differ from the reference program's by a relative error of at most 0.0085.
Values may be sent and summed in bfloat16 or wider, within the bound.
No kernel may reach another device: no remote copies, remote signals or barrier semaphores. Data moves between devices by JAX's collectives and lax.ppermute only.
A program may use at most 128 MiB of HBM per device.

```python
import jax
import jax.numpy as jnp
from jax import lax

D = 1152
HEAD = 72
HEADS = 16
HD = 1152
SLOTS = 8
PAIR = 12
PATCHES = 32
FRAMES = 16
CLIPS = 32


def draw_cameras(key, part):
    key = jax.random.fold_in(key, 5)
    key_lead, key_pick, key_order = jax.random.split(key, 3)
    pair_count = CLIPS // 2
    leading = jax.random.randint(key_lead, (pair_count,), PAIR - SLOTS, SLOTS + 1)
    chosen = jax.random.randint(key_pick, (), 0, pair_count)
    leading = jnp.where(jnp.arange(pair_count) == chosen, SLOTS, leading)
    swap_order = jax.random.randint(key_order, (pair_count,), 0, 2)
    first_clip = jnp.where(swap_order == 1, leading, PAIR - leading)
    return jnp.stack([first_clip, PAIR - first_clip], axis=1).reshape(CLIPS).astype(jnp.int32)


def draw_spatial_qkv(key, part):
    key = jax.random.fold_in(key, 11)
    drawn = jax.random.normal(key, (D, 3 * HEADS * HEAD), jnp.float32) * D ** (-0.5)
    return jnp.clip(drawn, -1.0, 1.0).astype(jnp.bfloat16)


def draw_temporal_qkv(key, part):
    key = jax.random.fold_in(key, 17)
    drawn = jax.random.normal(key, (D, 3 * HEADS * HEAD), jnp.float32) * D ** (-0.5)
    return jnp.clip(drawn, -1.0, 1.0).astype(jnp.bfloat16)


def level_of(key, dims, cuts, least, largest):
    level, own = 1.0, jax.random.fold_in(key, 6)
    for position, parts in cuts:
        steps = jnp.exp(jax.random.uniform(jax.random.fold_in(own, position), (parts,), jnp.float32, least / len(cuts), largest / len(cuts)))
        level = level * jnp.repeat(steps, dims[position] // parts).reshape([-1 if axis == position else 1 for axis in range(len(dims))])
    return level


def bell_draw(rng, extent, deviation, most, pieces=(), held_as=jnp.bfloat16):
    array = jax.random.normal(rng, extent, jnp.float32) * deviation
    if len(pieces) > 0:
        array = level_of(rng, extent, pieces, -0.22, 0.18) * array
    return jnp.clip(array, min=-most, max=most).astype(held_as)


def setup_inputs(seed: int = 0) -> dict:
    key_list = jax.random.split(jax.random.key(seed), 10)
    video = bell_draw(key_list[0], (FRAMES, CLIPS * SLOTS * PATCHES, D), 1.0, 6.0, ((0, 8), (1, 32)))
    cameras = draw_cameras(jax.random.fold_in(key_list[9], 71), 0)
    rays = bell_draw(key_list[2], (6, CLIPS * SLOTS * PATCHES), 1.0, 6.0, ((1, 32),), jnp.float32)
    ray_weight = bell_draw(key_list[3], (6, D), 0.4, 2.4, (), jnp.float32)
    modulation = bell_draw(key_list[4], (CLIPS, 6, D), 0.5, 3.0, ((0, 32),))
    spatial_qkv = draw_spatial_qkv(jax.random.fold_in(key_list[9], 71), 0)
    spatial_out = bell_draw(key_list[6], (HD, D), HD ** -0.5, 0.1875, ((0, 32),))
    temporal_qkv = draw_temporal_qkv(jax.random.fold_in(key_list[9], 71), 0)
    temporal_out = bell_draw(key_list[8], (HD, D), HD ** -0.5, 0.1875, ((0, 32),))
    return {"video": video, "cameras": cameras, "rays": rays, "ray_weight": ray_weight, "modulation": modulation, "spatial_qkv": spatial_qkv, "spatial_out": spatial_out, "temporal_qkv": temporal_qkv, "temporal_out": temporal_out}


epsilon = 1e-06

def normalize(values):
    center = lax.optimization_barrier(jnp.mean(values, axis=-1, keepdims=True))
    spread = lax.optimization_barrier(jnp.mean(jnp.square(values - center), axis=-1, keepdims=True))
    return (values - center) * lax.rsqrt(spread + epsilon)

def attend(queries, keys_in, values_in, alive_mask):
    scores = jnp.einsum('bqhe,bkhe->bhqk', queries.astype(jnp.float32), keys_in.astype(jnp.float32)) * HEAD ** (-0.5)
    if alive_mask is not None:
        scores = jnp.where(alive_mask[None, None, None, :], scores, -1e+30)
    row_max = lax.optimization_barrier(jnp.max(scores, axis=-1, keepdims=True))
    exponent = jnp.exp(scores - row_max)
    weights_soft = (exponent / lax.optimization_barrier(jnp.sum(exponent, axis=-1, keepdims=True))).astype(jnp.bfloat16)
    mixed_heads = jnp.einsum('bhqk,bkhe->bqhe', weights_soft.astype(jnp.float32), values_in.astype(jnp.float32))
    return mixed_heads.astype(jnp.bfloat16)

def reference(video, cameras, rays, ray_weight, modulation, spatial_qkv, spatial_out, temporal_qkv, temporal_out):
    slot_tokens = SLOTS * PATCHES
    head_width = HEADS * HEAD

    def one_clip(inputs):
        frames_in, camera_count, ray_block, modulate = inputs
        modulate = modulate.astype(jnp.float32)
        alive_mask = jnp.arange(slot_tokens) // PATCHES < camera_count
        ray_term = jnp.dot(ray_block.T, ray_weight, precision=lax.Precision.HIGHEST)
        hidden = frames_in.astype(jnp.float32) + ray_term[None]
        normed = (normalize(hidden) * (1.0 + modulate[1]) + modulate[0]).astype(jnp.bfloat16)
        packed = jnp.dot(normed.reshape(-1, D), spatial_qkv, preferred_element_type=jnp.float32).astype(jnp.bfloat16)
        packed = packed.reshape(FRAMES, slot_tokens, 3, HEADS, HEAD)
        mixed_heads = attend(packed[:, :, 0], packed[:, :, 1], packed[:, :, 2], alive_mask)
        projected = jnp.dot(mixed_heads.reshape(-1, head_width), spatial_out, preferred_element_type=jnp.float32)
        middle = (hidden + modulate[2] * projected.reshape(FRAMES, slot_tokens, D)).astype(jnp.bfloat16)
        normed_time = (normalize(middle.astype(jnp.float32)) * (1.0 + modulate[4]) + modulate[3]).astype(jnp.bfloat16)
        packed_time = jnp.dot(normed_time.reshape(-1, D), temporal_qkv, preferred_element_type=jnp.float32).astype(jnp.bfloat16)
        packed_time = jnp.transpose(packed_time.reshape(FRAMES, slot_tokens, 3, HEADS, HEAD), (1, 0, 2, 3, 4))
        mixed_time = attend(packed_time[:, :, 0], packed_time[:, :, 1], packed_time[:, :, 2], None)
        mixed_time = jnp.transpose(mixed_time, (1, 0, 2, 3))
        projected_time = jnp.dot(mixed_time.reshape(-1, head_width), temporal_out, preferred_element_type=jnp.float32)
        summed = middle.astype(jnp.float32) + modulate[5] * projected_time.reshape(FRAMES, slot_tokens, D)
        result = summed * alive_mask.astype(jnp.float32)[None, :, None]
        return result.astype(jnp.bfloat16)
    clips_video = jnp.transpose(video.reshape(FRAMES, CLIPS, slot_tokens, D), (1, 0, 2, 3))
    clip_rays = jnp.transpose(rays.reshape(6, CLIPS, slot_tokens), (1, 0, 2))
    outputs = lax.map(one_clip, (clips_video, cameras, clip_rays, modulation))
    return jnp.transpose(outputs, (1, 0, 2, 3)).reshape(FRAMES, CLIPS * slot_tokens, D)
```

```python
import functools

import jax
import jax.numpy as jnp
from jax import lax
from jax.experimental import pallas as pl
from jax.experimental.pallas import tpu as pltpu
from jax.sharding import PartitionSpec as P

D = 1152
HEAD = 72
HEADS = 16
PATCHES = 32
TOKENS = 256
ROWS = 36
XS = 4
ZS = 8
YS = 4
GROUP_HEADS = HEADS // XS
GROUP = GROUP_HEADS * HEAD
PAD = 384
HALF = 640
TQ = 1792
TQ_STEP = 1664
EPS = 1e-6
SOFT = HEAD ** (-0.5) * 1.4426950408889634
F32 = jnp.float32
BF16 = jnp.bfloat16
VMEM_LIMIT = 52 * 1024 * 1024


def z_send(a, s):
    pairs = [(z * YS + y, (z + s) % ZS * YS + y) for z in range(ZS) for y in range(YS)]
    return lax.ppermute(a, "clip", pairs)


def y_send(a, s):
    pairs = [(z * YS + y, z * YS + (y + s) % YS) for z in range(ZS) for y in range(YS)]
    return lax.ppermute(a, "clip", pairs)


def x_send(a, s):
    pairs = [(x * 2 + c, (x + s) % XS * 2 + c) for x in range(XS) for c in range(2)]
    return lax.ppermute(a, "tm", pairs)


def core_swap(a):
    return lax.ppermute(a, "tm", [(t, t ^ 1) for t in range(2 * XS)])


def tm_send(a, s):
    return lax.ppermute(a, "tm", [(t, (t + s) % (2 * XS)) for t in range(2 * XS)])


def in_order(pieces, me):
    n = len(pieces)
    back = pieces[::-1]
    both = jnp.stack(back + back[:-1])
    picked = lax.dynamic_slice_in_dim(both, n - 1 - me, n, axis=0)
    return picked.reshape(-1, pieces[0].shape[-1])


def attend(queries, keys, values_t, heads, masked):
    outs = []
    for h in range(heads):
        first, last = h * HEAD, h * HEAD + HEAD - 1
        lo, hi = first // 128 * 128, last // 128 * 128 + 128
        lane = lax.broadcasted_iota(jnp.int32, (1, hi - lo), 1) + lo
        own = jnp.logical_and(lane >= first, lane <= last)
        q = jnp.where(own, queries(lo, hi), jnp.zeros((), BF16))
        s = lax.dot_general(keys(lo, hi), q, (((1,), (1,)), ((), ())), preferred_element_type=F32)
        s = masked(s)
        m = jnp.max(s, axis=0, keepdims=True)
        e = jnp.exp2((s - m) * SOFT)
        total = jnp.sum(e, axis=0, keepdims=True)
        start = first // 16 * 16
        o = jnp.dot(values_t(start, start + 80), e.astype(BF16), preferred_element_type=F32)
        o = o * (1.0 / total)
        outs.append(o[first - start : first - start + HEAD])
    return jnp.concatenate(outs, axis=0)


def normalize(h, scale, shift):
    center = jnp.mean(h, axis=-1, keepdims=True)
    d = h - center
    spread = jnp.mean(d * d, axis=-1, keepdims=True)
    return (d * lax.rsqrt(spread + EPS) * scale + shift).astype(BF16)


def ray_sum(rays, weight):
    total = rays[:, 0:1] * weight[0:1, :]
    for k in range(1, 6):
        total += rays[:, k : k + 1] * weight[k : k + 1, :]
    return total


def spatial_kernel(parts, *refs):
    info, rays, ray_weight, mod, w_own, w_sib = refs[:6]
    videos = refs[6 : 6 + len(parts)]
    outs = refs[6 + len(parts) : 14 + len(parts)]
    ray, wp, normed, q2, ks, vt, of = refs[14 + len(parts) :]
    t, core, cameras = info[0], info[1], info[3]

    @pl.when(core == 0)
    def _():
        wp[:, 0:HALF] = w_own[...]
        wp[:, HALF:] = w_sib[:, 128:HALF]

    @pl.when(core == 1)
    def _():
        wp[:, 0:HALF] = w_sib[...]
        wp[:, HALF:] = w_own[:, 128:HALF]

    ray[...] = ray_sum(rays[...], ray_weight[...])
    scale = 1.0 + mod[1:2, :]
    shift = mod[0:1, :]
    limit = cameras * PATCHES
    alive = lax.broadcasted_iota(jnp.int32, (TOKENS, TOKENS), 0) < limit

    frames = [(v, f) for v, n in zip(videos, parts) for f in range(n)]
    for slot, (video, frame) in enumerate(frames):

        def rows_body(r, carry, video=video, frame=frame):
            rows = pl.ds(pl.multiple_of(r * 32, 32), 32)
            h = video[frame, rows, :].astype(F32) + ray[rows, :]
            normed[rows, :] = normalize(h, scale, shift)
            return carry

        lax.fori_loop(0, TOKENS // 32, rows_body, 0)
        packed = jnp.dot(normed[...], wp[...], preferred_element_type=F32)
        q = packed[:, 0:PAD].astype(BF16)
        q2[0:TOKENS, :] = q
        q2[TOKENS:, :] = q
        ks[...] = packed[:, PAD : 2 * PAD].astype(BF16)
        vt[...] = jnp.transpose(packed[:, 2 * PAD :]).astype(BF16)
        rotated = pl.ds(pl.multiple_of(t * PATCHES, PATCHES), TOKENS)
        of[slot] = attend(
            lambda lo, hi: q2[rotated, lo:hi],
            lambda lo, hi: ks[:, lo:hi],
            lambda lo, hi: vt[lo:hi, :],
            GROUP_HEADS,
            lambda s: jnp.where(alive, s, -1e30),
        )

    block = lax.broadcasted_iota(jnp.int32, (GROUP, 128), 1) // PATCHES
    for i in range(8):
        unit, place = i // 4, i % 4
        made = None
        for f in range(4):
            a = of[f, :, unit * 128 : unit * 128 + 128]
            by = (f - place) * PATCHES % 128
            if by:
                a = pltpu.roll(a, by, 1)
            made = a if made is None else jnp.where(block == f, a, made)
        outs[i][...] = made.astype(BF16)


def spatial(parts, info, rays, ray_weight, mod, w_own, w_sib, videos):
    vmem = pl.BlockSpec(memory_space=pltpu.VMEM)
    frames = sum(parts)
    return pl.pallas_call(
        functools.partial(spatial_kernel, parts),
        out_shape=[jax.ShapeDtypeStruct((GROUP, 128), BF16)] * 8,
        in_specs=[pl.BlockSpec(memory_space=pltpu.SMEM)] + [vmem] * (5 + len(parts)),
        out_specs=[vmem] * 8,
        scratch_shapes=[
            pltpu.VMEM((TOKENS, D), F32),
            pltpu.VMEM((D, 3 * PAD), BF16),
            pltpu.VMEM((TOKENS, D), BF16),
            pltpu.VMEM((2 * TOKENS, PAD), BF16),
            pltpu.VMEM((TOKENS, PAD), BF16),
            pltpu.VMEM((PAD, TOKENS), BF16),
            pltpu.VMEM((4, GROUP, TOKENS), F32),
        ],
        compiler_params=pltpu.CompilerParams(vmem_limit_bytes=VMEM_LIMIT),
        cost_estimate=pl.CostEstimate(
            flops=frames * 2 * TOKENS * D * 3 * PAD, bytes_accessed=8_000_000, transcendentals=frames * 4 * 65536
        ),
    )(info, rays, ray_weight, mod, w_own, w_sib, *videos)


def place_kernel(info, *refs):
    pieces, out = refs[:9], refs[9]
    z = info[4]
    block = YS * ROWS
    for s, piece in enumerate(pieces[:7]):
        shift = s if s < 4 else s - 3
        source = lax.rem(z + (ZS - shift if s < 4 else shift), ZS)
        out[pl.ds(pl.multiple_of(source * block, block), block), :] = piece[...]
    far = lax.rem(z + 4, ZS) * block
    out[pl.ds(pl.multiple_of(far, 16), 80), :] = pieces[7][...]
    out[pl.ds(pl.multiple_of(far + 80, 16), 64), :] = pieces[8][...]


def place(info, pieces):
    vmem = pl.BlockSpec(memory_space=pltpu.VMEM)
    return pl.pallas_call(
        place_kernel,
        out_shape=jax.ShapeDtypeStruct((D, HALF), BF16),
        in_specs=[pl.BlockSpec(memory_space=pltpu.SMEM)] + [vmem] * 9,
        out_specs=vmem,
        compiler_params=pltpu.CompilerParams(vmem_limit_bytes=VMEM_LIMIT),
        cost_estimate=pl.CostEstimate(flops=0, bytes_accessed=4_000_000, transcendentals=0),
    )(info, *pieces)


def temporal_kernel(*refs):
    info, rays, ray_weight, mod, v_own, v_sib = refs[:6]
    early, late = refs[6:14], refs[14:22]
    out_own, out_sib, order = refs[22:25]
    t_own, t_sib = refs[25:30], refs[30:35]
    outs = refs[35:43]
    (wo, wq, perm, mix_t, proj, mid, normed, packed, vt, bias, sem_o, sem_p, sem_q) = refs[43:]
    t, core, x, cameras, y = info[0], info[1], info[2], info[3], info[5]
    other = 1 - core

    out_copies = [
        pltpu.make_async_copy(out_own, wo.at[core], sem_o.at[0]),
        pltpu.make_async_copy(out_sib, wo.at[other], sem_o.at[1]),
    ]
    perm_copy = pltpu.make_async_copy(order, perm, sem_p)
    q_copies = []
    span = ZS * ROWS
    up, down, far = lax.rem(y + 3, YS), lax.rem(y + 1, YS), lax.rem(y + 2, YS)
    starts = [y * span, up * span, down * span, far * span, far * span + span // 2]
    sizes = [span, span, span, span // 2, span // 2]
    for which, pieces in ((core, t_own), (other, t_sib)):
        for start, size, piece in zip(starts, sizes, pieces):
            q_copies.append(
                pltpu.make_async_copy(
                    piece, wq.at[which, pl.ds(pl.multiple_of(start, 16), size)], sem_q.at[len(q_copies)]
                )
            )
    for copy in out_copies + [perm_copy] + q_copies:
        copy.start()

    for i in range(8):
        source = lax.rem(t + 8 - i, 8)
        sx, sc = source // 2, lax.rem(source, 2)
        both = jnp.concatenate([early[i][...], late[i][...]], axis=1).astype(F32)
        turned = pltpu.roll(both, sx * 64, 1)
        mix_t[sc, pl.ds(pl.multiple_of(sx * GROUP, 16), GROUP), :] = turned.astype(BF16)
    same = (
        lax.broadcasted_iota(jnp.int32, (TOKENS, TOKENS), 0) % 16
        == lax.broadcasted_iota(jnp.int32, (TOKENS, TOKENS), 1) % 16
    )
    bias[...] = jnp.where(same, 0.0, -1e30)
    for copy in out_copies:
        copy.wait()

    def project(half, first):
        mixed = mix_t[half]
        w0 = wo[0, :, first : first + HALF]
        w1 = wo[1, :, first + 128 : first + HALF]
        rows = slice(half * TOKENS, half * TOKENS + TOKENS)
        dims = (((0,), (0,)), ((), ()))
        proj[rows, 0:HALF] = lax.dot_general(mixed, w0, dims, preferred_element_type=F32)
        proj[rows, HALF:] = lax.dot_general(mixed, w1, dims, preferred_element_type=F32)

    for half in range(2):
        project(half, 0)

    here = rays[pl.ds(pl.multiple_of(t * PATCHES, PATCHES), PATCHES), :]
    ray = ray_sum(here, ray_weight[...])
    gate, shift, scale = mod[2:3, :], mod[3:4, :], 1.0 + mod[4:5, :]

    def slab(k, carry):
        j, f = k // 2, lax.rem(k, 2)
        frame_pair = lax.rem(x + j, XS)
        for which, video in ((core, v_own), (other, v_sib)):
            n = which * 8 + frame_pair * 2 + f
            h = video[k].astype(F32) + ray
            p = proj[pl.ds(pl.multiple_of(n * PATCHES, PATCHES), PATCHES), :]
            middle = (h + gate * p).astype(BF16)
            norm = normalize(middle.astype(F32), scale, shift)
            low = pl.ds(pl.multiple_of(n * 16, 16), 16)
            high = pl.ds(pl.multiple_of(TOKENS + n * 16, 16), 16)
            mid[low, :] = middle[0:16]
            mid[high, :] = middle[16:32]
            normed[low, :] = norm[0:16]
            normed[high, :] = norm[16:32]
        return carry

    lax.fori_loop(0, 8, slab, 0)
    perm_copy.wait()
    turned = jnp.dot(normed[...], perm[...], preferred_element_type=F32).astype(BF16)
    normed[...] = turned
    for copy in q_copies:
        copy.wait()
    for half in range(2):

        def column(n, carry, half=half):
            lanes = pl.ds(pl.multiple_of(n * 256, 256), 256)
            to = pl.ds(pl.multiple_of(n * 256 + half * TQ_STEP, 128), 256)
            packed[:, to] = jnp.dot(normed[...], wq[half, :, lanes], preferred_element_type=F32).astype(BF16)
            return carry

        lax.fori_loop(0, TQ // 256, column, 0)
    for g in range(2):
        rows = slice(g * TOKENS, g * TOKENS + TOKENS)
        vt[...] = jnp.transpose(packed[rows, 2 * D :])
        mix_t[g] = attend(
            lambda lo, hi: packed[rows, lo:hi],
            lambda lo, hi: packed[rows, D + lo : D + hi],
            lambda lo, hi: vt[lo:hi, :],
            HEADS,
            lambda s: s + bias[...],
        ).astype(BF16)
        project(g, HALF)
    alive = jnp.where(t < cameras, 1.0, 0.0)
    last_gate = mod[5:6, :]

    def finish(n, carry):
        rows = pl.ds(pl.multiple_of(n * 32, 32), 32)
        summed = mid[rows, :].astype(F32) + last_gate * proj[rows, :]
        mid[rows, :] = (summed * alive).astype(BF16)
        return carry

    lax.fori_loop(0, 16, finish, 0)
    for i in range(8):
        target = lax.rem(t + i, 8)
        first = lax.rem(target, 2) * 8 + target // 2 * 2
        for f in range(2):
            n = first + f
            outs[i][f, 0:16, :] = mid[pl.ds(pl.multiple_of(n * 16, 16), 16), :]
            outs[i][f, 16:32, :] = mid[pl.ds(pl.multiple_of(TOKENS + n * 16, 16), 16), :]


def temporal(info, rays, ray_weight, mod, v_own, v_sib, early, late, out_own, out_sib, order, t_own, t_sib):
    vmem = pl.BlockSpec(memory_space=pltpu.VMEM)
    far = pl.BlockSpec(memory_space=pl.ANY)
    return pl.pallas_call(
        temporal_kernel,
        out_shape=[jax.ShapeDtypeStruct((2, PATCHES, D), BF16)] * 8,
        in_specs=[pl.BlockSpec(memory_space=pltpu.SMEM)] + [vmem] * 21 + [far] * 13,
        out_specs=[vmem] * 8,
        scratch_shapes=[
            pltpu.VMEM((2, D, 2 * HALF), BF16),
            pltpu.VMEM((2, D, TQ), BF16),
            pltpu.VMEM((D, D), BF16),
            pltpu.VMEM((2, D, TOKENS), BF16),
            pltpu.VMEM((2 * TOKENS, D), F32),
            pltpu.VMEM((2 * TOKENS, D), BF16),
            pltpu.VMEM((2 * TOKENS, D), BF16),
            pltpu.VMEM((2 * TOKENS, 3 * D), BF16),
            pltpu.VMEM((D, TOKENS), BF16),
            pltpu.VMEM((TOKENS, TOKENS), F32),
            pltpu.SemaphoreType.DMA((2,)),
            pltpu.SemaphoreType.DMA,
            pltpu.SemaphoreType.DMA((10,)),
        ],
        compiler_params=pltpu.CompilerParams(vmem_limit_bytes=VMEM_LIMIT),
        cost_estimate=pl.CostEstimate(flops=16_000_000_000, bytes_accessed=24_000_000, transcendentals=2_100_000),
    )(info, rays, ray_weight, mod, v_own, v_sib, *early, *late, out_own, out_sib, order, *t_own, *t_sib)


def join_kernel(info, *refs):
    pieces, out = refs[:8], refs[8]
    t = info[0]
    for i, piece in enumerate(pieces):
        source = lax.rem(t + 8 - i, 8)
        out[:, pl.ds(pl.multiple_of(source * PATCHES, PATCHES), PATCHES), :] = piece[...]


def join(info, pieces):
    vmem = pl.BlockSpec(memory_space=pltpu.VMEM)
    return pl.pallas_call(
        join_kernel,
        out_shape=jax.ShapeDtypeStruct((2, TOKENS, D), BF16),
        in_specs=[pl.BlockSpec(memory_space=pltpu.SMEM)] + [vmem] * 8,
        out_specs=vmem,
        compiler_params=pltpu.CompilerParams(vmem_limit_bytes=VMEM_LIMIT),
        cost_estimate=pl.CostEstimate(flops=0, bytes_accessed=2_400_000, transcendentals=0),
    )(info, *pieces)


def on_device(
    video,
    cameras,
    rays,
    ray_weight,
    modulation,
    spatial_qkv,
    spatial_out,
    temporal_qkv,
    temporal_out,
):
    t = lax.axis_index("tm")
    clip = lax.axis_index("clip")
    x, core = t // 2, t % 2
    z, y = clip // YS, clip % YS
    info = jnp.stack([t, core, x, cameras[0], z, y]).astype(jnp.int32)
    mod = modulation[0].astype(F32)
    rays_t = rays.T

    def columns(a, start, size):
        return lax.dynamic_slice_in_dim(a, start, size, axis=1)

    x_up = x_send(video, 1)
    x_down = x_send(video, -1)

    heads = [jnp.pad(columns(spatial_qkv, k * D + x * GROUP, GROUP), ((0, 0), (0, PAD - GROUP))) for k in range(3)]
    first = jnp.concatenate(
        [
            columns(jnp.concatenate(heads, axis=1), core * (HALF - 128), HALF),
            columns(spatial_out, core * (HALF - 128), HALF),
            columns(temporal_out, core * (HALF - 128), HALF),
        ],
        axis=1,
    )
    rows = in_order([first, y_send(first, 1), y_send(first, 2), y_send(first, 3)], y)
    a, b = rows[:, :HALF], rows[:, HALF:]
    up, down = [a], [a]
    for _ in range(3):
        up.append(z_send(up[-1], 1))
        down.append(z_send(down[-1], -1))
    far_up = z_send(up[-1][:80], 1)
    far_down = z_send(down[-1][80:], -1)
    w_own = place(info, up + down[1:] + [far_up, far_down])
    w_sib = core_swap(w_own)
    zgroups = [[zz * YS + yy for zz in range(ZS)] for yy in range(YS)]
    out_own = lax.all_gather(b, "clip", axis=0, tiled=True, axis_index_groups=zgroups)
    out_sib = core_swap(out_own)

    tq = columns(temporal_qkv, core * TQ_STEP, TQ)
    own = in_order([tq] + [z_send(tq, s) for s in range(1, ZS)], z)
    y_up, y_down = y_send(own, 1), y_send(own, -1)
    half = ZS * ROWS // 2
    y_far_up = y_send(y_up[:half], 1)
    y_far_down = y_send(y_down[half:], -1)
    t_own = [own, y_up, y_down, y_far_up, y_far_down]
    t_sib = [core_swap(p) for p in t_own]

    x_far_up = x_send(x_up[0:1], 1)
    x_far_down = x_send(x_down[1:2], -1)

    early = spatial((2, 2), info, rays_t, ray_weight, mod, w_own, w_sib, [video, x_down])
    early = [early[0]] + [tm_send(early[i], i) for i in range(1, 8)]
    late = spatial((1, 1, 2), info, rays_t, ray_weight, mod, w_own, w_sib, [x_far_up, x_far_down, x_up])
    late = [late[0]] + [tm_send(late[i], i) for i in range(1, 8)]

    def cut(who):
        parts = [video, x_down, x_far_up, x_far_down, x_up]
        return jnp.concatenate([lax.dynamic_slice_in_dim(p, who * PATCHES, PATCHES, axis=1) for p in parts], axis=0)

    v_own = cut(t)
    v_sib = core_swap(cut(t + 1 - 2 * core))

    k = jnp.arange(D)
    goes = k // (ZS * ROWS) * ROWS + k // ROWS % ZS * (YS * ROWS) + k % ROWS
    order = (k[:, None] == goes[None, :]).astype(BF16)
    pieces = temporal(info, rays_t, ray_weight, mod, v_own, v_sib, early, late, out_own, out_sib, order, t_own, t_sib)
    return join(info, [pieces[0]] + [tm_send(pieces[i], i) for i in range(1, 8)])


def solution(mesh):
    placed = (
        P("tm", "clip", None),
        P("clip"),
        P(None, "clip"),
        P(),
        P("clip", None, None),
        P("clip", None),
        P("clip", None),
        P("clip", None),
        P("clip", None),
    )
    return jax.shard_map(
        on_device, mesh=mesh, in_specs=placed, out_specs=P("tm", "clip", None), check_vma=False
    )
```

```python
import functools

import jax
import jax.numpy as jnp
import numpy as np
from jax import lax
from jax.experimental import pallas as pl
from jax.experimental.pallas import tpu as pltpu
from jax.sharding import PartitionSpec as P

D = 1152
HEAD = 72
HEADS = 16
PATCHES = 32
TOKENS = 256
ROWS = 36
XS = 4
ZS = 8
YS = 4
GROUP_HEADS = HEADS // XS
GROUP = GROUP_HEADS * HEAD
PAD = 384
HALF = 640
TQ = 1792
TQ_STEP = 1664
EPS = 1e-6
SOFT = HEAD ** (-0.5) * 1.4426950408889634
F32 = jnp.float32
BF16 = jnp.bfloat16
VMEM_LIMIT = 52 * 1024 * 1024


def z_send(a, s):
    pairs = [(z * YS + y, (z + s) % ZS * YS + y) for z in range(ZS) for y in range(YS)]
    return lax.ppermute(a, "clip", pairs)


def y_send(a, s):
    pairs = [(z * YS + y, z * YS + (y + s) % YS) for z in range(ZS) for y in range(YS)]
    return lax.ppermute(a, "clip", pairs)


def x_send(a, s):
    pairs = [(x * 2 + c, (x + s) % XS * 2 + c) for x in range(XS) for c in range(2)]
    return lax.ppermute(a, "tm", pairs)


def core_swap(a):
    return lax.ppermute(a, "tm", [(t, t ^ 1) for t in range(2 * XS)])


def in_order(pieces, me):
    n = len(pieces)
    back = pieces[::-1]
    both = jnp.stack(back + back[:-1])
    picked = lax.dynamic_slice_in_dim(both, n - 1 - me, n, axis=0)
    return picked.reshape(-1, pieces[0].shape[-1])


def attend(queries, keys, values_t, heads, masked, held, soft, inverse):
    for h in range(heads):
        first, last = h * HEAD, h * HEAD + HEAD - 1
        lo, hi = first // 128 * 128, last // 128 * 128 + 128
        lane = lax.broadcasted_iota(jnp.int32, (1, hi - lo), 1) + lo
        own = jnp.logical_and(lane >= first, lane <= last)
        q = jnp.where(own, queries(lo, hi), jnp.zeros((), BF16))
        held[h] = lax.dot_general(keys(lo, hi), q, (((1,), (1,)), ((), ())), preferred_element_type=F32)
    for h in range(heads):
        s = masked(held[h])
        m = jnp.max(s, axis=0, keepdims=True)
        e = jnp.exp2((s - m) * SOFT)
        inverse[h] = 1.0 / jnp.sum(e, axis=0, keepdims=True)
        soft[h] = e.astype(BF16)
    outs = []
    for h in range(heads):
        first = h * HEAD
        start = first // 16 * 16
        o = jnp.dot(values_t(start, start + 80), soft[h], preferred_element_type=F32) * inverse[h]
        outs.append(o[first - start : first - start + HEAD])
    return jnp.concatenate(outs, axis=0)


def normalize(h, scale, shift):
    center = jnp.mean(h, axis=-1, keepdims=True)
    d = h - center
    spread = jnp.mean(d * d, axis=-1, keepdims=True)
    return (d * lax.rsqrt(spread + EPS) * scale + shift).astype(BF16)


def ray_sum(rays, weight):
    total = rays[:, 0:1] * weight[0:1, :]
    for k in range(1, 6):
        total += rays[:, k : k + 1] * weight[k : k + 1, :]
    return total


def spatial_kernel(parts, *refs):
    info, rays, ray_weight, mod, w_own, w_sib = refs[:6]
    videos = refs[6 : 6 + len(parts)]
    out = refs[6 + len(parts)]
    ray, wp, sems, normed, packed, vt, of, held, soft, inverse = refs[7 + len(parts) :]
    core, cameras = info[1], info[3]

    def copies(left, right):
        return [
            pltpu.make_async_copy(left, wp.at[:, 0:HALF], sems.at[0]),
            pltpu.make_async_copy(right.at[:, 128:HALF], wp.at[:, HALF:], sems.at[1]),
        ]

    @pl.when(core == 0)
    def _():
        for copy in copies(w_own, w_sib):
            copy.start()

    @pl.when(core == 1)
    def _():
        for copy in copies(w_sib, w_own):
            copy.start()

    ray[...] = ray_sum(rays[...], ray_weight[...])
    scale = 1.0 + mod[1:2, :]
    shift = mod[0:1, :]
    alive = lax.broadcasted_iota(jnp.int32, (TOKENS, TOKENS), 0) < cameras * PATCHES

    frames = [(v, f) for v, n in zip(videos, parts) for f in range(n)]

    def norm_frame(slot):
        video, frame = frames[slot]
        for r in range(TOKENS // 32):
            rows = slice(r * 32, r * 32 + 32)
            h = video[frame, rows, :].astype(F32) + ray[rows, :]
            normed[slot % 2, rows, :] = normalize(h, scale, shift)

    norm_frame(0)
    for copy in copies(w_own, w_sib):
        copy.wait()
    for slot in range(4):
        turn = slot % 2
        made = jnp.dot(normed[turn], wp[...], preferred_element_type=F32)
        packed[turn] = made[:, : 2 * PAD].astype(BF16)
        vt[turn] = jnp.transpose(made[:, 2 * PAD :]).astype(BF16)
        if slot < 3:
            norm_frame(slot + 1)
        of[slot] = attend(
            lambda lo, hi: packed[turn, :, lo:hi],
            lambda lo, hi: packed[turn, :, PAD + lo : PAD + hi],
            lambda lo, hi: vt[turn, lo:hi, :],
            GROUP_HEADS,
            lambda s: jnp.where(alive, s, -1e30),
            held.at[turn],
            soft.at[turn],
            inverse.at[turn],
        )

    block = lax.broadcasted_iota(jnp.int32, (GROUP, 128), 1) // PATCHES
    for i in range(8):
        unit, place = i // 4, i % 4
        made = None
        for f in range(4):
            a = of[f, :, unit * 128 : unit * 128 + 128]
            by = (f - place) * PATCHES % 128
            if by:
                a = pltpu.roll(a, by, 1)
            made = a if made is None else jnp.where(block == f, a, made)
        out[i] = made.astype(BF16)


def spatial(parts, info, rays, ray_weight, mod, w_own, w_sib, videos):
    vmem = pl.BlockSpec(memory_space=pltpu.VMEM)
    far = pl.BlockSpec(memory_space=pl.ANY)
    frames = sum(parts)
    return pl.pallas_call(
        functools.partial(spatial_kernel, parts),
        out_shape=jax.ShapeDtypeStruct((8, GROUP, 128), BF16),
        in_specs=[pl.BlockSpec(memory_space=pltpu.SMEM)] + [vmem] * 3 + [far] * 2 + [vmem] * len(parts),
        out_specs=vmem,
        scratch_shapes=[
            pltpu.VMEM((TOKENS, D), F32),
            pltpu.VMEM((D, 3 * PAD), BF16),
            pltpu.SemaphoreType.DMA((2,)),
            pltpu.VMEM((2, TOKENS, D), BF16),
            pltpu.VMEM((2, TOKENS, 2 * PAD), BF16),
            pltpu.VMEM((2, PAD, TOKENS), BF16),
            pltpu.VMEM((4, GROUP, TOKENS), F32),
            pltpu.VMEM((2, GROUP_HEADS, TOKENS, TOKENS), F32),
            pltpu.VMEM((2, GROUP_HEADS, TOKENS, TOKENS), BF16),
            pltpu.VMEM((2, GROUP_HEADS, 1, TOKENS), F32),
        ],
        compiler_params=pltpu.CompilerParams(vmem_limit_bytes=VMEM_LIMIT),
        cost_estimate=pl.CostEstimate(
            flops=frames * 2 * TOKENS * D * 3 * PAD, bytes_accessed=8_000_000, transcendentals=frames * 4 * 65536
        ),
    )(info, rays, ray_weight, mod, w_own, w_sib, *videos)


def place_kernel(info, *refs):
    pieces, out = refs[:9], refs[9]
    z = info[4]
    block = YS * ROWS
    for s, piece in enumerate(pieces[:7]):
        shift = s if s < 4 else s - 3
        source = lax.rem(z + (ZS - shift if s < 4 else shift), ZS)
        out[pl.ds(pl.multiple_of(source * block, block), block), :] = piece[...]
    far = lax.rem(z + 4, ZS) * block
    out[pl.ds(pl.multiple_of(far, 16), 80), :] = pieces[7][...]
    out[pl.ds(pl.multiple_of(far + 80, 16), 64), :] = pieces[8][...]


def place(info, pieces):
    vmem = pl.BlockSpec(memory_space=pltpu.VMEM)
    return pl.pallas_call(
        place_kernel,
        out_shape=jax.ShapeDtypeStruct((D, HALF), BF16),
        in_specs=[pl.BlockSpec(memory_space=pltpu.SMEM)] + [vmem] * 9,
        out_specs=vmem,
        compiler_params=pltpu.CompilerParams(vmem_limit_bytes=VMEM_LIMIT),
        cost_estimate=pl.CostEstimate(flops=0, bytes_accessed=4_000_000, transcendentals=0),
    )(info, *pieces)


def temporal_kernel(
    info, rays, ray_weight, mod, v_own, v_sib, early, late, s_own, s_sib, o_own, o_sib, order, t_own, t_sib,
    out, wq, wo, perm, mix_t, proj, mid, normed, packed, vt, bias, held, soft, inverse, sems,
):
    t, core, x, cameras = info[0], info[1], info[2], info[3]
    other = 1 - core
    perm_copy = pltpu.make_async_copy(order, perm, sems.at[0])
    q_copies = [
        pltpu.make_async_copy(t_own, wq.at[0], sems.at[1]),
        pltpu.make_async_copy(t_sib, wq.at[1], sems.at[2]),
    ]
    out_copies = [
        pltpu.make_async_copy(o_own, wo.at[0], sems.at[3]),
        pltpu.make_async_copy(o_sib, wo.at[1], sems.at[4]),
    ]
    for copy in [perm_copy] + q_copies + out_copies:
        copy.start()

    for source in range(8):
        sx, sc = source // 2, source % 2
        both = jnp.concatenate([early[source], late[source]], axis=1)
        if sx:
            both = pltpu.roll(both.astype(F32), sx * 64, 1).astype(BF16)
        mix_t[sc, sx * GROUP : sx * GROUP + GROUP, :] = both
    key = lax.broadcasted_iota(jnp.int32, (128, 128), 0)
    query = lax.broadcasted_iota(jnp.int32, (128, 128), 1)
    bias[...] = jnp.where(key % 8 == query % 8, 0.0, -1e30)

    def project(half, weights):
        mixed = mix_t[half]
        rows = slice(half * TOKENS, half * TOKENS + TOKENS)
        dims = (((0,), (0,)), ((), ()))
        for which, w in zip((core, other), weights):
            to = pl.ds(pl.multiple_of(which * (HALF - 128), 128), HALF)
            proj[rows, to] = lax.dot_general(mixed, w[...], dims, preferred_element_type=F32)

    for half in range(2):
        project(half, (s_own, s_sib))

    here = rays[pl.ds(pl.multiple_of(t * PATCHES, PATCHES), PATCHES), :]
    ray = ray_sum(here, ray_weight[...])
    gate, shift, scale = mod[2:3, :], mod[3:4, :], 1.0 + mod[4:5, :]

    def slab(j, which, video):
        pair = which * 4 + lax.rem(x + j, XS)
        middles, norms = [], []
        for f in range(2):
            h = video[2 * j + f].astype(F32) + ray
            p = proj[pl.ds(pl.multiple_of(pair * 64 + f * PATCHES, PATCHES), PATCHES), :]
            middle = (h + gate * p).astype(BF16).astype(F32)
            middles.append(middle)
            norms.append(normalize(middle, scale, shift).astype(F32))
        for g in range(4):
            rows = pl.ds(pl.multiple_of(g * 128 + pair * 16, 16), 16)
            cut = slice(g * 8, g * 8 + 8)
            mid[rows, :] = jnp.concatenate([m[cut] for m in middles], axis=0).astype(BF16)
            normed[rows, :] = jnp.concatenate([m[cut] for m in norms], axis=0).astype(BF16)

    for j in range(4):
        slab(j, core, v_own)
        slab(j, other, v_sib)
    perm_copy.wait()
    normed[...] = jnp.dot(normed[...], perm[...], preferred_element_type=F32).astype(BF16)
    for which, copy in ((core, q_copies[0]), (other, q_copies[1])):
        copy.wait()
        w = wq.at[0] if copy is q_copies[0] else wq.at[1]
        for n in range(TQ // 256):
            to = pl.ds(pl.multiple_of(which * TQ_STEP + n * 256, 128), 256)
            made = jnp.dot(normed[...], w[:, n * 256 : n * 256 + 256], preferred_element_type=F32)
            packed[:, to] = made.astype(BF16)
    for copy in out_copies:
        copy.wait()
    for half in range(2):
        for g in (2 * half, 2 * half + 1):
            rows = slice(g * 128, g * 128 + 128)
            vt[g] = jnp.transpose(packed[rows, 2 * D :])
            lanes = slice((g % 2) * 128, (g % 2) * 128 + 128)
            mix_t[half, :, lanes] = attend(
                lambda lo, hi: packed[rows, lo:hi],
                lambda lo, hi: packed[rows, D + lo : D + hi],
                lambda lo, hi: vt[g, lo:hi, :],
                HEADS,
                lambda s: s + bias[...],
                held.at[g],
                soft.at[g],
                inverse.at[g],
            ).astype(BF16)
        project(half, (wo.at[0], wo.at[1]))
    alive = jnp.where(t < cameras, 1.0, 0.0)
    last_gate = mod[5:6, :]
    for target in range(8):
        pair = target % 2 * 4 + target // 2
        for g in range(4):
            rows = slice(g * 128 + pair * 16, g * 128 + pair * 16 + 16)
            done = (mid[rows, :].astype(F32) + last_gate * proj[rows, :]) * alive
            for f in range(2):
                out[target, f, g * 8 : g * 8 + 8, :] = done[f * 8 : f * 8 + 8].astype(BF16)


def temporal(info, rays, ray_weight, mod, v_own, v_sib, early, late, s_own, s_sib, o_own, o_sib, order, t_own, t_sib):
    vmem = pl.BlockSpec(memory_space=pltpu.VMEM)
    far = pl.BlockSpec(memory_space=pl.ANY)
    return pl.pallas_call(
        temporal_kernel,
        out_shape=jax.ShapeDtypeStruct((8, 2, PATCHES, D), BF16),
        in_specs=[pl.BlockSpec(memory_space=pltpu.SMEM)] + [vmem] * 9 + [far] * 5,
        out_specs=vmem,
        scratch_shapes=[
            pltpu.VMEM((2, D, TQ), BF16),
            pltpu.VMEM((2, D, HALF), BF16),
            pltpu.VMEM((D, D), BF16),
            pltpu.VMEM((2, D, TOKENS), BF16),
            pltpu.VMEM((2 * TOKENS, D), F32),
            pltpu.VMEM((2 * TOKENS, D), BF16),
            pltpu.VMEM((2 * TOKENS, D), BF16),
            pltpu.VMEM((2 * TOKENS, 3 * D), BF16),
            pltpu.VMEM((4, D, 128), BF16),
            pltpu.VMEM((128, 128), F32),
            pltpu.VMEM((4, HEADS, 128, 128), F32),
            pltpu.VMEM((4, HEADS, 128, 128), BF16),
            pltpu.VMEM((4, HEADS, 1, 128), F32),
            pltpu.SemaphoreType.DMA((5,)),
        ],
        compiler_params=pltpu.CompilerParams(vmem_limit_bytes=VMEM_LIMIT),
        cost_estimate=pl.CostEstimate(flops=16_000_000_000, bytes_accessed=24_000_000, transcendentals=2_100_000),
    )(info, rays, ray_weight, mod, v_own, v_sib, early, late, s_own, s_sib, o_own, o_sib, order, t_own, t_sib)


def on_device(
    video,
    cameras,
    rays,
    ray_weight,
    modulation,
    spatial_qkv,
    spatial_out,
    temporal_qkv,
    temporal_out,
):
    t = lax.axis_index("tm")
    clip = lax.axis_index("clip")
    x, core = t // 2, t % 2
    z, y = clip // YS, clip % YS
    info = jnp.stack([t, core, x, cameras[0], z, y]).astype(jnp.int32)
    mod = modulation[0].astype(F32)
    rays_t = rays.T

    def columns(a, start, size):
        return lax.dynamic_slice_in_dim(a, start, size, axis=1)

    x_up = x_send(video, 1)
    x_down = x_send(video, -1)

    zgroups = [[zz * YS + yy for zz in range(ZS)] for yy in range(YS)]
    ygroups = [[zz * YS + yy for yy in range(YS)] for zz in range(ZS)]
    tq = columns(temporal_qkv, core * TQ_STEP, TQ)
    tq = lax.all_gather(tq, "clip", axis=0, tiled=True, axis_index_groups=zgroups)
    t_own = lax.all_gather(tq, "clip", axis=0, tiled=True, axis_index_groups=ygroups)
    t_sib = core_swap(t_own)

    heads = [jnp.pad(columns(spatial_qkv, k * D + x * GROUP, GROUP), ((0, 0), (0, PAD - GROUP))) for k in range(3)]
    first = jnp.concatenate(
        [
            columns(jnp.concatenate(heads, axis=1), core * (HALF - 128), HALF),
            columns(spatial_out, core * (HALF - 128), HALF),
            columns(temporal_out, core * (HALF - 128), HALF),
        ],
        axis=1,
    )
    rows = in_order([first, y_send(first, 1), y_send(first, 2), y_send(first, 3)], y)
    a, b, c = rows[:, :HALF], rows[:, HALF : 2 * HALF], rows[:, 2 * HALF :]

    def ring(a, near):
        up, down = [a], [a]
        for _ in range(3):
            up.append(z_send(up[-1], 1))
            down.append(z_send(down[-1], -1))
        up[3], down[3], near = lax.optimization_barrier((up[3], down[3], near))
        far_up = z_send(up[3][:80], 1)
        far_down = z_send(down[3][80:], -1)
        return place(info, up + down[1:] + [far_up, far_down]), near

    w_own, (x_up, x_down, b) = ring(a, (x_up, x_down, b))
    w_sib = core_swap(w_own)
    x_far_up = x_send(x_up[0:1], 1)
    x_far_down = x_send(x_down[1:2], -1)
    s_own, (x_far_up, x_far_down, c) = ring(b, (x_far_up, x_far_down, c))
    s_sib = core_swap(s_own)
    o_own, _ = ring(c, ())
    o_sib = core_swap(o_own)

    early = spatial((2, 2), info, rays_t, ray_weight, mod, w_own, w_sib, [video, x_down])
    early = lax.all_to_all(early, "tm", split_axis=0, concat_axis=0, tiled=True)
    late = spatial((1, 1, 2), info, rays_t, ray_weight, mod, w_own, w_sib, [x_far_up, x_far_down, x_up])
    late = lax.all_to_all(late, "tm", split_axis=0, concat_axis=0, tiled=True)

    def cut(who):
        parts = [video, x_down, x_far_up, x_far_down, x_up]
        return jnp.concatenate([lax.dynamic_slice_in_dim(p, who * PATCHES, PATCHES, axis=1) for p in parts], axis=0)

    v_own = cut(t)
    v_sib = core_swap(cut(t + 1 - 2 * core))

    k = np.arange(D)
    goes = k // (ZS * ROWS) * ROWS + k // ROWS % ZS * (YS * ROWS) + k % ROWS
    order = jnp.asarray(k[:, None] == goes[None, :], BF16)
    result = temporal(
        info, rays_t, ray_weight, mod, v_own, v_sib, early, late, s_own, s_sib, o_own, o_sib, order, t_own, t_sib
    )
    result = lax.all_to_all(result, "tm", split_axis=0, concat_axis=0, tiled=True)
    return jnp.transpose(result, (1, 0, 2, 3)).reshape(2, TOKENS, D)


def solution(mesh):
    placed = (
        P("tm", "clip", None),
        P("clip"),
        P(None, "clip"),
        P(),
        P("clip", None, None),
        P("clip", None),
        P("clip", None),
        P("clip", None),
        P("clip", None),
    )
    return jax.shard_map(
        on_device, mesh=mesh, in_specs=placed, out_specs=P("tm", "clip", None), check_vma=False
    )
```

```python
import functools

import jax
import jax.numpy as jnp
import numpy as np
from jax import lax
from jax.experimental import pallas as pl
from jax.experimental.pallas import tpu as pltpu
from jax.sharding import PartitionSpec as P

D = 1152
HEAD = 72
HEADS = 16
PATCHES = 32
TOKENS = 256
ROWS = 36
XS = 4
ZS = 8
YS = 4
GROUP_HEADS = HEADS // XS
GROUP = GROUP_HEADS * HEAD
PAD = 384
HALF = 640
TQ = 1792
TQ_STEP = 1664
EPS = 1e-6
SOFT = HEAD ** (-0.5) * 1.4426950408889634
F32 = jnp.float32
BF16 = jnp.bfloat16
VMEM_LIMIT = 52 * 1024 * 1024


def z_send(a, s):
    pairs = [(z * YS + y, (z + s) % ZS * YS + y) for z in range(ZS) for y in range(YS)]
    return lax.ppermute(a, "clip", pairs)


def y_send(a, s):
    pairs = [(z * YS + y, z * YS + (y + s) % YS) for z in range(ZS) for y in range(YS)]
    return lax.ppermute(a, "clip", pairs)


def x_send(a, s):
    pairs = [(x * 2 + c, (x + s) % XS * 2 + c) for x in range(XS) for c in range(2)]
    return lax.ppermute(a, "tm", pairs)


def core_swap(a):
    return lax.ppermute(a, "tm", [(t, t ^ 1) for t in range(2 * XS)])


def in_order(pieces, me):
    n = len(pieces)
    back = pieces[::-1]
    both = jnp.stack(back + back[:-1])
    picked = lax.dynamic_slice_in_dim(both, n - 1 - me, n, axis=0)
    return picked.reshape(-1, pieces[0].shape[-1])


def attend(queries, keys, values_t, heads, masked, held, soft, inverse):
    for h in range(heads):
        first, last = h * HEAD, h * HEAD + HEAD - 1
        lo, hi = first // 128 * 128, last // 128 * 128 + 128
        lane = lax.broadcasted_iota(jnp.int32, (1, hi - lo), 1) + lo
        own = jnp.logical_and(lane >= first, lane <= last)
        q = jnp.where(own, queries(lo, hi), jnp.zeros((), BF16))
        held[h] = lax.dot_general(keys(lo, hi), q, (((1,), (1,)), ((), ())), preferred_element_type=F32)
    for h in range(heads):
        s = masked(held[h])
        m = jnp.max(s, axis=0, keepdims=True)
        e = jnp.exp2((s - m) * SOFT)
        inverse[h] = 1.0 / jnp.sum(e, axis=0, keepdims=True)
        soft[h] = e.astype(BF16)
    outs = []
    for h in range(heads):
        first = h * HEAD
        start = first // 16 * 16
        o = jnp.dot(values_t(start, start + 80), soft[h], preferred_element_type=F32) * inverse[h]
        outs.append(o[first - start : first - start + HEAD])
    return jnp.concatenate(outs, axis=0)


def normalize(h, scale, shift):
    center = jnp.mean(h, axis=-1, keepdims=True)
    d = h - center
    spread = jnp.mean(d * d, axis=-1, keepdims=True)
    return (d * lax.rsqrt(spread + EPS) * scale + shift).astype(BF16)


def ray_sum(rays, weight):
    total = rays[:, 0:1] * weight[0:1, :]
    for k in range(1, 6):
        total += rays[:, k : k + 1] * weight[k : k + 1, :]
    return total


def spatial_kernel(parts, *refs):
    info, rays, ray_weight, mod, w_own, w_sib = refs[:6]
    videos = refs[6 : 6 + len(parts)]
    out, kept = refs[6 + len(parts) : 8 + len(parts)]
    ray, wp, sems, normed, packed, vt, of, held, soft, inverse = refs[8 + len(parts) :]
    t, core, cameras = info[0], info[1], info[3]

    def copies(left, right):
        return [
            pltpu.make_async_copy(left, wp.at[:, 0:HALF], sems.at[0]),
            pltpu.make_async_copy(right.at[:, 128:HALF], wp.at[:, HALF:], sems.at[1]),
        ]

    @pl.when(core == 0)
    def _():
        for copy in copies(w_own, w_sib):
            copy.start()

    @pl.when(core == 1)
    def _():
        for copy in copies(w_sib, w_own):
            copy.start()

    ray[...] = ray_sum(rays[...], ray_weight[...])
    scale = 1.0 + mod[1:2, :]
    shift = mod[0:1, :]
    alive = lax.broadcasted_iota(jnp.int32, (TOKENS, TOKENS), 0) < cameras * PATCHES

    frames = [(v, f) for v, n in zip(videos, parts) for f in range(n)]

    def norm_frame(slot):
        video, frame = frames[slot]
        for r in range(TOKENS // 32):
            rows = slice(r * 32, r * 32 + 32)
            h = video[frame, rows, :].astype(F32) + ray[rows, :]
            normed[slot % 2, rows, :] = normalize(h, scale, shift)

    for who, owner in enumerate((t, t + 1 - 2 * core)):
        mine = pl.ds(pl.multiple_of(owner * PATCHES, PATCHES), PATCHES)
        for slot, (video, frame) in enumerate(frames):
            kept[who, slot] = video[frame, mine, :]
    norm_frame(0)
    for copy in copies(w_own, w_sib):
        copy.wait()
    for slot in range(4):
        turn = slot % 2
        made = jnp.dot(normed[turn], wp[...], preferred_element_type=F32)
        packed[turn] = made[:, : 2 * PAD].astype(BF16)
        vt[turn] = jnp.transpose(made[:, 2 * PAD :]).astype(BF16)
        if slot < 3:
            norm_frame(slot + 1)
        of[slot] = attend(
            lambda lo, hi: packed[turn, :, lo:hi],
            lambda lo, hi: packed[turn, :, PAD + lo : PAD + hi],
            lambda lo, hi: vt[turn, lo:hi, :],
            GROUP_HEADS,
            lambda s: jnp.where(alive, s, -1e30),
            held.at[turn],
            soft.at[turn],
            inverse.at[turn],
        )

    block = lax.broadcasted_iota(jnp.int32, (GROUP, 128), 1) // PATCHES
    for i in range(8):
        unit, place = i // 4, i % 4
        made = None
        for f in range(4):
            a = of[f, :, unit * 128 : unit * 128 + 128]
            by = (f - place) * PATCHES % 128
            if by:
                a = pltpu.roll(a, by, 1)
            made = a if made is None else jnp.where(block == f, a, made)
        out[i] = made.astype(BF16)


def spatial(parts, info, rays, ray_weight, mod, w_own, w_sib, videos):
    vmem = pl.BlockSpec(memory_space=pltpu.VMEM)
    far = pl.BlockSpec(memory_space=pl.ANY)
    frames = sum(parts)
    return pl.pallas_call(
        functools.partial(spatial_kernel, parts),
        out_shape=[
            jax.ShapeDtypeStruct((8, GROUP, 128), BF16),
            jax.ShapeDtypeStruct((2, 4, PATCHES, D), BF16),
        ],
        in_specs=[pl.BlockSpec(memory_space=pltpu.SMEM)] + [vmem] * 3 + [far] * 2 + [vmem] * len(parts),
        out_specs=[vmem, vmem],
        scratch_shapes=[
            pltpu.VMEM((TOKENS, D), F32),
            pltpu.VMEM((D, 3 * PAD), BF16),
            pltpu.SemaphoreType.DMA((2,)),
            pltpu.VMEM((2, TOKENS, D), BF16),
            pltpu.VMEM((2, TOKENS, 2 * PAD), BF16),
            pltpu.VMEM((2, PAD, TOKENS), BF16),
            pltpu.VMEM((4, GROUP, TOKENS), F32),
            pltpu.VMEM((2, GROUP_HEADS, TOKENS, TOKENS), F32),
            pltpu.VMEM((2, GROUP_HEADS, TOKENS, TOKENS), BF16),
            pltpu.VMEM((2, GROUP_HEADS, 1, TOKENS), F32),
        ],
        compiler_params=pltpu.CompilerParams(vmem_limit_bytes=VMEM_LIMIT),
        cost_estimate=pl.CostEstimate(
            flops=frames * 2 * TOKENS * D * 3 * PAD, bytes_accessed=8_000_000, transcendentals=frames * 4 * 65536
        ),
    )(info, rays, ray_weight, mod, w_own, w_sib, *videos)


def place_kernel(info, *refs):
    pieces, out = refs[:9], refs[9]
    z = info[4]
    block = YS * ROWS
    for s, piece in enumerate(pieces[:7]):
        shift = s if s < 4 else s - 3
        source = lax.rem(z + (ZS - shift if s < 4 else shift), ZS)
        out[pl.ds(pl.multiple_of(source * block, block), block), :] = piece[...]
    far = lax.rem(z + 4, ZS) * block
    out[pl.ds(pl.multiple_of(far, 16), 80), :] = pieces[7][...]
    out[pl.ds(pl.multiple_of(far + 80, 16), 64), :] = pieces[8][...]


def place(info, pieces):
    vmem = pl.BlockSpec(memory_space=pltpu.VMEM)
    return pl.pallas_call(
        place_kernel,
        out_shape=jax.ShapeDtypeStruct((D, HALF), BF16),
        in_specs=[pl.BlockSpec(memory_space=pltpu.SMEM)] + [vmem] * 9,
        out_specs=vmem,
        compiler_params=pltpu.CompilerParams(vmem_limit_bytes=VMEM_LIMIT),
        cost_estimate=pl.CostEstimate(flops=0, bytes_accessed=4_000_000, transcendentals=0),
    )(info, *pieces)


def turn_kernel(info, order, *refs):
    pieces, out_s, out_t, held = refs[:5], refs[5], refs[6], refs[7]
    y = info[5]
    span = ZS * ROWS
    far = lax.rem(y + 2, YS) * span
    starts = [y * span, lax.rem(y + 3, YS) * span, lax.rem(y + 1, YS) * span, far, far + span // 2]
    for start, piece in zip(starts, pieces):
        held[pl.ds(pl.multiple_of(start, 16), piece.shape[0]), :] = piece[...]
    for n in range(5):
        made = jnp.dot(order[...], held[:, n * 256 : n * 256 + 256], preferred_element_type=F32).astype(BF16)
        for part in range(2):
            at = n * 256 + part * 128
            if at < HALF:
                out_s[:, at : at + 128] = made[:, part * 128 : part * 128 + 128]
            else:
                out_t[:, at - HALF : at - HALF + 128] = made[:, part * 128 : part * 128 + 128]


def turn(info, order, pieces):
    vmem = pl.BlockSpec(memory_space=pltpu.VMEM)
    return pl.pallas_call(
        turn_kernel,
        out_shape=[jax.ShapeDtypeStruct((D, HALF), BF16)] * 2,
        in_specs=[pl.BlockSpec(memory_space=pltpu.SMEM)] + [vmem] * 6,
        out_specs=[vmem, vmem],
        scratch_shapes=[pltpu.VMEM((D, 2 * HALF), BF16)],
        compiler_params=pltpu.CompilerParams(vmem_limit_bytes=VMEM_LIMIT),
        cost_estimate=pl.CostEstimate(flops=3_400_000_000, bytes_accessed=8_000_000, transcendentals=0),
    )(info, order, *pieces)


def temporal_kernel(
    info, rays, ray_weight, mod, ve_own, ve_sib, vl_own, vl_sib, early, late, s_own, s_sib, o_own, o_sib, t_own, t_sib,
    out, wq, wo, mix_t, proj, mid, normed, packed, vt, bias, held, soft, inverse, sems,
):
    t, core, x, cameras = info[0], info[1], info[2], info[3]
    other = 1 - core
    q_copies = [
        pltpu.make_async_copy(t_own, wq.at[0], sems.at[0]),
        pltpu.make_async_copy(t_sib, wq.at[1], sems.at[1]),
    ]
    out_copies = [
        pltpu.make_async_copy(o_own, wo.at[0], sems.at[2]),
        pltpu.make_async_copy(o_sib, wo.at[1], sems.at[3]),
    ]
    for copy in q_copies + out_copies:
        copy.start()

    for source in range(8):
        sx, sc = source // 2, source % 2
        both = jnp.concatenate([early[source], late[source]], axis=1)
        if sx:
            both = pltpu.roll(both.astype(F32), sx * 64, 1).astype(BF16)
        mix_t[sc, sx * GROUP : sx * GROUP + GROUP, :] = both
    key = lax.broadcasted_iota(jnp.int32, (128, 128), 0)
    query = lax.broadcasted_iota(jnp.int32, (128, 128), 1)
    bias[...] = jnp.where(key % 8 == query % 8, 0.0, -1e30)

    def project(half, weights):
        mixed = mix_t[half]
        rows = slice(half * TOKENS, half * TOKENS + TOKENS)
        dims = (((0,), (0,)), ((), ()))
        for which, w in zip((core, other), weights):
            to = pl.ds(pl.multiple_of(which * (HALF - 128), 128), HALF)
            proj[rows, to] = lax.dot_general(mixed, w[...], dims, preferred_element_type=F32)

    for half in range(2):
        project(half, (s_own, s_sib))

    here = rays[pl.ds(pl.multiple_of(t * PATCHES, PATCHES), PATCHES), :]
    ray = ray_sum(here, ray_weight[...])
    gate, shift, scale = mod[2:3, :], mod[3:4, :], 1.0 + mod[4:5, :]

    def slab(j, which, video):
        pair = which * 4 + lax.rem(x + j, XS)
        middles, norms = [], []
        for f in range(2):
            h = video[2 * (j % 2) + f].astype(F32) + ray
            p = proj[pl.ds(pl.multiple_of(pair * 64 + f * PATCHES, PATCHES), PATCHES), :]
            middle = (h + gate * p).astype(BF16).astype(F32)
            middles.append(middle)
            norms.append(normalize(middle, scale, shift).astype(F32))
        for g in range(4):
            rows = pl.ds(pl.multiple_of(g * 128 + pair * 16, 16), 16)
            cut = slice(g * 8, g * 8 + 8)
            mid[rows, :] = jnp.concatenate([m[cut] for m in middles], axis=0).astype(BF16)
            normed[rows, :] = jnp.concatenate([m[cut] for m in norms], axis=0).astype(BF16)

    for j in range(4):
        slab(j, core, ve_own if j < 2 else vl_own)
        slab(j, other, ve_sib if j < 2 else vl_sib)
    for which, copy in ((core, q_copies[0]), (other, q_copies[1])):
        copy.wait()
        w = wq.at[0] if copy is q_copies[0] else wq.at[1]
        for n in range(TQ // 256):
            to = pl.ds(pl.multiple_of(which * TQ_STEP + n * 256, 128), 256)
            made = jnp.dot(normed[...], w[:, n * 256 : n * 256 + 256], preferred_element_type=F32)
            packed[:, to] = made.astype(BF16)
    for copy in out_copies:
        copy.wait()
    for half in range(2):
        for g in (2 * half, 2 * half + 1):
            rows = slice(g * 128, g * 128 + 128)
            vt[g] = jnp.transpose(packed[rows, 2 * D :])
            lanes = slice((g % 2) * 128, (g % 2) * 128 + 128)
            mix_t[half, :, lanes] = attend(
                lambda lo, hi: packed[rows, lo:hi],
                lambda lo, hi: packed[rows, D + lo : D + hi],
                lambda lo, hi: vt[g, lo:hi, :],
                HEADS,
                lambda s: s + bias[...],
                held.at[g],
                soft.at[g],
                inverse.at[g],
            ).astype(BF16)
        project(half, (wo.at[0], wo.at[1]))
    alive = jnp.where(t < cameras, 1.0, 0.0)
    last_gate = mod[5:6, :]
    for target in range(8):
        pair = target % 2 * 4 + target // 2
        for g in range(4):
            rows = slice(g * 128 + pair * 16, g * 128 + pair * 16 + 16)
            done = (mid[rows, :].astype(F32) + last_gate * proj[rows, :]) * alive
            for f in range(2):
                out[target, f, g * 8 : g * 8 + 8, :] = done[f * 8 : f * 8 + 8].astype(BF16)


def temporal(info, rays, ray_weight, mod, ve_own, ve_sib, vl_own, vl_sib, early, late, s_own, s_sib, o_own, o_sib, t_own, t_sib):
    vmem = pl.BlockSpec(memory_space=pltpu.VMEM)
    far = pl.BlockSpec(memory_space=pl.ANY)
    return pl.pallas_call(
        temporal_kernel,
        out_shape=jax.ShapeDtypeStruct((8, 2, PATCHES, D), BF16),
        in_specs=[pl.BlockSpec(memory_space=pltpu.SMEM)] + [vmem] * 11 + [far] * 4,
        out_specs=vmem,
        scratch_shapes=[
            pltpu.VMEM((2, D, TQ), BF16),
            pltpu.VMEM((2, D, HALF), BF16),
            pltpu.VMEM((2, D, TOKENS), BF16),
            pltpu.VMEM((2 * TOKENS, D), F32),
            pltpu.VMEM((2 * TOKENS, D), BF16),
            pltpu.VMEM((2 * TOKENS, D), BF16),
            pltpu.VMEM((2 * TOKENS, 3 * D), BF16),
            pltpu.VMEM((4, D, 128), BF16),
            pltpu.VMEM((128, 128), F32),
            pltpu.VMEM((4, HEADS, 128, 128), F32),
            pltpu.VMEM((4, HEADS, 128, 128), BF16),
            pltpu.VMEM((4, HEADS, 1, 128), F32),
            pltpu.SemaphoreType.DMA((4,)),
        ],
        compiler_params=pltpu.CompilerParams(vmem_limit_bytes=VMEM_LIMIT),
        cost_estimate=pl.CostEstimate(flops=16_000_000_000, bytes_accessed=24_000_000, transcendentals=2_100_000),
    )(info, rays, ray_weight, mod, ve_own, ve_sib, vl_own, vl_sib, early, late, s_own, s_sib, o_own, o_sib, t_own, t_sib)


def on_device(
    video,
    cameras,
    rays,
    ray_weight,
    modulation,
    spatial_qkv,
    spatial_out,
    temporal_qkv,
    temporal_out,
):
    t = lax.axis_index("tm")
    clip = lax.axis_index("clip")
    x, core = t // 2, t % 2
    z, y = clip // YS, clip % YS
    info = jnp.stack([t, core, x, cameras[0], z, y]).astype(jnp.int32)
    mod = modulation[0].astype(F32)
    rays_t = rays.T

    def columns(a, start, size):
        return lax.dynamic_slice_in_dim(a, start, size, axis=1)

    x_up = x_send(video, 1)
    x_down = x_send(video, -1)

    zgroups = [[zz * YS + yy for zz in range(ZS)] for yy in range(YS)]
    heads = [jnp.pad(columns(spatial_qkv, k * D + x * GROUP, GROUP), ((0, 0), (0, PAD - GROUP))) for k in range(3)]
    first = jnp.concatenate(
        [
            columns(jnp.concatenate(heads, axis=1), core * (HALF - 128), HALF),
            columns(temporal_qkv, core * TQ_STEP, TQ),
        ],
        axis=1,
    )
    rows = in_order([first, y_send(first, 1), y_send(first, 2), y_send(first, 3)], y)
    a, b = rows[:, :HALF], rows[:, HALF:]
    t_own = lax.all_gather(b, "clip", axis=0, tiled=True, axis_index_groups=zgroups)

    second = jnp.concatenate(
        [columns(spatial_out, core * (HALF - 128), HALF), columns(temporal_out, core * (HALF - 128), HALF)], axis=1
    )
    far_rows = [second] + [z_send(second, s) for s in range(1, ZS)]

    up, down = [a], [a]
    for _ in range(3):
        up.append(z_send(up[-1], 1))
        down.append(z_send(down[-1], -1))
    up[3], down[3], x_up, x_down = lax.optimization_barrier((up[3], down[3], x_up, x_down))
    far_up = z_send(up[3][:80], 1)
    far_down = z_send(down[3][80:], -1)
    x_far_up = x_send(x_up[0:1], 1)
    x_far_down = x_send(x_down[1:2], -1)
    w_own = place(info, up + down[1:] + [far_up, far_down])
    w_sib = core_swap(w_own)

    own = in_order(far_rows, z)
    own, w_own = lax.optimization_barrier((own, w_own))
    y_up, y_down = y_send(own, 1), y_send(own, -1)

    early, kept_e = spatial((2, 2), info, rays_t, ray_weight, mod, w_own, w_sib, [video, x_down])
    y_up, y_down, x_far_up, x_far_down, early = lax.optimization_barrier((y_up, y_down, x_far_up, x_far_down, early))
    early = lax.all_to_all(early, "tm", split_axis=0, concat_axis=0, tiled=True)
    half = ZS * ROWS // 2
    y_far_up = y_send(y_up[:half], 1)
    y_far_down = y_send(y_down[half:], -1)
    ve_sib = core_swap(kept_e[1])

    late, kept_l = spatial((1, 1, 2), info, rays_t, ray_weight, mod, w_own, w_sib, [x_far_up, x_far_down, x_up])
    t_own, y_far_up, y_far_down, late = lax.optimization_barrier((t_own, y_far_up, y_far_down, late))
    late = lax.all_to_all(late, "tm", split_axis=0, concat_axis=0, tiled=True)
    t_sib = core_swap(t_own)
    vl_sib = core_swap(kept_l[1])
    k = np.arange(D)
    goes = k // (ZS * ROWS) * ROWS + k // ROWS % ZS * (YS * ROWS) + k % ROWS
    order = jnp.asarray(k[:, None] == goes[None, :], BF16)
    s_own, o_own = turn(info, order, [own, y_up, y_down, y_far_up, y_far_down])
    s_sib, o_sib = core_swap(s_own), core_swap(o_own)

    result = temporal(
        info, rays_t, ray_weight, mod, kept_e[0], ve_sib, kept_l[0], vl_sib, early, late,
        s_own, s_sib, o_own, o_sib, t_own, t_sib,
    )
    result = lax.all_to_all(result, "tm", split_axis=0, concat_axis=0, tiled=True)
    return jnp.transpose(result, (1, 0, 2, 3)).reshape(2, TOKENS, D)


def solution(mesh):
    placed = (
        P("tm", "clip", None),
        P("clip"),
        P(None, "clip"),
        P(),
        P("clip", None, None),
        P("clip", None),
        P("clip", None),
        P("clip", None),
        P("clip", None),
    )
    return jax.shard_map(
        on_device, mesh=mesh, in_specs=placed, out_specs=P("tm", "clip", None), check_vma=False
    )
```

```python
import functools

import jax
import jax.numpy as jnp
import numpy as np
from jax import lax
from jax.experimental import pallas as pl
from jax.experimental.pallas import tpu as pltpu
from jax.sharding import PartitionSpec as P

D = 1152
HEAD = 72
HEADS = 16
PATCHES = 32
TOKENS = 256
ROWS = 36
XS = 4
ZS = 8
YS = 4
GROUP_HEADS = HEADS // XS
GROUP = GROUP_HEADS * HEAD
PAD = 384
HALF = 640
TQ = 1792
TQ_STEP = 1664
EPS = 1e-6
SOFT = HEAD ** (-0.5) * 1.4426950408889634
F32 = jnp.float32
BF16 = jnp.bfloat16
VMEM_LIMIT = 52 * 1024 * 1024


def z_send(a, s):
    pairs = [(z * YS + y, (z + s) % ZS * YS + y) for z in range(ZS) for y in range(YS)]
    return lax.ppermute(a, "clip", pairs)


def y_send(a, s):
    pairs = [(z * YS + y, z * YS + (y + s) % YS) for z in range(ZS) for y in range(YS)]
    return lax.ppermute(a, "clip", pairs)


def x_send(a, s):
    pairs = [(x * 2 + c, (x + s) % XS * 2 + c) for x in range(XS) for c in range(2)]
    return lax.ppermute(a, "tm", pairs)


def core_swap(a):
    return lax.ppermute(a, "tm", [(t, t ^ 1) for t in range(2 * XS)])


def attend(queries, keys, values_t, heads, masked, held, soft, inverse):
    for h in range(heads):
        first, last = h * HEAD, h * HEAD + HEAD - 1
        lo, hi = first // 128 * 128, last // 128 * 128 + 128
        lane = lax.broadcasted_iota(jnp.int32, (1, hi - lo), 1) + lo
        own = jnp.logical_and(lane >= first, lane <= last)
        q = jnp.where(own, queries(lo, hi), jnp.zeros((), BF16))
        held[h] = lax.dot_general(keys(lo, hi), q, (((1,), (1,)), ((), ())), preferred_element_type=F32)
    for h in range(heads):
        s = masked(held[h])
        m = jnp.max(s, axis=0, keepdims=True)
        e = jnp.exp2((s - m) * SOFT)
        inverse[h] = 1.0 / jnp.sum(e, axis=0, keepdims=True)
        soft[h] = e.astype(BF16)
    outs = []
    for h in range(heads):
        first = h * HEAD
        start = first // 16 * 16
        o = jnp.dot(values_t(start, start + 80), soft[h], preferred_element_type=F32) * inverse[h]
        outs.append(o[first - start : first - start + HEAD])
    return jnp.concatenate(outs, axis=0)


def normalize(h, scale, shift):
    center = jnp.mean(h, axis=-1, keepdims=True)
    d = h - center
    spread = jnp.mean(d * d, axis=-1, keepdims=True)
    return (d * lax.rsqrt(spread + EPS) * scale + shift).astype(BF16)


def ray_sum(rays, weight):
    total = rays[:, 0:1] * weight[0:1, :]
    for k in range(1, 6):
        total += rays[:, k : k + 1] * weight[k : k + 1, :]
    return total


def spatial_kernel(parts, *refs):
    info, rays, ray_weight, mod, w_own, w_sib = refs[:6]
    videos = refs[6 : 6 + len(parts)]
    out, kept = refs[6 + len(parts) : 8 + len(parts)]
    ray, wp, sems, normed, packed, vt, of, held, soft, inverse = refs[8 + len(parts) :]
    t, core, cameras = info[0], info[1], info[3]

    def copies(left, right):
        return [
            pltpu.make_async_copy(left, wp.at[:, 0:HALF], sems.at[0]),
            pltpu.make_async_copy(right.at[:, 128:HALF], wp.at[:, HALF:], sems.at[1]),
        ]

    @pl.when(core == 0)
    def _():
        for copy in copies(w_own, w_sib):
            copy.start()

    @pl.when(core == 1)
    def _():
        for copy in copies(w_sib, w_own):
            copy.start()

    ray[...] = ray_sum(rays[...], ray_weight[...])
    scale = 1.0 + mod[1:2, :]
    shift = mod[0:1, :]
    alive = lax.broadcasted_iota(jnp.int32, (TOKENS, TOKENS), 0) < cameras * PATCHES

    frames = [(v, f) for v, n in zip(videos, parts) for f in range(n)]

    def norm_frame(slot):
        video, frame = frames[slot]
        for r in range(TOKENS // 32):
            rows = slice(r * 32, r * 32 + 32)
            h = video[frame, rows, :].astype(F32) + ray[rows, :]
            normed[slot % 2, rows, :] = normalize(h, scale, shift)

    for who, owner in enumerate((t, t + 1 - 2 * core)):
        mine = pl.ds(pl.multiple_of(owner * PATCHES, PATCHES), PATCHES)
        for slot, (video, frame) in enumerate(frames):
            kept[who, slot] = video[frame, mine, :]
    norm_frame(0)
    for copy in copies(w_own, w_sib):
        copy.wait()
    for slot in range(4):
        turn = slot % 2
        made = jnp.dot(normed[turn], wp[...], preferred_element_type=F32)
        packed[turn] = made[:, : 2 * PAD].astype(BF16)
        vt[turn] = jnp.transpose(made[:, 2 * PAD :]).astype(BF16)
        if slot < 3:
            norm_frame(slot + 1)
        of[slot] = attend(
            lambda lo, hi: packed[turn, :, lo:hi],
            lambda lo, hi: packed[turn, :, PAD + lo : PAD + hi],
            lambda lo, hi: vt[turn, lo:hi, :],
            GROUP_HEADS,
            lambda s: jnp.where(alive, s, -1e30),
            held.at[turn],
            soft.at[turn],
            inverse.at[turn],
        )

    block = lax.broadcasted_iota(jnp.int32, (GROUP, 128), 1) // PATCHES
    for i in range(8):
        unit, place = i // 4, i % 4
        made = None
        for f in range(4):
            a = of[f, :, unit * 128 : unit * 128 + 128]
            by = (f - place) * PATCHES % 128
            if by:
                a = pltpu.roll(a, by, 1)
            made = a if made is None else jnp.where(block == f, a, made)
        out[i] = made.astype(BF16)


def spatial(parts, info, rays, ray_weight, mod, w_own, w_sib, videos):
    vmem = pl.BlockSpec(memory_space=pltpu.VMEM)
    far = pl.BlockSpec(memory_space=pl.ANY)
    frames = sum(parts)
    return pl.pallas_call(
        functools.partial(spatial_kernel, parts),
        out_shape=[
            jax.ShapeDtypeStruct((8, GROUP, 128), BF16),
            jax.ShapeDtypeStruct((2, 4, PATCHES, D), BF16),
        ],
        in_specs=[pl.BlockSpec(memory_space=pltpu.SMEM)] + [vmem] * 3 + [far] * 2 + [vmem] * len(parts),
        out_specs=[vmem, vmem],
        scratch_shapes=[
            pltpu.VMEM((TOKENS, D), F32),
            pltpu.VMEM((D, 3 * PAD), BF16),
            pltpu.SemaphoreType.DMA((2,)),
            pltpu.VMEM((2, TOKENS, D), BF16),
            pltpu.VMEM((2, TOKENS, 2 * PAD), BF16),
            pltpu.VMEM((2, PAD, TOKENS), BF16),
            pltpu.VMEM((4, GROUP, TOKENS), F32),
            pltpu.VMEM((2, GROUP_HEADS, TOKENS, TOKENS), F32),
            pltpu.VMEM((2, GROUP_HEADS, TOKENS, TOKENS), BF16),
            pltpu.VMEM((2, GROUP_HEADS, 1, TOKENS), F32),
        ],
        compiler_params=pltpu.CompilerParams(vmem_limit_bytes=VMEM_LIMIT),
        cost_estimate=pl.CostEstimate(
            flops=frames * 2 * TOKENS * D * 3 * PAD, bytes_accessed=8_000_000, transcendentals=frames * 4 * 65536
        ),
    )(info, rays, ray_weight, mod, w_own, w_sib, *videos)


def place_kernel(info, *refs):
    pieces, out = refs[:9], refs[9]
    z = info[4]
    block = YS * ROWS
    for s, piece in enumerate(pieces[:7]):
        shift = s if s < 4 else s - 3
        source = lax.rem(z + (ZS - shift if s < 4 else shift), ZS)
        out[pl.ds(pl.multiple_of(source * block, block), block), :] = piece[...]
    far = lax.rem(z + 4, ZS) * block
    out[pl.ds(pl.multiple_of(far, 16), 80), :] = pieces[7][...]
    out[pl.ds(pl.multiple_of(far + 80, 16), 64), :] = pieces[8][...]


def place(info, pieces):
    vmem = pl.BlockSpec(memory_space=pltpu.VMEM)
    return pl.pallas_call(
        place_kernel,
        out_shape=jax.ShapeDtypeStruct((D, HALF), BF16),
        in_specs=[pl.BlockSpec(memory_space=pltpu.SMEM)] + [vmem] * 9,
        out_specs=vmem,
        compiler_params=pltpu.CompilerParams(vmem_limit_bytes=VMEM_LIMIT),
        cost_estimate=pl.CostEstimate(flops=0, bytes_accessed=4_000_000, transcendentals=0),
    )(info, *pieces)


def turn_kernel(info, order, *refs):
    pieces, out_s, out_t, held = refs[:5], refs[5], refs[6], refs[7]
    y = info[5]
    span = ZS * ROWS
    far = lax.rem(y + 2, YS) * span
    starts = [y * span, lax.rem(y + 3, YS) * span, lax.rem(y + 1, YS) * span, far, far + span // 2]
    for start, piece in zip(starts, pieces):
        held[pl.ds(pl.multiple_of(start, 16), piece.shape[0]), :] = piece[...]
    for n in range(5):
        made = jnp.dot(order[...], held[:, n * 256 : n * 256 + 256], preferred_element_type=F32).astype(BF16)
        for part in range(2):
            at = n * 256 + part * 128
            if at < HALF:
                out_s[:, at : at + 128] = made[:, part * 128 : part * 128 + 128]
            else:
                out_t[:, at - HALF : at - HALF + 128] = made[:, part * 128 : part * 128 + 128]


def turn(info, order, pieces):
    vmem = pl.BlockSpec(memory_space=pltpu.VMEM)
    return pl.pallas_call(
        turn_kernel,
        out_shape=[jax.ShapeDtypeStruct((D, HALF), BF16)] * 2,
        in_specs=[pl.BlockSpec(memory_space=pltpu.SMEM)] + [vmem] * 6,
        out_specs=[vmem, vmem],
        scratch_shapes=[pltpu.VMEM((D, 2 * HALF), BF16)],
        compiler_params=pltpu.CompilerParams(vmem_limit_bytes=VMEM_LIMIT),
        cost_estimate=pl.CostEstimate(flops=3_400_000_000, bytes_accessed=8_000_000, transcendentals=0),
    )(info, order, *pieces)


def temporal_kernel(
    info, rays, ray_weight, mod, ve_own, ve_sib, vl_own, vl_sib, early, late, s_own, s_sib, o_own, o_sib, t_own, t_sib,
    out, wq, wo, mix_t, proj, mid, normed, packed, vt, bias, held, soft, inverse, sems,
):
    t, core, x, cameras = info[0], info[1], info[2], info[3]
    other = 1 - core
    q_copies = [
        pltpu.make_async_copy(t_own, wq.at[0], sems.at[0]),
        pltpu.make_async_copy(t_sib, wq.at[1], sems.at[1]),
    ]
    out_copies = [
        pltpu.make_async_copy(o_own, wo.at[0], sems.at[2]),
        pltpu.make_async_copy(o_sib, wo.at[1], sems.at[3]),
    ]
    for copy in q_copies + out_copies:
        copy.start()

    for source in range(8):
        sx, sc = source // 2, source % 2
        both = jnp.concatenate([early[source], late[source]], axis=1)
        if sx:
            both = pltpu.roll(both.astype(F32), sx * 64, 1).astype(BF16)
        mix_t[sc, sx * GROUP : sx * GROUP + GROUP, :] = both
    key = lax.broadcasted_iota(jnp.int32, (128, 128), 0)
    query = lax.broadcasted_iota(jnp.int32, (128, 128), 1)
    bias[...] = jnp.where(key % 8 == query % 8, 0.0, -1e30)

    def project(half, weights):
        mixed = mix_t[half]
        rows = slice(half * TOKENS, half * TOKENS + TOKENS)
        dims = (((0,), (0,)), ((), ()))
        for which, w in zip((core, other), weights):
            to = pl.ds(pl.multiple_of(which * (HALF - 128), 128), HALF)
            proj[rows, to] = lax.dot_general(mixed, w[...], dims, preferred_element_type=F32)

    for half in range(2):
        project(half, (s_own, s_sib))

    here = rays[pl.ds(pl.multiple_of(t * PATCHES, PATCHES), PATCHES), :]
    ray = ray_sum(here, ray_weight[...])
    gate, shift, scale = mod[2:3, :], mod[3:4, :], 1.0 + mod[4:5, :]

    def slab(j, which, video):
        pair = which * 4 + lax.rem(x + j, XS)
        middles, norms = [], []
        for f in range(2):
            h = video[2 * (j % 2) + f].astype(F32) + ray
            p = proj[pl.ds(pl.multiple_of(pair * 64 + f * PATCHES, PATCHES), PATCHES), :]
            middle = (h + gate * p).astype(BF16).astype(F32)
            middles.append(middle)
            norms.append(normalize(middle, scale, shift).astype(F32))
        for g in range(4):
            rows = pl.ds(pl.multiple_of(g * 128 + pair * 16, 16), 16)
            cut = slice(g * 8, g * 8 + 8)
            mid[rows, :] = jnp.concatenate([m[cut] for m in middles], axis=0).astype(BF16)
            normed[rows, :] = jnp.concatenate([m[cut] for m in norms], axis=0).astype(BF16)

    for j in range(4):
        slab(j, core, ve_own if j < 2 else vl_own)
        slab(j, other, ve_sib if j < 2 else vl_sib)
    for which, copy in ((core, q_copies[0]), (other, q_copies[1])):
        copy.wait()
        w = wq.at[0] if copy is q_copies[0] else wq.at[1]
        for n in range(TQ // 256):
            to = pl.ds(pl.multiple_of(which * TQ_STEP + n * 256, 128), 256)
            made = jnp.dot(normed[...], w[:, n * 256 : n * 256 + 256], preferred_element_type=F32)
            packed[:, to] = made.astype(BF16)
    for copy in out_copies:
        copy.wait()
    for half in range(2):
        for g in (2 * half, 2 * half + 1):
            rows = slice(g * 128, g * 128 + 128)
            vt[g] = jnp.transpose(packed[rows, 2 * D :])
            lanes = slice((g % 2) * 128, (g % 2) * 128 + 128)
            mix_t[half, :, lanes] = attend(
                lambda lo, hi: packed[rows, lo:hi],
                lambda lo, hi: packed[rows, D + lo : D + hi],
                lambda lo, hi: vt[g, lo:hi, :],
                HEADS,
                lambda s: s + bias[...],
                held.at[g],
                soft.at[g],
                inverse.at[g],
            ).astype(BF16)
        project(half, (wo.at[0], wo.at[1]))
    alive = jnp.where(t < cameras, 1.0, 0.0)
    last_gate = mod[5:6, :]
    for target in range(8):
        pair = target % 2 * 4 + target // 2
        for g in range(4):
            rows = slice(g * 128 + pair * 16, g * 128 + pair * 16 + 16)
            done = (mid[rows, :].astype(F32) + last_gate * proj[rows, :]) * alive
            for f in range(2):
                out[target, f, g * 8 : g * 8 + 8, :] = done[f * 8 : f * 8 + 8].astype(BF16)


def temporal(info, rays, ray_weight, mod, ve_own, ve_sib, vl_own, vl_sib, early, late, s_own, s_sib, o_own, o_sib, t_own, t_sib):
    vmem = pl.BlockSpec(memory_space=pltpu.VMEM)
    far = pl.BlockSpec(memory_space=pl.ANY)
    return pl.pallas_call(
        temporal_kernel,
        out_shape=jax.ShapeDtypeStruct((8, 2, PATCHES, D), BF16),
        in_specs=[pl.BlockSpec(memory_space=pltpu.SMEM)] + [vmem] * 11 + [far] * 4,
        out_specs=vmem,
        scratch_shapes=[
            pltpu.VMEM((2, D, TQ), BF16),
            pltpu.VMEM((2, D, HALF), BF16),
            pltpu.VMEM((2, D, TOKENS), BF16),
            pltpu.VMEM((2 * TOKENS, D), F32),
            pltpu.VMEM((2 * TOKENS, D), BF16),
            pltpu.VMEM((2 * TOKENS, D), BF16),
            pltpu.VMEM((2 * TOKENS, 3 * D), BF16),
            pltpu.VMEM((4, D, 128), BF16),
            pltpu.VMEM((128, 128), F32),
            pltpu.VMEM((4, HEADS, 128, 128), F32),
            pltpu.VMEM((4, HEADS, 128, 128), BF16),
            pltpu.VMEM((4, HEADS, 1, 128), F32),
            pltpu.SemaphoreType.DMA((4,)),
        ],
        compiler_params=pltpu.CompilerParams(vmem_limit_bytes=VMEM_LIMIT),
        cost_estimate=pl.CostEstimate(flops=16_000_000_000, bytes_accessed=24_000_000, transcendentals=2_100_000),
    )(info, rays, ray_weight, mod, ve_own, ve_sib, vl_own, vl_sib, early, late, s_own, s_sib, o_own, o_sib, t_own, t_sib)


def on_device(
    video,
    cameras,
    rays,
    ray_weight,
    modulation,
    spatial_qkv,
    spatial_out,
    temporal_qkv,
    temporal_out,
):
    t = lax.axis_index("tm")
    clip = lax.axis_index("clip")
    x, core = t // 2, t % 2
    z, y = clip // YS, clip % YS
    info = jnp.stack([t, core, x, cameras[0], z, y]).astype(jnp.int32)
    mod = modulation[0].astype(F32)
    rays_t = rays.T

    def columns(a, start, size):
        return lax.dynamic_slice_in_dim(a, start, size, axis=1)

    zgroups = [[zz * YS + yy for zz in range(ZS)] for yy in range(YS)]
    ygroups = [[zz * YS + yy for yy in range(YS)] for zz in range(ZS)]

    def spread(a, groups):
        copies = jnp.broadcast_to(a[None], (len(groups[0]),) + a.shape)
        return lax.all_to_all(copies, "clip", 0, 0, axis_index_groups=groups, tiled=True).reshape(-1, a.shape[1])

    frame_0, frame_1 = video[0:1], video[1:2]
    up_0, down_0 = x_send(frame_0, 1), x_send(frame_0, -1)

    heads = [jnp.pad(columns(spatial_qkv, k * D + x * GROUP, GROUP), ((0, 0), (0, PAD - GROUP))) for k in range(3)]
    first = jnp.concatenate(
        [
            columns(jnp.concatenate(heads, axis=1), core * (HALF - 128), HALF),
            columns(temporal_qkv, core * TQ_STEP, TQ),
        ],
        axis=1,
    )
    rows = spread(first, ygroups)
    a, b = rows[:, :HALF], rows[:, HALF:]
    t_own = lax.all_gather(b, "clip", axis=0, tiled=True, axis_index_groups=zgroups)

    second = jnp.concatenate(
        [columns(spatial_out, core * (HALF - 128), HALF), columns(temporal_out, core * (HALF - 128), HALF)], axis=1
    )
    own = spread(second, zgroups)

    a, up_0, down_0, frame_1 = lax.optimization_barrier((a, up_0, down_0, frame_1))
    up_1, down_1, far_0 = x_send(frame_1, 1), x_send(frame_1, -1), x_send(up_0, 1)
    up, down = [a], [a]
    for _ in range(3):
        up.append(z_send(up[-1], 1))
        down.append(z_send(down[-1], -1))
    up[3], down[3], up_1, down_1, far_0, own = lax.optimization_barrier((up[3], down[3], up_1, down_1, far_0, own))
    far_up = z_send(up[3][:80], 1)
    far_down = z_send(down[3][80:], -1)
    far_1 = x_send(down_1, -1)
    y_up, y_down = y_send(own, 1), y_send(own, -1)
    w_own = place(info, up + down[1:] + [far_up, far_down])
    w_sib = core_swap(w_own)

    early, kept_e = spatial((2, 1, 1), info, rays_t, ray_weight, mod, w_own, w_sib, [video, down_0, down_1])
    y_up, y_down, far_1, early = lax.optimization_barrier((y_up, y_down, far_1, early))
    early = lax.all_to_all(early, "tm", split_axis=0, concat_axis=0, tiled=True)
    half = ZS * ROWS // 2
    y_far_up = y_send(y_up[:half], 1)
    y_far_down = y_send(y_down[half:], -1)
    ve_sib = core_swap(kept_e[1])

    late, kept_l = spatial((1, 1, 1, 1), info, rays_t, ray_weight, mod, w_own, w_sib, [far_0, far_1, up_0, up_1])
    t_own, y_far_up, y_far_down, late = lax.optimization_barrier((t_own, y_far_up, y_far_down, late))
    late = lax.all_to_all(late, "tm", split_axis=0, concat_axis=0, tiled=True)
    t_sib = core_swap(t_own)
    vl_sib = core_swap(kept_l[1])
    k = np.arange(D)
    goes = k // (ZS * ROWS) * ROWS + k // ROWS % ZS * (YS * ROWS) + k % ROWS
    order = jnp.asarray(k[:, None] == goes[None, :], BF16)
    s_own, o_own = turn(info, order, [own, y_up, y_down, y_far_up, y_far_down])
    s_sib, o_sib = core_swap(s_own), core_swap(o_own)

    result = temporal(
        info, rays_t, ray_weight, mod, kept_e[0], ve_sib, kept_l[0], vl_sib, early, late,
        s_own, s_sib, o_own, o_sib, t_own, t_sib,
    )
    result = lax.all_to_all(result, "tm", split_axis=0, concat_axis=0, tiled=True)
    return jnp.transpose(result, (1, 0, 2, 3)).reshape(2, TOKENS, D)


def solution(mesh):
    placed = (
        P("tm", "clip", None),
        P("clip"),
        P(None, "clip"),
        P(),
        P("clip", None, None),
        P("clip", None),
        P("clip", None),
        P("clip", None),
        P("clip", None),
    )
    return jax.shard_map(
        on_device, mesh=mesh, in_specs=placed, out_specs=P("tm", "clip", None), check_vma=False
    )
```

```python
import functools

import jax
import jax.numpy as jnp
import numpy as np
from jax import lax
from jax.experimental import pallas as pl
from jax.experimental.pallas import tpu as pltpu
from jax.sharding import PartitionSpec as P

D = 1152
HEAD = 72
HEADS = 16
PATCHES = 32
TOKENS = 256
ROWS = 36
XS = 4
ZS = 8
YS = 4
GROUP_HEADS = HEADS // XS
GROUP = GROUP_HEADS * HEAD
PAD = 384
HALF = 640
TQ = 1792
TQ_STEP = 1664
EPS = 1e-6
SOFT = HEAD ** (-0.5) * 1.4426950408889634
F32 = jnp.float32
BF16 = jnp.bfloat16
VMEM_LIMIT = 52 * 1024 * 1024


def z_send(a, s):
    pairs = [(z * YS + y, (z + s) % ZS * YS + y) for z in range(ZS) for y in range(YS)]
    return lax.ppermute(a, "clip", pairs)


def y_send(a, s):
    pairs = [(z * YS + y, z * YS + (y + s) % YS) for z in range(ZS) for y in range(YS)]
    return lax.ppermute(a, "clip", pairs)


def x_send(a, s):
    pairs = [(x * 2 + c, (x + s) % XS * 2 + c) for x in range(XS) for c in range(2)]
    return lax.ppermute(a, "tm", pairs)


def core_swap(a):
    return lax.ppermute(a, "tm", [(t, t ^ 1) for t in range(2 * XS)])


def in_order(pieces, me):
    n = len(pieces)
    back = pieces[::-1]
    both = jnp.stack(back + back[:-1])
    picked = lax.dynamic_slice_in_dim(both, n - 1 - me, n, axis=0)
    return picked.reshape(-1, pieces[0].shape[-1])


def spread(a, groups):
    copies = jnp.broadcast_to(a[None], (len(groups[0]),) + a.shape)
    return lax.all_to_all(copies, "clip", 0, 0, axis_index_groups=groups, tiled=True).reshape(-1, a.shape[1])


def attend(queries, keys, values_t, heads, masked, held, soft, inverse):
    for h in range(heads):
        first, last = h * HEAD, h * HEAD + HEAD - 1
        lo, hi = first // 128 * 128, last // 128 * 128 + 128
        lane = lax.broadcasted_iota(jnp.int32, (1, hi - lo), 1) + lo
        own = jnp.logical_and(lane >= first, lane <= last)
        q = jnp.where(own, queries(lo, hi), jnp.zeros((), BF16))
        held[h] = lax.dot_general(keys(lo, hi), q, (((1,), (1,)), ((), ())), preferred_element_type=F32)
    for h in range(heads):
        s = masked(held[h])
        m = jnp.max(s, axis=0, keepdims=True)
        e = jnp.exp2((s - m) * SOFT)
        inverse[h] = 1.0 / jnp.sum(e, axis=0, keepdims=True)
        soft[h] = e.astype(BF16)
    outs = []
    for h in range(heads):
        first = h * HEAD
        start = first // 16 * 16
        o = jnp.dot(values_t(start, start + 80), soft[h], preferred_element_type=F32) * inverse[h]
        outs.append(o[first - start : first - start + HEAD])
    return jnp.concatenate(outs, axis=0)


def normalize(h, scale, shift):
    center = jnp.mean(h, axis=-1, keepdims=True)
    d = h - center
    spread = jnp.mean(d * d, axis=-1, keepdims=True)
    return (d * lax.rsqrt(spread + EPS) * scale + shift).astype(BF16)


def ray_sum(rays, weight):
    total = rays[:, 0:1] * weight[0:1, :]
    for k in range(1, 6):
        total += rays[:, k : k + 1] * weight[k : k + 1, :]
    return total


def spatial_kernel(parts, before, *refs):
    info, rays, ray_weight, mod, w_own, w_sib = refs[:6]
    videos = refs[6 : 6 + len(parts)]
    refs = refs[6 + len(parts) :]
    if before:
        old, out, kept = refs[:3]
        refs = refs[3:]
        out[:, 0] = old[...]
    else:
        out, kept = refs[:2]
        refs = refs[2:]
    ray, wp, sems, normed, packed, vt, of, held, soft, inverse = refs
    t, core, cameras = info[0], info[1], info[3]

    def copies(left, right):
        return [
            pltpu.make_async_copy(left, wp.at[:, 0:HALF], sems.at[0]),
            pltpu.make_async_copy(right.at[:, 128:HALF], wp.at[:, HALF:], sems.at[1]),
        ]

    @pl.when(core == 0)
    def _():
        for copy in copies(w_own, w_sib):
            copy.start()

    @pl.when(core == 1)
    def _():
        for copy in copies(w_sib, w_own):
            copy.start()

    ray[...] = ray_sum(rays[...], ray_weight[...])
    scale = 1.0 + mod[1:2, :]
    shift = mod[0:1, :]
    alive = lax.broadcasted_iota(jnp.int32, (TOKENS, TOKENS), 0) < cameras * PATCHES

    frames = [(v, f) for v, n in zip(videos, parts) for f in range(n)]

    def norm_frame(slot):
        video, frame = frames[slot]
        for r in range(TOKENS // 32):
            rows = slice(r * 32, r * 32 + 32)
            h = video[frame, rows, :].astype(F32) + ray[rows, :]
            normed[slot % 2, rows, :] = normalize(h, scale, shift)

    for who, owner in enumerate((t, t + 1 - 2 * core)):
        mine = pl.ds(pl.multiple_of(owner * PATCHES, PATCHES), PATCHES)
        for slot, (video, frame) in enumerate(frames):
            kept[who, slot] = video[frame, mine, :]
    norm_frame(0)
    for copy in copies(w_own, w_sib):
        copy.wait()
    for slot in range(4):
        turn = slot % 2
        made = jnp.dot(normed[turn], wp[...], preferred_element_type=F32)
        packed[turn] = made[:, : 2 * PAD].astype(BF16)
        vt[turn] = jnp.transpose(made[:, 2 * PAD :]).astype(BF16)
        if slot < 3:
            norm_frame(slot + 1)
        of[slot] = attend(
            lambda lo, hi: packed[turn, :, lo:hi],
            lambda lo, hi: packed[turn, :, PAD + lo : PAD + hi],
            lambda lo, hi: vt[turn, lo:hi, :],
            GROUP_HEADS,
            lambda s: jnp.where(alive, s, -1e30),
            held.at[turn],
            soft.at[turn],
            inverse.at[turn],
        )

    block = lax.broadcasted_iota(jnp.int32, (GROUP, 128), 1) // PATCHES
    for i in range(8):
        unit, place = i // 4, i % 4
        made = None
        for f in range(4):
            a = of[f, :, unit * 128 : unit * 128 + 128]
            by = (f - place) * PATCHES % 128
            if by:
                a = pltpu.roll(a, by, 1)
            made = a if made is None else jnp.where(block == f, a, made)
        if before:
            out[i, 1] = made.astype(BF16)
        else:
            out[i] = made.astype(BF16)


def spatial(parts, info, rays, ray_weight, mod, w_own, w_sib, videos, before=()):
    vmem = pl.BlockSpec(memory_space=pltpu.VMEM)
    far = pl.BlockSpec(memory_space=pl.ANY)
    frames = sum(parts)
    return pl.pallas_call(
        functools.partial(spatial_kernel, parts, len(before)),
        out_shape=[
            jax.ShapeDtypeStruct((8, 2, GROUP, 128) if before else (8, GROUP, 128), BF16),
            jax.ShapeDtypeStruct((2, 4, PATCHES, D), BF16),
        ],
        in_specs=[pl.BlockSpec(memory_space=pltpu.SMEM)] + [vmem] * 3 + [far] * 2 + [vmem] * (len(parts) + len(before)),
        out_specs=[vmem, vmem],
        scratch_shapes=[
            pltpu.VMEM((TOKENS, D), F32),
            pltpu.VMEM((D, 3 * PAD), BF16),
            pltpu.SemaphoreType.DMA((2,)),
            pltpu.VMEM((2, TOKENS, D), BF16),
            pltpu.VMEM((2, TOKENS, 2 * PAD), BF16),
            pltpu.VMEM((2, PAD, TOKENS), BF16),
            pltpu.VMEM((4, GROUP, TOKENS), F32),
            pltpu.VMEM((2, GROUP_HEADS, TOKENS, TOKENS), F32),
            pltpu.VMEM((2, GROUP_HEADS, TOKENS, TOKENS), BF16),
            pltpu.VMEM((2, GROUP_HEADS, 1, TOKENS), F32),
        ],
        compiler_params=pltpu.CompilerParams(vmem_limit_bytes=VMEM_LIMIT),
        cost_estimate=pl.CostEstimate(
            flops=frames * 2 * TOKENS * D * 3 * PAD, bytes_accessed=8_000_000, transcendentals=frames * 4 * 65536
        ),
    )(info, rays, ray_weight, mod, w_own, w_sib, *videos, *before)


def turn_kernel(info, order, *refs):
    pieces, outs, held = refs[:5], refs[5:-1], refs[-1]
    y = info[5]
    span = ZS * ROWS
    far = lax.rem(y + 2, YS) * span
    starts = [y * span, lax.rem(y + 3, YS) * span, lax.rem(y + 1, YS) * span, far, far + span // 2]
    for start, piece in zip(starts, pieces):
        held[pl.ds(pl.multiple_of(start, 16), piece.shape[0]), :] = piece[...]
    for n, out in enumerate(outs):
        made = jnp.dot(order[...], held[:, n * HALF : n * HALF + HALF], preferred_element_type=F32)
        out[...] = made.astype(BF16)


def turn(info, order, pieces):
    vmem = pl.BlockSpec(memory_space=pltpu.VMEM)
    width = pieces[0].shape[1]
    return pl.pallas_call(
        turn_kernel,
        out_shape=[jax.ShapeDtypeStruct((D, HALF), BF16)] * (width // HALF),
        in_specs=[pl.BlockSpec(memory_space=pltpu.SMEM)] + [vmem] * 6,
        out_specs=[vmem] * (width // HALF),
        scratch_shapes=[pltpu.VMEM((D, width), BF16)],
        compiler_params=pltpu.CompilerParams(vmem_limit_bytes=VMEM_LIMIT),
        cost_estimate=pl.CostEstimate(flops=2 * D * D * width, bytes_accessed=8_000_000, transcendentals=0),
    )(info, order, *pieces)


def temporal_kernel(
    info, rays, ray_weight, mod, ve_own, ve_sib, vl_own, vl_sib, mixed_in, s_own, s_sib, o_own, o_sib, t_own, t_sib,
    out, wq, wo, mix_t, proj, mid, normed, packed, vt, bias, held, soft, inverse, sems,
):
    t, core, x, cameras = info[0], info[1], info[2], info[3]
    other = 1 - core
    q_copies = [
        pltpu.make_async_copy(t_own, wq.at[0], sems.at[0]),
        pltpu.make_async_copy(t_sib, wq.at[1], sems.at[1]),
    ]
    out_copies = [
        pltpu.make_async_copy(o_own, wo.at[0], sems.at[2]),
        pltpu.make_async_copy(o_sib, wo.at[1], sems.at[3]),
    ]
    for copy in q_copies + out_copies:
        copy.start()

    for source in range(8):
        sx, sc = source // 2, source % 2
        both = jnp.concatenate([mixed_in[source, 0], mixed_in[source, 1]], axis=1)
        if sx:
            both = pltpu.roll(both.astype(F32), sx * 64, 1).astype(BF16)
        mix_t[sc, sx * GROUP : sx * GROUP + GROUP, :] = both
    key = lax.broadcasted_iota(jnp.int32, (128, 128), 0)
    query = lax.broadcasted_iota(jnp.int32, (128, 128), 1)
    bias[...] = jnp.where(key % 8 == query % 8, 0.0, -1e30)

    def project(half, weights):
        mixed = mix_t[half]
        rows = slice(half * TOKENS, half * TOKENS + TOKENS)
        dims = (((0,), (0,)), ((), ()))
        for which, w in zip((core, other), weights):
            to = pl.ds(pl.multiple_of(which * (HALF - 128), 128), HALF)
            proj[rows, to] = lax.dot_general(mixed, w[...], dims, preferred_element_type=F32)

    for half in range(2):
        project(half, (s_own, s_sib))

    here = rays[pl.ds(pl.multiple_of(t * PATCHES, PATCHES), PATCHES), :]
    ray = ray_sum(here, ray_weight[...])
    gate, shift, scale = mod[2:3, :], mod[3:4, :], 1.0 + mod[4:5, :]

    def slab(j, which, video):
        pair = which * 4 + lax.rem(x + j, XS)
        middles, norms = [], []
        for f in range(2):
            h = video[2 * (j % 2) + f].astype(F32) + ray
            p = proj[pl.ds(pl.multiple_of(pair * 64 + f * PATCHES, PATCHES), PATCHES), :]
            middle = (h + gate * p).astype(BF16).astype(F32)
            middles.append(middle)
            norms.append(normalize(middle, scale, shift).astype(F32))
        for g in range(4):
            rows = pl.ds(pl.multiple_of(g * 128 + pair * 16, 16), 16)
            cut = slice(g * 8, g * 8 + 8)
            mid[rows, :] = jnp.concatenate([m[cut] for m in middles], axis=0).astype(BF16)
            normed[rows, :] = jnp.concatenate([m[cut] for m in norms], axis=0).astype(BF16)

    for j in range(4):
        slab(j, core, ve_own if j < 2 else vl_own)
        slab(j, other, ve_sib if j < 2 else vl_sib)
    for which, copy in ((core, q_copies[0]), (other, q_copies[1])):
        copy.wait()
        w = wq.at[0] if copy is q_copies[0] else wq.at[1]
        for n in range(TQ // 256):
            to = pl.ds(pl.multiple_of(which * TQ_STEP + n * 256, 128), 256)
            made = jnp.dot(normed[...], w[:, n * 256 : n * 256 + 256], preferred_element_type=F32)
            packed[:, to] = made.astype(BF16)
    for copy in out_copies:
        copy.wait()
    for half in range(2):
        for g in (2 * half, 2 * half + 1):
            rows = slice(g * 128, g * 128 + 128)
            vt[g] = jnp.transpose(packed[rows, 2 * D :])
            lanes = slice((g % 2) * 128, (g % 2) * 128 + 128)
            mix_t[half, :, lanes] = attend(
                lambda lo, hi: packed[rows, lo:hi],
                lambda lo, hi: packed[rows, D + lo : D + hi],
                lambda lo, hi: vt[g, lo:hi, :],
                HEADS,
                lambda s: s + bias[...],
                held.at[g],
                soft.at[g],
                inverse.at[g],
            ).astype(BF16)
        project(half, (wo.at[0], wo.at[1]))
    alive = jnp.where(t < cameras, 1.0, 0.0)
    last_gate = mod[5:6, :]
    for target in range(8):
        pair = target % 2 * 4 + target // 2
        for g in range(4):
            rows = slice(g * 128 + pair * 16, g * 128 + pair * 16 + 16)
            done = (mid[rows, :].astype(F32) + last_gate * proj[rows, :]) * alive
            for f in range(2):
                out[target, f, g * 8 : g * 8 + 8, :] = done[f * 8 : f * 8 + 8].astype(BF16)


def temporal(info, rays, ray_weight, mod, ve_own, ve_sib, vl_own, vl_sib, mixed_in, s_own, s_sib, o_own, o_sib, t_own, t_sib):
    vmem = pl.BlockSpec(memory_space=pltpu.VMEM)
    far = pl.BlockSpec(memory_space=pl.ANY)
    return pl.pallas_call(
        temporal_kernel,
        out_shape=jax.ShapeDtypeStruct((8, 2, PATCHES, D), BF16),
        in_specs=[pl.BlockSpec(memory_space=pltpu.SMEM)] + [vmem] * 10 + [far] * 4,
        out_specs=vmem,
        scratch_shapes=[
            pltpu.VMEM((2, D, TQ), BF16),
            pltpu.VMEM((2, D, HALF), BF16),
            pltpu.VMEM((2, D, TOKENS), BF16),
            pltpu.VMEM((2 * TOKENS, D), F32),
            pltpu.VMEM((2 * TOKENS, D), BF16),
            pltpu.VMEM((2 * TOKENS, D), BF16),
            pltpu.VMEM((2 * TOKENS, 3 * D), BF16),
            pltpu.VMEM((4, D, 128), BF16),
            pltpu.VMEM((128, 128), F32),
            pltpu.VMEM((4, HEADS, 128, 128), F32),
            pltpu.VMEM((4, HEADS, 128, 128), BF16),
            pltpu.VMEM((4, HEADS, 1, 128), F32),
            pltpu.SemaphoreType.DMA((4,)),
        ],
        compiler_params=pltpu.CompilerParams(vmem_limit_bytes=VMEM_LIMIT),
        cost_estimate=pl.CostEstimate(flops=16_000_000_000, bytes_accessed=24_000_000, transcendentals=2_100_000),
    )(info, rays, ray_weight, mod, ve_own, ve_sib, vl_own, vl_sib, mixed_in, s_own, s_sib, o_own, o_sib, t_own, t_sib)


def on_device(
    video,
    cameras,
    rays,
    ray_weight,
    modulation,
    spatial_qkv,
    spatial_out,
    temporal_qkv,
    temporal_out,
):
    t = lax.axis_index("tm")
    clip = lax.axis_index("clip")
    x, core = t // 2, t % 2
    z, y = clip // YS, clip % YS
    info = jnp.stack([t, core, x, cameras[0], z, y]).astype(jnp.int32)
    mod = modulation[0].astype(F32)
    rays_t = rays.T
    zgroups = [[zz * YS + yy for zz in range(ZS)] for yy in range(YS)]

    def columns(a, start, size):
        return lax.dynamic_slice_in_dim(a, start, size, axis=1)

    zgroups = [[zz * YS + yy for zz in range(ZS)] for yy in range(YS)]
    ygroups = [[zz * YS + yy for yy in range(YS)] for zz in range(ZS)]

    def spread(a, groups):
        copies = jnp.broadcast_to(a[None], (len(groups[0]),) + a.shape)
        return lax.all_to_all(copies, "clip", 0, 0, axis_index_groups=groups, tiled=True).reshape(-1, a.shape[1])

    k = np.arange(D)
    goes = k // (ZS * ROWS) * ROWS + k // ROWS % ZS * (YS * ROWS) + k % ROWS
    order = jnp.asarray(k[:, None] == goes[None, :], BF16)
    low = core * (HALF - 128)

    frame_0, frame_1 = video[0:1], video[1:2]
    up_0, down_0 = x_send(frame_0, 1), x_send(frame_0, -1)

    tq = columns(temporal_qkv, core * TQ_STEP, TQ)
    tq = in_order([tq, y_send(tq, 1), y_send(tq, 2), y_send(tq, 3)], y)

    heads = [jnp.pad(columns(spatial_qkv, n * D + x * GROUP, GROUP), ((0, 0), (0, PAD - GROUP))) for n in range(3)]
    w = spread(columns(jnp.concatenate(heads, axis=1), low, HALF), zgroups)

    tq, w, up_0, down_0, frame_1, spatial_out = lax.optimization_barrier((tq, w, up_0, down_0, frame_1, spatial_out))
    t_own = lax.all_gather(tq, "clip", axis=0, tiled=True, axis_index_groups=zgroups)
    up_1, down_1, far_0 = x_send(frame_1, 1), x_send(frame_1, -1), x_send(up_0, 1)
    w_up, w_down = y_send(w, 1), y_send(w, -1)
    o = spread(jnp.concatenate([columns(spatial_out, low, HALF), columns(temporal_out, low, HALF)], axis=1), zgroups)

    w_up, w_down, up_1, down_1, far_0, o = lax.optimization_barrier((w_up, w_down, up_1, down_1, far_0, o))
    half = ZS * ROWS // 2
    w_far_up = y_send(w_up[:half], 1)
    w_far_down = y_send(w_down[half:], -1)
    far_1 = x_send(down_1, -1)
    o_up, o_down = y_send(o, 1), y_send(o, -1)
    (w_own,) = turn(info, order, [w, w_up, w_down, w_far_up, w_far_down])
    w_sib = core_swap(w_own)

    early, kept_e = spatial((2, 1, 1), info, rays_t, ray_weight, mod, w_own, w_sib, [video, down_0, down_1])
    o_up, o_down, far_1, early = lax.optimization_barrier((o_up, o_down, far_1, early))
    o_far_up = y_send(o_up[:half], 1)
    o_far_down = y_send(o_down[half:], -1)
    ve_sib = core_swap(kept_e[1])

    mixed, kept_l = spatial(
        (1, 1, 1, 1), info, rays_t, ray_weight, mod, w_own, w_sib, [far_0, far_1, up_0, up_1], [early]
    )
    t_own, o_far_up, o_far_down, mixed = lax.optimization_barrier((t_own, o_far_up, o_far_down, mixed))
    mixed = lax.all_to_all(mixed, "tm", split_axis=0, concat_axis=0, tiled=True)
    t_sib = core_swap(t_own)
    vl_sib = core_swap(kept_l[1])
    s_own, o_own = turn(info, order, [o, o_up, o_down, o_far_up, o_far_down])
    s_sib, o_sib = core_swap(s_own), core_swap(o_own)

    result = temporal(
        info, rays_t, ray_weight, mod, kept_e[0], ve_sib, kept_l[0], vl_sib, mixed,
        s_own, s_sib, o_own, o_sib, t_own, t_sib,
    )
    result = lax.all_to_all(result, "tm", split_axis=0, concat_axis=0, tiled=True)
    return jnp.transpose(result, (1, 0, 2, 3)).reshape(2, TOKENS, D)


def solution(mesh):
    placed = (
        P("tm", "clip", None),
        P("clip"),
        P(None, "clip"),
        P(),
        P("clip", None, None),
        P("clip", None),
        P("clip", None),
        P("clip", None),
        P("clip", None),
    )
    return jax.shard_map(
        on_device, mesh=mesh, in_specs=placed, out_specs=P("tm", "clip", None), check_vma=False
    )
```

```python
import functools

import jax
import jax.numpy as jnp
import numpy as np
from jax import lax
from jax.experimental import pallas as pl
from jax.experimental.pallas import tpu as pltpu
from jax.sharding import PartitionSpec as P

D = 1152
HEAD = 72
HEADS = 16
PATCHES = 32
TOKENS = 256
ROWS = 36
XS = 4
ZS = 8
YS = 4
GROUP_HEADS = HEADS // XS
GROUP = GROUP_HEADS * HEAD
PAD = 384
HALF = 640
TQ = 1792
TQ_STEP = 1664
EPS = 1e-6
SOFT = HEAD ** (-0.5) * 1.4426950408889634
F32 = jnp.float32
BF16 = jnp.bfloat16
VMEM_LIMIT = 52 * 1024 * 1024
SMALL = pl.CostEstimate(flops=1000, bytes_accessed=1000, transcendentals=0)


def z_send(a, s):
    pairs = [(z * YS + y, (z + s) % ZS * YS + y) for z in range(ZS) for y in range(YS)]
    return lax.ppermute(a, "clip", pairs)


def y_send(a, s):
    pairs = [(z * YS + y, z * YS + (y + s) % YS) for z in range(ZS) for y in range(YS)]
    return lax.ppermute(a, "clip", pairs)


def x_send(a, s):
    pairs = [(x * 2 + c, (x + s) % XS * 2 + c) for x in range(XS) for c in range(2)]
    return lax.ppermute(a, "tm", pairs)


def core_swap(a):
    return lax.ppermute(a, "tm", [(t, t ^ 1) for t in range(2 * XS)])


def in_order(pieces, me):
    n = len(pieces)
    back = pieces[::-1]
    both = jnp.stack(back + back[:-1])
    picked = lax.dynamic_slice_in_dim(both, n - 1 - me, n, axis=0)
    return picked.reshape(-1, pieces[0].shape[-1])


def spread(a, groups):
    copies = jnp.broadcast_to(a[None], (len(groups[0]),) + a.shape)
    return lax.all_to_all(copies, "clip", 0, 0, axis_index_groups=groups, tiled=True).reshape(-1, a.shape[1])


def attend(queries, keys, values_t, heads, masked, held, soft, inverse):
    for h in range(heads):
        first, last = h * HEAD, h * HEAD + HEAD - 1
        lo, hi = first // 128 * 128, last // 128 * 128 + 128
        lane = lax.broadcasted_iota(jnp.int32, (1, hi - lo), 1) + lo
        own = jnp.logical_and(lane >= first, lane <= last)
        q = jnp.where(own, queries(lo, hi), jnp.zeros((), BF16))
        held[h] = lax.dot_general(keys(lo, hi), q, (((1,), (1,)), ((), ())), preferred_element_type=F32)
    for h in range(heads):
        s = masked(held[h])
        m = jnp.max(s, axis=0, keepdims=True)
        e = jnp.exp2((s - m) * SOFT)
        inverse[h] = 1.0 / jnp.sum(e, axis=0, keepdims=True)
        soft[h] = e.astype(BF16)
    outs = []
    for h in range(heads):
        first = h * HEAD
        start = first // 16 * 16
        o = jnp.dot(values_t(start, start + 80), soft[h], preferred_element_type=F32) * inverse[h]
        outs.append(o[first - start : first - start + HEAD])
    return jnp.concatenate(outs, axis=0)


def normalize(h, scale, shift):
    center = jnp.mean(h, axis=-1, keepdims=True)
    d = h - center
    spread = jnp.mean(d * d, axis=-1, keepdims=True)
    return (d * lax.rsqrt(spread + EPS) * scale + shift).astype(BF16)


def ray_sum(rays, weight):
    total = rays[:, 0:1] * weight[0:1, :]
    for k in range(1, 6):
        total += rays[:, k : k + 1] * weight[k : k + 1, :]
    return total


def spatial_kernel(parts, before, *refs):
    info, rays, ray_weight, mod, w_own, w_sib = refs[:6]
    videos = refs[6 : 6 + len(parts)]
    refs = refs[6 + len(parts) :]
    if before:
        old, out, kept = refs[:3]
        refs = refs[3:]
        out[:, 0] = old[...]
    else:
        out, kept = refs[:2]
        refs = refs[2:]
    ray, wp, sems, normed, packed, vt, of, held, soft, inverse = refs
    t, core, cameras = info[0], info[1], info[3]

    def copies(left, right):
        return [
            pltpu.make_async_copy(left, wp.at[:, 0:HALF], sems.at[0]),
            pltpu.make_async_copy(right.at[:, 128:HALF], wp.at[:, HALF:], sems.at[1]),
        ]

    @pl.when(core == 0)
    def _():
        for copy in copies(w_own, w_sib):
            copy.start()

    @pl.when(core == 1)
    def _():
        for copy in copies(w_sib, w_own):
            copy.start()

    ray[...] = ray_sum(rays[...], ray_weight[...])
    scale = 1.0 + mod[1:2, :]
    shift = mod[0:1, :]
    alive = lax.broadcasted_iota(jnp.int32, (TOKENS, TOKENS), 0) < cameras * PATCHES

    frames = [(v, f) for v, n in zip(videos, parts) for f in range(n)]

    def norm_frame(slot):
        video, frame = frames[slot]
        for r in range(TOKENS // 32):
            rows = slice(r * 32, r * 32 + 32)
            h = video[frame, rows, :].astype(F32) + ray[rows, :]
            normed[slot % 2, rows, :] = normalize(h, scale, shift)

    for who, owner in enumerate((t, t + 1 - 2 * core)):
        mine = pl.ds(pl.multiple_of(owner * PATCHES, PATCHES), PATCHES)
        for slot, (video, frame) in enumerate(frames):
            kept[who, slot] = video[frame, mine, :]
    norm_frame(0)
    for copy in copies(w_own, w_sib):
        copy.wait()
    for slot in range(4):
        turn = slot % 2
        made = jnp.dot(normed[turn], wp[...], preferred_element_type=F32)
        packed[turn] = made[:, : 2 * PAD].astype(BF16)
        vt[turn] = jnp.transpose(made[:, 2 * PAD :]).astype(BF16)
        if slot < 3:
            norm_frame(slot + 1)
        of[slot] = attend(
            lambda lo, hi: packed[turn, :, lo:hi],
            lambda lo, hi: packed[turn, :, PAD + lo : PAD + hi],
            lambda lo, hi: vt[turn, lo:hi, :],
            GROUP_HEADS,
            lambda s: jnp.where(alive, s, -1e30),
            held.at[turn],
            soft.at[turn],
            inverse.at[turn],
        )

    block = lax.broadcasted_iota(jnp.int32, (GROUP, 128), 1) // PATCHES
    for i in range(8):
        unit, place = i // 4, i % 4
        made = None
        for f in range(4):
            a = of[f, :, unit * 128 : unit * 128 + 128]
            by = (f - place) * PATCHES % 128
            if by:
                a = pltpu.roll(a, by, 1)
            made = a if made is None else jnp.where(block == f, a, made)
        if before:
            out[i, 1] = made.astype(BF16)
        else:
            out[i] = made.astype(BF16)


def spatial(parts, info, rays, ray_weight, mod, w_own, w_sib, videos, before=()):
    vmem = pl.BlockSpec(memory_space=pltpu.VMEM)
    far = pl.BlockSpec(memory_space=pl.ANY)
    frames = sum(parts)
    return pl.pallas_call(
        functools.partial(spatial_kernel, parts, len(before)),
        out_shape=[
            jax.ShapeDtypeStruct((8, 2, GROUP, 128) if before else (8, GROUP, 128), BF16),
            jax.ShapeDtypeStruct((2, 4, PATCHES, D), BF16),
        ],
        in_specs=[pl.BlockSpec(memory_space=pltpu.SMEM)] + [vmem] * 3 + [far] * 2 + [vmem] * (len(parts) + len(before)),
        out_specs=[vmem, vmem],
        scratch_shapes=[
            pltpu.VMEM((TOKENS, D), F32),
            pltpu.VMEM((D, 3 * PAD), BF16),
            pltpu.SemaphoreType.DMA((2,)),
            pltpu.VMEM((2, TOKENS, D), BF16),
            pltpu.VMEM((2, TOKENS, 2 * PAD), BF16),
            pltpu.VMEM((2, PAD, TOKENS), BF16),
            pltpu.VMEM((4, GROUP, TOKENS), F32),
            pltpu.VMEM((2, GROUP_HEADS, TOKENS, TOKENS), F32),
            pltpu.VMEM((2, GROUP_HEADS, TOKENS, TOKENS), BF16),
            pltpu.VMEM((2, GROUP_HEADS, 1, TOKENS), F32),
        ],
        compiler_params=pltpu.CompilerParams(vmem_limit_bytes=VMEM_LIMIT),
        cost_estimate=SMALL,
    )(info, rays, ray_weight, mod, w_own, w_sib, *videos, *before)


def turn_kernel(info, order, *refs):
    pieces, outs, held = refs[:5], refs[5:-1], refs[-1]
    y = info[5]
    span = ZS * ROWS
    far = lax.rem(y + 2, YS) * span
    starts = [y * span, lax.rem(y + 3, YS) * span, lax.rem(y + 1, YS) * span, far, far + span // 2]
    for start, piece in zip(starts, pieces):
        held[pl.ds(pl.multiple_of(start, 16), piece.shape[0]), :] = piece[...]
    for n, out in enumerate(outs):
        made = jnp.dot(order[...], held[:, n * HALF : n * HALF + HALF], preferred_element_type=F32)
        out[...] = made.astype(BF16)


def turn(info, order, pieces):
    vmem = pl.BlockSpec(memory_space=pltpu.VMEM)
    width = pieces[0].shape[1]
    return pl.pallas_call(
        turn_kernel,
        out_shape=[jax.ShapeDtypeStruct((D, HALF), BF16)] * (width // HALF),
        in_specs=[pl.BlockSpec(memory_space=pltpu.SMEM)] + [vmem] * 6,
        out_specs=[vmem] * (width // HALF),
        scratch_shapes=[pltpu.VMEM((D, width), BF16)],
        compiler_params=pltpu.CompilerParams(vmem_limit_bytes=VMEM_LIMIT),
        cost_estimate=SMALL,
    )(info, order, *pieces)


def temporal_kernel(
    info, rays, ray_weight, mod, ve_own, ve_sib, vl_own, vl_sib, mixed_in, s_own, s_sib, o_own, o_sib, t_own, t_sib,
    out, wq, wo, mix_t, proj, mid, normed, packed, vt, bias, held, soft, inverse, sems,
):
    t, core, x, cameras = info[0], info[1], info[2], info[3]
    other = 1 - core
    q_copies = [
        pltpu.make_async_copy(t_own, wq.at[0], sems.at[0]),
        pltpu.make_async_copy(t_sib, wq.at[1], sems.at[1]),
    ]
    out_copies = [
        pltpu.make_async_copy(o_own, wo.at[0], sems.at[2]),
        pltpu.make_async_copy(o_sib, wo.at[1], sems.at[3]),
    ]
    for copy in q_copies + out_copies:
        copy.start()

    for source in range(8):
        sx, sc = source // 2, source % 2
        both = jnp.concatenate([mixed_in[source, 0], mixed_in[source, 1]], axis=1)
        if sx:
            both = pltpu.roll(both.astype(F32), sx * 64, 1).astype(BF16)
        mix_t[sc, sx * GROUP : sx * GROUP + GROUP, :] = both
    key = lax.broadcasted_iota(jnp.int32, (128, 128), 0)
    query = lax.broadcasted_iota(jnp.int32, (128, 128), 1)
    bias[...] = jnp.where(key % 8 == query % 8, 0.0, -1e30)

    def project(half, weights):
        mixed = mix_t[half]
        rows = slice(half * TOKENS, half * TOKENS + TOKENS)
        dims = (((0,), (0,)), ((), ()))
        for which, w in zip((core, other), weights):
            to = pl.ds(pl.multiple_of(which * (HALF - 128), 128), HALF)
            proj[rows, to] = lax.dot_general(mixed, w[...], dims, preferred_element_type=F32)

    for half in range(2):
        project(half, (s_own, s_sib))

    here = rays[pl.ds(pl.multiple_of(t * PATCHES, PATCHES), PATCHES), :]
    ray = ray_sum(here, ray_weight[...])
    gate, shift, scale = mod[2:3, :], mod[3:4, :], 1.0 + mod[4:5, :]

    def slab(j, which, video):
        pair = which * 4 + lax.rem(x + j, XS)
        middles, norms = [], []
        for f in range(2):
            h = video[2 * (j % 2) + f].astype(F32) + ray
            p = proj[pl.ds(pl.multiple_of(pair * 64 + f * PATCHES, PATCHES), PATCHES), :]
            middle = (h + gate * p).astype(BF16).astype(F32)
            middles.append(middle)
            norms.append(normalize(middle, scale, shift).astype(F32))
        for g in range(4):
            rows = pl.ds(pl.multiple_of(g * 128 + pair * 16, 16), 16)
            cut = slice(g * 8, g * 8 + 8)
            mid[rows, :] = jnp.concatenate([m[cut] for m in middles], axis=0).astype(BF16)
            normed[rows, :] = jnp.concatenate([m[cut] for m in norms], axis=0).astype(BF16)

    for j in range(4):
        slab(j, core, ve_own if j < 2 else vl_own)
        slab(j, other, ve_sib if j < 2 else vl_sib)
    for which, copy in ((core, q_copies[0]), (other, q_copies[1])):
        copy.wait()
        w = wq.at[0] if copy is q_copies[0] else wq.at[1]
        for n in range(TQ // 256):
            to = pl.ds(pl.multiple_of(which * TQ_STEP + n * 256, 128), 256)
            made = jnp.dot(normed[...], w[:, n * 256 : n * 256 + 256], preferred_element_type=F32)
            packed[:, to] = made.astype(BF16)
    for copy in out_copies:
        copy.wait()
    for half in range(2):
        for g in (2 * half, 2 * half + 1):
            rows = slice(g * 128, g * 128 + 128)
            vt[g] = jnp.transpose(packed[rows, 2 * D :])
            lanes = slice((g % 2) * 128, (g % 2) * 128 + 128)
            mix_t[half, :, lanes] = attend(
                lambda lo, hi: packed[rows, lo:hi],
                lambda lo, hi: packed[rows, D + lo : D + hi],
                lambda lo, hi: vt[g, lo:hi, :],
                HEADS,
                lambda s: s + bias[...],
                held.at[g],
                soft.at[g],
                inverse.at[g],
            ).astype(BF16)
        project(half, (wo.at[0], wo.at[1]))
    alive = jnp.where(t < cameras, 1.0, 0.0)
    last_gate = mod[5:6, :]
    for target in range(8):
        pair = target % 2 * 4 + target // 2
        for g in range(4):
            rows = slice(g * 128 + pair * 16, g * 128 + pair * 16 + 16)
            done = (mid[rows, :].astype(F32) + last_gate * proj[rows, :]) * alive
            for f in range(2):
                out[target, f, g * 8 : g * 8 + 8, :] = done[f * 8 : f * 8 + 8].astype(BF16)


def temporal(info, rays, ray_weight, mod, ve_own, ve_sib, vl_own, vl_sib, mixed_in, s_own, s_sib, o_own, o_sib, t_own, t_sib):
    vmem = pl.BlockSpec(memory_space=pltpu.VMEM)
    far = pl.BlockSpec(memory_space=pl.ANY)
    return pl.pallas_call(
        temporal_kernel,
        out_shape=jax.ShapeDtypeStruct((8, 2, PATCHES, D), BF16),
        in_specs=[pl.BlockSpec(memory_space=pltpu.SMEM)] + [vmem] * 10 + [far] * 4,
        out_specs=vmem,
        scratch_shapes=[
            pltpu.VMEM((2, D, TQ), BF16),
            pltpu.VMEM((2, D, HALF), BF16),
            pltpu.VMEM((2, D, TOKENS), BF16),
            pltpu.VMEM((2 * TOKENS, D), F32),
            pltpu.VMEM((2 * TOKENS, D), BF16),
            pltpu.VMEM((2 * TOKENS, D), BF16),
            pltpu.VMEM((2 * TOKENS, 3 * D), BF16),
            pltpu.VMEM((4, D, 128), BF16),
            pltpu.VMEM((128, 128), F32),
            pltpu.VMEM((4, HEADS, 128, 128), F32),
            pltpu.VMEM((4, HEADS, 128, 128), BF16),
            pltpu.VMEM((4, HEADS, 1, 128), F32),
            pltpu.SemaphoreType.DMA((4,)),
        ],
        compiler_params=pltpu.CompilerParams(vmem_limit_bytes=VMEM_LIMIT),
        cost_estimate=SMALL,
    )(info, rays, ray_weight, mod, ve_own, ve_sib, vl_own, vl_sib, mixed_in, s_own, s_sib, o_own, o_sib, t_own, t_sib)


def on_device(
    video,
    cameras,
    rays,
    ray_weight,
    modulation,
    spatial_qkv,
    spatial_out,
    temporal_qkv,
    temporal_out,
):
    t = lax.axis_index("tm")
    clip = lax.axis_index("clip")
    x, core = t // 2, t % 2
    z, y = clip // YS, clip % YS
    info = jnp.stack([t, core, x, cameras[0], z, y]).astype(jnp.int32)
    mod = modulation[0].astype(F32)
    rays_t = rays.T
    zgroups = [[zz * YS + yy for zz in range(ZS)] for yy in range(YS)]

    def columns(a, start, size):
        return lax.dynamic_slice_in_dim(a, start, size, axis=1)

    zgroups = [[zz * YS + yy for zz in range(ZS)] for yy in range(YS)]
    ygroups = [[zz * YS + yy for yy in range(YS)] for zz in range(ZS)]

    def spread(a, groups):
        copies = jnp.broadcast_to(a[None], (len(groups[0]),) + a.shape)
        return lax.all_to_all(copies, "clip", 0, 0, axis_index_groups=groups, tiled=True).reshape(-1, a.shape[1])

    k = np.arange(D)
    goes = k // (ZS * ROWS) * ROWS + k // ROWS % ZS * (YS * ROWS) + k % ROWS
    order = jnp.asarray(k[:, None] == goes[None, :], BF16)
    low = core * (HALF - 128)

    frame_0, frame_1 = video[0:1], video[1:2]
    up_0, down_0 = x_send(frame_0, 1), x_send(frame_0, -1)

    tq = columns(temporal_qkv, core * TQ_STEP, TQ)
    tq = in_order([tq, y_send(tq, 1), y_send(tq, 2), y_send(tq, 3)], y)

    heads = [jnp.pad(columns(spatial_qkv, n * D + x * GROUP, GROUP), ((0, 0), (0, PAD - GROUP))) for n in range(3)]
    w = spread(columns(jnp.concatenate(heads, axis=1), low, HALF), zgroups)

    tq, w, up_0, down_0, frame_1, spatial_out = lax.optimization_barrier((tq, w, up_0, down_0, frame_1, spatial_out))
    t_own = lax.all_gather(tq, "clip", axis=0, tiled=True, axis_index_groups=zgroups)
    up_1, down_1, far_0 = x_send(frame_1, 1), x_send(frame_1, -1), x_send(up_0, 1)
    w_up, w_down = y_send(w, 1), y_send(w, -1)
    o = spread(jnp.concatenate([columns(spatial_out, low, HALF), columns(temporal_out, low, HALF)], axis=1), zgroups)

    w_up, w_down, up_1, down_1, far_0 = lax.optimization_barrier((w_up, w_down, up_1, down_1, far_0))
    half = ZS * ROWS // 2
    w_far_up = y_send(w_up[:half], 1)
    w_far_down = y_send(w_down[half:], -1)
    far_1 = x_send(down_1, -1)
    (w_own,) = turn(info, order, [w, w_up, w_down, w_far_up, w_far_down])
    w_sib = core_swap(w_own)

    early, kept_e = spatial((2, 1, 1), info, rays_t, ray_weight, mod, w_own, w_sib, [video, down_0, down_1])
    o, far_1, early = lax.optimization_barrier((o, far_1, early))
    o_up, o_down = y_send(o, 1), y_send(o, -1)
    ve_sib = core_swap(kept_e[1])

    mixed, kept_l = spatial(
        (1, 1, 1, 1), info, rays_t, ray_weight, mod, w_own, w_sib, [far_0, far_1, up_0, up_1], [early]
    )
    t_own, o_up, o_down, mixed = lax.optimization_barrier((t_own, o_up, o_down, mixed))
    mixed = lax.all_to_all(mixed, "tm", split_axis=0, concat_axis=0, tiled=True)
    o_far_up = y_send(o_up[:half], 1)
    o_far_down = y_send(o_down[half:], -1)
    t_sib = core_swap(t_own)
    vl_sib = core_swap(kept_l[1])
    s_own, o_own = turn(info, order, [o, o_up, o_down, o_far_up, o_far_down])
    s_sib, o_sib = core_swap(s_own), core_swap(o_own)

    result = temporal(
        info, rays_t, ray_weight, mod, kept_e[0], ve_sib, kept_l[0], vl_sib, mixed,
        s_own, s_sib, o_own, o_sib, t_own, t_sib,
    )
    result = lax.all_to_all(result, "tm", split_axis=0, concat_axis=0, tiled=True)
    return jnp.transpose(result, (1, 0, 2, 3)).reshape(2, TOKENS, D)


def solution(mesh):
    placed = (
        P("tm", "clip", None),
        P("clip"),
        P(None, "clip"),
        P(),
        P("clip", None, None),
        P("clip", None),
        P("clip", None),
        P("clip", None),
        P("clip", None),
    )
    return jax.shard_map(
        on_device, mesh=mesh, in_specs=placed, out_specs=P("tm", "clip", None), check_vma=False
    )
```

```python
import functools

import jax
import jax.numpy as jnp
import numpy as np
from jax import lax
from jax.experimental import pallas as pl
from jax.experimental.pallas import tpu as pltpu
from jax.sharding import PartitionSpec as P

D = 1152
HEAD = 72
HEADS = 16
PATCHES = 32
TOKENS = 256
ROWS = 36
XS = 4
ZS = 8
YS = 4
GROUP_HEADS = HEADS // XS
GROUP = GROUP_HEADS * HEAD
PAD = 384
HALF = 640
TQ = 1792
TQ_STEP = 1664
EPS = 1e-6
SOFT = HEAD ** (-0.5) * 1.4426950408889634
F32 = jnp.float32
BF16 = jnp.bfloat16
VMEM_LIMIT = 52 * 1024 * 1024
SMALL = pl.CostEstimate(flops=1000, bytes_accessed=1000, transcendentals=0)


def z_send(a, s):
    pairs = [(z * YS + y, (z + s) % ZS * YS + y) for z in range(ZS) for y in range(YS)]
    return lax.ppermute(a, "clip", pairs)


def y_send(a, s):
    pairs = [(z * YS + y, z * YS + (y + s) % YS) for z in range(ZS) for y in range(YS)]
    return lax.ppermute(a, "clip", pairs)


def x_send(a, s):
    pairs = [(x * 2 + c, (x + s) % XS * 2 + c) for x in range(XS) for c in range(2)]
    return lax.ppermute(a, "tm", pairs)


def core_swap(a):
    return lax.ppermute(a, "tm", [(t, t ^ 1) for t in range(2 * XS)])


def in_order(pieces, me):
    n = len(pieces)
    back = pieces[::-1]
    both = jnp.stack(back + back[:-1])
    picked = lax.dynamic_slice_in_dim(both, n - 1 - me, n, axis=0)
    return picked.reshape(-1, pieces[0].shape[-1])


def spread(a, groups):
    copies = jnp.broadcast_to(a[None], (len(groups[0]),) + a.shape)
    return lax.all_to_all(copies, "clip", 0, 0, axis_index_groups=groups, tiled=True).reshape(-1, a.shape[1])


def attend(queries, keys, values_t, heads, masked, held, soft, inverse):
    for h in range(heads):
        first, last = h * HEAD, h * HEAD + HEAD - 1
        lo, hi = first // 128 * 128, last // 128 * 128 + 128
        lane = lax.broadcasted_iota(jnp.int32, (1, hi - lo), 1) + lo
        own = jnp.logical_and(lane >= first, lane <= last)
        q = jnp.where(own, queries(lo, hi), jnp.zeros((), BF16))
        held[h] = lax.dot_general(keys(lo, hi), q, (((1,), (1,)), ((), ())), preferred_element_type=F32)
    for h in range(heads):
        s = masked(held[h])
        m = jnp.max(s, axis=0, keepdims=True)
        e = jnp.exp2((s - m) * SOFT)
        inverse[h] = 1.0 / jnp.sum(e, axis=0, keepdims=True)
        soft[h] = e.astype(BF16)
    outs = []
    for h in range(heads):
        first = h * HEAD
        start = first // 16 * 16
        o = jnp.dot(values_t(start, start + 80), soft[h], preferred_element_type=F32) * inverse[h]
        outs.append(o[first - start : first - start + HEAD])
    return jnp.concatenate(outs, axis=0)


def normalize(h, scale, shift):
    center = jnp.mean(h, axis=-1, keepdims=True)
    d = h - center
    spread = jnp.mean(d * d, axis=-1, keepdims=True)
    return (d * lax.rsqrt(spread + EPS) * scale + shift).astype(BF16)


def ray_sum(rays, weight):
    total = rays[:, 0:1] * weight[0:1, :]
    for k in range(1, 6):
        total += rays[:, k : k + 1] * weight[k : k + 1, :]
    return total


def spatial_kernel(parts, before, *refs):
    info, rays, ray_weight, mod, w_own, w_sib = refs[:6]
    videos = refs[6 : 6 + len(parts)]
    refs = refs[6 + len(parts) :]
    if before:
        old, out, kept = refs[:3]
        refs = refs[3:]
        out[:, 0] = old[...]
    else:
        out, kept = refs[:2]
        refs = refs[2:]
    ray, wp, sems, normed, packed, vt, of, held, soft, inverse = refs
    t, core, cameras = info[0], info[1], info[3]

    def copies(left, right):
        return [
            pltpu.make_async_copy(left, wp.at[:, 0:HALF], sems.at[0]),
            pltpu.make_async_copy(right.at[:, 128:HALF], wp.at[:, HALF:], sems.at[1]),
        ]

    @pl.when(core == 0)
    def _():
        for copy in copies(w_own, w_sib):
            copy.start()

    @pl.when(core == 1)
    def _():
        for copy in copies(w_sib, w_own):
            copy.start()

    ray[...] = ray_sum(rays[...], ray_weight[...])
    scale = 1.0 + mod[1:2, :]
    shift = mod[0:1, :]
    alive = lax.broadcasted_iota(jnp.int32, (TOKENS, TOKENS), 0) < cameras * PATCHES

    frames = [(v, f) for v, n in zip(videos, parts) for f in range(n)]

    def norm_frame(slot):
        video, frame = frames[slot]
        for r in range(TOKENS // 32):
            rows = slice(r * 32, r * 32 + 32)
            h = video[frame, rows, :].astype(F32) + ray[rows, :]
            normed[slot % 2, rows, :] = normalize(h, scale, shift)

    for who, owner in enumerate((t, t + 1 - 2 * core)):
        mine = pl.ds(pl.multiple_of(owner * PATCHES, PATCHES), PATCHES)
        for slot, (video, frame) in enumerate(frames):
            kept[who, slot] = video[frame, mine, :]
    norm_frame(0)
    for copy in copies(w_own, w_sib):
        copy.wait()
    for slot in range(4):
        turn = slot % 2
        made = jnp.dot(normed[turn], wp[...], preferred_element_type=F32)
        packed[turn] = made[:, : 2 * PAD].astype(BF16)
        vt[turn] = jnp.transpose(made[:, 2 * PAD :]).astype(BF16)
        if slot < 3:
            norm_frame(slot + 1)
        of[slot] = attend(
            lambda lo, hi: packed[turn, :, lo:hi],
            lambda lo, hi: packed[turn, :, PAD + lo : PAD + hi],
            lambda lo, hi: vt[turn, lo:hi, :],
            GROUP_HEADS,
            lambda s: jnp.where(alive, s, -1e30),
            held.at[turn],
            soft.at[turn],
            inverse.at[turn],
        )

    block = lax.broadcasted_iota(jnp.int32, (GROUP, 128), 1) // PATCHES
    for i in range(8):
        unit, place = i // 4, i % 4
        made = None
        for f in range(4):
            a = of[f, :, unit * 128 : unit * 128 + 128]
            by = (f - place) * PATCHES % 128
            if by:
                a = pltpu.roll(a, by, 1)
            made = a if made is None else jnp.where(block == f, a, made)
        if before:
            out[i, 1] = made.astype(BF16)
        else:
            out[i] = made.astype(BF16)


def spatial(parts, info, rays, ray_weight, mod, w_own, w_sib, videos, before=()):
    vmem = pl.BlockSpec(memory_space=pltpu.VMEM)
    far = pl.BlockSpec(memory_space=pl.ANY)
    frames = sum(parts)
    return pl.pallas_call(
        functools.partial(spatial_kernel, parts, len(before)),
        out_shape=[
            jax.ShapeDtypeStruct((8, 2, GROUP, 128) if before else (8, GROUP, 128), BF16),
            jax.ShapeDtypeStruct((2, 4, PATCHES, D), BF16),
        ],
        in_specs=[pl.BlockSpec(memory_space=pltpu.SMEM)] + [vmem] * 3 + [far] * 2 + [vmem] * (len(parts) + len(before)),
        out_specs=[vmem, vmem],
        scratch_shapes=[
            pltpu.VMEM((TOKENS, D), F32),
            pltpu.VMEM((D, 3 * PAD), BF16),
            pltpu.SemaphoreType.DMA((2,)),
            pltpu.VMEM((2, TOKENS, D), BF16),
            pltpu.VMEM((2, TOKENS, 2 * PAD), BF16),
            pltpu.VMEM((2, PAD, TOKENS), BF16),
            pltpu.VMEM((4, GROUP, TOKENS), F32),
            pltpu.VMEM((2, GROUP_HEADS, TOKENS, TOKENS), F32),
            pltpu.VMEM((2, GROUP_HEADS, TOKENS, TOKENS), BF16),
            pltpu.VMEM((2, GROUP_HEADS, 1, TOKENS), F32),
        ],
        compiler_params=pltpu.CompilerParams(vmem_limit_bytes=VMEM_LIMIT),
        cost_estimate=SMALL,
    )(info, rays, ray_weight, mod, w_own, w_sib, *videos, *before)


def turn_kernel(info, order, *refs):
    pieces, outs, held = refs[:5], refs[5:-1], refs[-1]
    y = info[5]
    span = ZS * ROWS
    far = lax.rem(y + 2, YS) * span
    starts = [y * span, lax.rem(y + 3, YS) * span, lax.rem(y + 1, YS) * span, far, far + span // 2]
    for start, piece in zip(starts, pieces):
        held[pl.ds(pl.multiple_of(start, 16), piece.shape[0]), :] = piece[...]
    for n, out in enumerate(outs):
        made = jnp.dot(order[...], held[:, n * HALF : n * HALF + HALF], preferred_element_type=F32)
        out[...] = made.astype(BF16)


def turn(info, order, pieces):
    vmem = pl.BlockSpec(memory_space=pltpu.VMEM)
    width = pieces[0].shape[1]
    return pl.pallas_call(
        turn_kernel,
        out_shape=[jax.ShapeDtypeStruct((D, HALF), BF16)] * (width // HALF),
        in_specs=[pl.BlockSpec(memory_space=pltpu.SMEM)] + [vmem] * 6,
        out_specs=[vmem] * (width // HALF),
        scratch_shapes=[pltpu.VMEM((D, width), BF16)],
        compiler_params=pltpu.CompilerParams(vmem_limit_bytes=VMEM_LIMIT),
        cost_estimate=SMALL,
    )(info, order, *pieces)


def temporal_kernel(
    info, rays, ray_weight, mod, ve_own, ve_sib, vl_own, vl_sib, mixed_in, g_own, g_sib,
    out, wq, ws, wo, mix_t, proj, mid, normed, packed, vt, bias, held, soft, inverse, sems,
):
    t, core, x, cameras = info[0], info[1], info[2], info[3]
    other = 1 - core
    s_copies, q_copies, out_copies = [], [], []
    for which, g in enumerate((g_own, g_sib)):
        at = 0
        for k, (copies, to) in enumerate(((q_copies, wq), (s_copies, ws), (out_copies, wo))):
            width = to.shape[2]
            copies.append(pltpu.make_async_copy(g.at[:, at : at + width], to.at[which], sems.at[which * 3 + k]))
            at += width
    for copy in s_copies + q_copies + out_copies:
        copy.start()

    for source in range(8):
        sx, sc = source // 2, source % 2
        both = jnp.concatenate([mixed_in[source, 0], mixed_in[source, 1]], axis=1)
        if sx:
            both = pltpu.roll(both.astype(F32), sx * 64, 1).astype(BF16)
        mix_t[sc, sx * GROUP : sx * GROUP + GROUP, :] = both
    key = lax.broadcasted_iota(jnp.int32, (128, 128), 0)
    query = lax.broadcasted_iota(jnp.int32, (128, 128), 1)
    bias[...] = jnp.where(key % 8 == query % 8, 0.0, -1e30)

    def project(half, weights):
        mixed = mix_t[half]
        rows = slice(half * TOKENS, half * TOKENS + TOKENS)
        dims = (((0,), (0,)), ((), ()))
        for which, w in zip((core, other), weights):
            to = pl.ds(pl.multiple_of(which * (HALF - 128), 128), HALF)
            proj[rows, to] = lax.dot_general(mixed, w[...], dims, preferred_element_type=F32)

    for copy in s_copies:
        copy.wait()
    for half in range(2):
        project(half, (ws.at[0], ws.at[1]))

    here = rays[pl.ds(pl.multiple_of(t * PATCHES, PATCHES), PATCHES), :]
    ray = ray_sum(here, ray_weight[...])
    gate, shift, scale = mod[2:3, :], mod[3:4, :], 1.0 + mod[4:5, :]

    def slab(j, which, video):
        pair = which * 4 + lax.rem(x + j, XS)
        middles, norms = [], []
        for f in range(2):
            h = video[2 * (j % 2) + f].astype(F32) + ray
            p = proj[pl.ds(pl.multiple_of(pair * 64 + f * PATCHES, PATCHES), PATCHES), :]
            middle = (h + gate * p).astype(BF16).astype(F32)
            middles.append(middle)
            norms.append(normalize(middle, scale, shift).astype(F32))
        for g in range(4):
            rows = pl.ds(pl.multiple_of(g * 128 + pair * 16, 16), 16)
            cut = slice(g * 8, g * 8 + 8)
            mid[rows, :] = jnp.concatenate([m[cut] for m in middles], axis=0).astype(BF16)
            normed[rows, :] = jnp.concatenate([m[cut] for m in norms], axis=0).astype(BF16)

    for j in range(4):
        slab(j, core, ve_own if j < 2 else vl_own)
        slab(j, other, ve_sib if j < 2 else vl_sib)
    for which, copy in ((core, q_copies[0]), (other, q_copies[1])):
        copy.wait()
        w = wq.at[0] if copy is q_copies[0] else wq.at[1]
        for n in range(TQ // 256):
            to = pl.ds(pl.multiple_of(which * TQ_STEP + n * 256, 128), 256)
            made = jnp.dot(normed[...], w[:, n * 256 : n * 256 + 256], preferred_element_type=F32)
            packed[:, to] = made.astype(BF16)
    for copy in out_copies:
        copy.wait()
    for half in range(2):
        for g in (2 * half, 2 * half + 1):
            rows = slice(g * 128, g * 128 + 128)
            vt[g] = jnp.transpose(packed[rows, 2 * D :])
            lanes = slice((g % 2) * 128, (g % 2) * 128 + 128)
            mix_t[half, :, lanes] = attend(
                lambda lo, hi: packed[rows, lo:hi],
                lambda lo, hi: packed[rows, D + lo : D + hi],
                lambda lo, hi: vt[g, lo:hi, :],
                HEADS,
                lambda s: s + bias[...],
                held.at[g],
                soft.at[g],
                inverse.at[g],
            ).astype(BF16)
        project(half, (wo.at[0], wo.at[1]))
    alive = jnp.where(t < cameras, 1.0, 0.0)
    last_gate = mod[5:6, :]
    for target in range(8):
        pair = target % 2 * 4 + target // 2
        for g in range(4):
            rows = slice(g * 128 + pair * 16, g * 128 + pair * 16 + 16)
            done = (mid[rows, :].astype(F32) + last_gate * proj[rows, :]) * alive
            for f in range(2):
                out[target, f, g * 8 : g * 8 + 8, :] = done[f * 8 : f * 8 + 8].astype(BF16)


def temporal(info, rays, ray_weight, mod, ve_own, ve_sib, vl_own, vl_sib, mixed_in, g_own, g_sib):
    vmem = pl.BlockSpec(memory_space=pltpu.VMEM)
    far = pl.BlockSpec(memory_space=pl.ANY)
    return pl.pallas_call(
        temporal_kernel,
        out_shape=jax.ShapeDtypeStruct((8, 2, PATCHES, D), BF16),
        in_specs=[pl.BlockSpec(memory_space=pltpu.SMEM)] + [vmem] * 8 + [far] * 2,
        out_specs=vmem,
        scratch_shapes=[
            pltpu.VMEM((2, D, TQ), BF16),
            pltpu.VMEM((2, D, HALF), BF16),
            pltpu.VMEM((2, D, HALF), BF16),
            pltpu.VMEM((2, D, TOKENS), BF16),
            pltpu.VMEM((2 * TOKENS, D), F32),
            pltpu.VMEM((2 * TOKENS, D), BF16),
            pltpu.VMEM((2 * TOKENS, D), BF16),
            pltpu.VMEM((2 * TOKENS, 3 * D), BF16),
            pltpu.VMEM((4, D, 128), BF16),
            pltpu.VMEM((128, 128), F32),
            pltpu.VMEM((4, HEADS, 128, 128), F32),
            pltpu.VMEM((4, HEADS, 128, 128), BF16),
            pltpu.VMEM((4, HEADS, 1, 128), F32),
            pltpu.SemaphoreType.DMA((6,)),
        ],
        compiler_params=pltpu.CompilerParams(vmem_limit_bytes=VMEM_LIMIT),
        cost_estimate=SMALL,
    )(info, rays, ray_weight, mod, ve_own, ve_sib, vl_own, vl_sib, mixed_in, g_own, g_sib)


def on_device(
    video,
    cameras,
    rays,
    ray_weight,
    modulation,
    spatial_qkv,
    spatial_out,
    temporal_qkv,
    temporal_out,
):
    t = lax.axis_index("tm")
    clip = lax.axis_index("clip")
    x, core = t // 2, t % 2
    z, y = clip // YS, clip % YS
    info = jnp.stack([t, core, x, cameras[0], z, y]).astype(jnp.int32)
    mod = modulation[0].astype(F32)
    rays_t = rays.T
    zgroups = [[zz * YS + yy for zz in range(ZS)] for yy in range(YS)]

    def columns(a, start, size):
        return lax.dynamic_slice_in_dim(a, start, size, axis=1)

    zgroups = [[zz * YS + yy for zz in range(ZS)] for yy in range(YS)]
    ygroups = [[zz * YS + yy for yy in range(YS)] for zz in range(ZS)]

    def spread(a, groups):
        copies = jnp.broadcast_to(a[None], (len(groups[0]),) + a.shape)
        return lax.all_to_all(copies, "clip", 0, 0, axis_index_groups=groups, tiled=True).reshape(-1, a.shape[1])

    k = np.arange(D)
    goes = k // (ZS * ROWS) * ROWS + k // ROWS % ZS * (YS * ROWS) + k % ROWS
    order = jnp.asarray(k[:, None] == goes[None, :], BF16)
    low = core * (HALF - 128)

    x_up, x_down = x_send(video, 1), x_send(video, -1)

    heads = [jnp.pad(columns(spatial_qkv, n * D + x * GROUP, GROUP), ((0, 0), (0, PAD - GROUP))) for n in range(3)]
    w = spread(columns(jnp.concatenate(heads, axis=1), low, HALF), zgroups)

    g = jnp.concatenate(
        [
            columns(temporal_qkv, core * TQ_STEP, TQ),
            columns(spatial_out, low, HALF),
            columns(temporal_out, low, HALF),
        ],
        axis=1,
    )
    g = in_order([g, y_send(g, 1), y_send(g, 2), y_send(g, 3)], y)
    g_own = lax.all_gather(g, "clip", axis=0, tiled=True, axis_index_groups=zgroups)

    w, x_up, x_down = lax.optimization_barrier((w, x_up, x_down))
    w_up, w_down = y_send(w, 1), y_send(w, -1)
    far_0, far_1 = x_send(x_up[0:1], 1), x_send(x_down[1:2], -1)
    half = ZS * ROWS // 2
    w_far_up = y_send(w_up[:half], 1)
    w_far_down = y_send(w_down[half:], -1)
    (w_own,) = turn(info, order, [w, w_up, w_down, w_far_up, w_far_down])
    w_sib = core_swap(w_own)

    early, kept_e = spatial((2, 2), info, rays_t, ray_weight, mod, w_own, w_sib, [video, x_down])
    far_0, far_1, early = lax.optimization_barrier((far_0, far_1, early))
    ve_sib = core_swap(kept_e[1])
    mixed, kept_l = spatial(
        (1, 1, 2), info, rays_t, ray_weight, mod, w_own, w_sib, [far_0, far_1, x_up], [early]
    )
    g_own, mixed = lax.optimization_barrier((g_own, mixed))
    mixed = lax.all_to_all(mixed, "tm", split_axis=0, concat_axis=0, tiled=True)
    g_sib = core_swap(g_own)
    vl_sib = core_swap(kept_l[1])

    result = temporal(
        info, rays_t, ray_weight, mod, kept_e[0], ve_sib, kept_l[0], vl_sib, mixed, g_own, g_sib
    )
    result = lax.all_to_all(result, "tm", split_axis=0, concat_axis=0, tiled=True)
    return jnp.transpose(result, (1, 0, 2, 3)).reshape(2, TOKENS, D)


def solution(mesh):
    placed = (
        P("tm", "clip", None),
        P("clip"),
        P(None, "clip"),
        P(),
        P("clip", None, None),
        P("clip", None),
        P("clip", None),
        P("clip", None),
        P("clip", None),
    )
    return jax.shard_map(
        on_device, mesh=mesh, in_specs=placed, out_specs=P("tm", "clip", None), check_vma=False
    )
```

```python
import functools

import jax
import jax.numpy as jnp
import numpy as np
from jax import lax
from jax.experimental import pallas as pl
from jax.experimental.pallas import tpu as pltpu
from jax.sharding import PartitionSpec as P

D = 1152
HEAD = 72
HEADS = 16
PATCHES = 32
TOKENS = 256
ROWS = 36
XS = 4
ZS = 8
YS = 4
GROUP_HEADS = HEADS // XS
GROUP = GROUP_HEADS * HEAD
PAD = 384
HALF = 640
TQ = 1792
TQ_STEP = 1664
EPS = 1e-6
SOFT = HEAD ** (-0.5) * 1.4426950408889634
F32 = jnp.float32
BF16 = jnp.bfloat16
VMEM_LIMIT = 52 * 1024 * 1024
SMALL = pl.CostEstimate(flops=1000, bytes_accessed=1000, transcendentals=0)


def z_send(a, s):
    pairs = [(z * YS + y, (z + s) % ZS * YS + y) for z in range(ZS) for y in range(YS)]
    return lax.ppermute(a, "clip", pairs)


def y_send(a, s):
    pairs = [(z * YS + y, z * YS + (y + s) % YS) for z in range(ZS) for y in range(YS)]
    return lax.ppermute(a, "clip", pairs)


def x_send(a, s):
    pairs = [(x * 2 + c, (x + s) % XS * 2 + c) for x in range(XS) for c in range(2)]
    return lax.ppermute(a, "tm", pairs)


def core_swap(a):
    return lax.ppermute(a, "tm", [(t, t ^ 1) for t in range(2 * XS)])


def in_order(pieces, me):
    n = len(pieces)
    back = pieces[::-1]
    both = jnp.stack(back + back[:-1])
    picked = lax.dynamic_slice_in_dim(both, n - 1 - me, n, axis=0)
    return picked.reshape(-1, pieces[0].shape[-1])


def spread(a, groups):
    copies = jnp.broadcast_to(a[None], (len(groups[0]),) + a.shape)
    return lax.all_to_all(copies, "clip", 0, 0, axis_index_groups=groups, tiled=True).reshape(-1, a.shape[1])


def attend(queries, keys, values_t, heads, masked, held, soft, inverse):
    for h in range(heads):
        first, last = h * HEAD, h * HEAD + HEAD - 1
        lo, hi = first // 128 * 128, last // 128 * 128 + 128
        lane = lax.broadcasted_iota(jnp.int32, (1, hi - lo), 1) + lo
        own = jnp.logical_and(lane >= first, lane <= last)
        q = jnp.where(own, queries(lo, hi), jnp.zeros((), BF16))
        held[h] = lax.dot_general(keys(lo, hi), q, (((1,), (1,)), ((), ())), preferred_element_type=F32)
    for h in range(heads):
        s = masked(held[h])
        m = jnp.max(s, axis=0, keepdims=True)
        e = jnp.exp2((s - m) * SOFT)
        inverse[h] = 1.0 / jnp.sum(e, axis=0, keepdims=True)
        soft[h] = e.astype(BF16)
    outs = []
    for h in range(heads):
        first = h * HEAD
        start = first // 16 * 16
        o = jnp.dot(values_t(start, start + 80), soft[h], preferred_element_type=F32) * inverse[h]
        outs.append(o[first - start : first - start + HEAD])
    return jnp.concatenate(outs, axis=0)


def normalize(h, scale, shift):
    center = jnp.mean(h, axis=-1, keepdims=True)
    d = h - center
    spread = jnp.mean(d * d, axis=-1, keepdims=True)
    return (d * lax.rsqrt(spread + EPS) * scale + shift).astype(BF16)


def ray_sum(rays, weight):
    total = rays[:, 0:1] * weight[0:1, :]
    for k in range(1, 6):
        total += rays[:, k : k + 1] * weight[k : k + 1, :]
    return total


def spatial_kernel(parts, before, *refs):
    info, rays, ray_weight, mod, w_own, w_sib = refs[:6]
    videos = refs[6 : 6 + len(parts)]
    refs = refs[6 + len(parts) :]
    if before:
        old, out, kept = refs[:3]
        refs = refs[3:]
        out[:, 0] = old[...]
    else:
        out, kept = refs[:2]
        refs = refs[2:]
    ray, wp, sems, normed, packed, vt, of, held, soft, inverse = refs
    t, core, cameras = info[0], info[1], info[3]

    def copies(left, right):
        return [
            pltpu.make_async_copy(left, wp.at[:, 0:HALF], sems.at[0]),
            pltpu.make_async_copy(right.at[:, 128:HALF], wp.at[:, HALF:], sems.at[1]),
        ]

    @pl.when(core == 0)
    def _():
        for copy in copies(w_own, w_sib):
            copy.start()

    @pl.when(core == 1)
    def _():
        for copy in copies(w_sib, w_own):
            copy.start()

    ray[...] = ray_sum(rays[...], ray_weight[...])
    scale = 1.0 + mod[1:2, :]
    shift = mod[0:1, :]
    alive = lax.broadcasted_iota(jnp.int32, (TOKENS, TOKENS), 0) < cameras * PATCHES

    frames = [(v, f) for v, n in zip(videos, parts) for f in range(n)]

    def norm_frame(slot):
        video, frame = frames[slot]
        for r in range(TOKENS // 32):
            rows = slice(r * 32, r * 32 + 32)
            h = video[frame, rows, :].astype(F32) + ray[rows, :]
            normed[slot % 2, rows, :] = normalize(h, scale, shift)

    for who, owner in enumerate((t, t + 1 - 2 * core)):
        mine = pl.ds(pl.multiple_of(owner * PATCHES, PATCHES), PATCHES)
        for slot, (video, frame) in enumerate(frames):
            kept[who, slot] = video[frame, mine, :]
    norm_frame(0)
    for copy in copies(w_own, w_sib):
        copy.wait()
    for slot in range(4):
        turn = slot % 2
        made = jnp.dot(normed[turn], wp[...], preferred_element_type=F32)
        packed[turn] = made[:, : 2 * PAD].astype(BF16)
        vt[turn] = jnp.transpose(made[:, 2 * PAD :]).astype(BF16)
        if slot < 3:
            norm_frame(slot + 1)
        of[slot] = attend(
            lambda lo, hi: packed[turn, :, lo:hi],
            lambda lo, hi: packed[turn, :, PAD + lo : PAD + hi],
            lambda lo, hi: vt[turn, lo:hi, :],
            GROUP_HEADS,
            lambda s: jnp.where(alive, s, -1e30),
            held.at[turn],
            soft.at[turn],
            inverse.at[turn],
        )

    block = lax.broadcasted_iota(jnp.int32, (GROUP, 128), 1) // PATCHES
    for i in range(8):
        unit, place = i // 4, i % 4
        made = None
        for f in range(4):
            a = of[f, :, unit * 128 : unit * 128 + 128]
            by = (f - place) * PATCHES % 128
            if by:
                a = pltpu.roll(a, by, 1)
            made = a if made is None else jnp.where(block == f, a, made)
        if before:
            out[i, 1] = made.astype(BF16)
        else:
            out[i] = made.astype(BF16)


def spatial(parts, info, rays, ray_weight, mod, w_own, w_sib, videos, before=()):
    vmem = pl.BlockSpec(memory_space=pltpu.VMEM)
    far = pl.BlockSpec(memory_space=pl.ANY)
    frames = sum(parts)
    return pl.pallas_call(
        functools.partial(spatial_kernel, parts, len(before)),
        out_shape=[
            jax.ShapeDtypeStruct((8, 2, GROUP, 128) if before else (8, GROUP, 128), BF16),
            jax.ShapeDtypeStruct((2, 4, PATCHES, D), BF16),
        ],
        in_specs=[pl.BlockSpec(memory_space=pltpu.SMEM)] + [vmem] * 3 + [far] * 2 + [vmem] * (len(parts) + len(before)),
        out_specs=[vmem, vmem],
        scratch_shapes=[
            pltpu.VMEM((TOKENS, D), F32),
            pltpu.VMEM((D, 3 * PAD), BF16),
            pltpu.SemaphoreType.DMA((2,)),
            pltpu.VMEM((2, TOKENS, D), BF16),
            pltpu.VMEM((2, TOKENS, 2 * PAD), BF16),
            pltpu.VMEM((2, PAD, TOKENS), BF16),
            pltpu.VMEM((4, GROUP, TOKENS), F32),
            pltpu.VMEM((2, GROUP_HEADS, TOKENS, TOKENS), F32),
            pltpu.VMEM((2, GROUP_HEADS, TOKENS, TOKENS), BF16),
            pltpu.VMEM((2, GROUP_HEADS, 1, TOKENS), F32),
        ],
        compiler_params=pltpu.CompilerParams(vmem_limit_bytes=VMEM_LIMIT),
        cost_estimate=pl.CostEstimate(
            flops=frames * 2 * TOKENS * D * 3 * PAD, bytes_accessed=8_000_000, transcendentals=frames * 4 * 65536
        ),
    )(info, rays, ray_weight, mod, w_own, w_sib, *videos, *before)


def ring_rows(info):
    y = info[5]
    span = ZS * ROWS
    far = lax.rem(y + 2, YS) * span
    return [y * span, lax.rem(y + 3, YS) * span, lax.rem(y + 1, YS) * span, far, far + span // 2]


def turn_kernel(info, order, *refs):
    pieces, out, held = refs[:5], refs[5], refs[6]
    for start, piece in zip(ring_rows(info), pieces):
        held[pl.ds(pl.multiple_of(start, 16), piece.shape[0]), :] = piece[...]
    out[...] = jnp.dot(order[...], held[...], preferred_element_type=F32).astype(BF16)


def collect_kernel(info, *refs):
    pieces, out = refs[:5], refs[5]
    for start, piece in zip(ring_rows(info), pieces):
        out[pl.ds(pl.multiple_of(start, 16), piece.shape[0]), :] = piece[...]


def collect(info, pieces, order=None):
    vmem = pl.BlockSpec(memory_space=pltpu.VMEM)
    width = pieces[0].shape[1]
    turned = order is not None
    return pl.pallas_call(
        turn_kernel if turned else collect_kernel,
        out_shape=jax.ShapeDtypeStruct((D, width), BF16),
        in_specs=[pl.BlockSpec(memory_space=pltpu.SMEM)] + [vmem] * (6 if turned else 5),
        out_specs=vmem,
        scratch_shapes=[pltpu.VMEM((D, width), BF16)] if turned else [],
        compiler_params=pltpu.CompilerParams(vmem_limit_bytes=VMEM_LIMIT),
        cost_estimate=SMALL,
    )(info, *([order] if turned else []), *pieces)


def temporal_kernel(
    info, rays, ray_weight, mod, ve_own, ve_sib, vl_own, vl_sib, mixed_in, g_own, g_sib, o_own, o_sib,
    out, wq, ws, wo, mix_t, proj, mid, normed, packed, vt, bias, held, soft, inverse, sems,
):
    t, core, x, cameras = info[0], info[1], info[2], info[3]
    other = 1 - core
    s_copies, q_copies, out_copies = [], [], []
    for which, (g, o) in enumerate(((g_own, o_own), (g_sib, o_sib))):
        s_copies.append(pltpu.make_async_copy(o.at[:, 0:HALF], ws.at[which], sems.at[which * 3]))
        q_copies.append(pltpu.make_async_copy(g, wq.at[which], sems.at[which * 3 + 1]))
        out_copies.append(pltpu.make_async_copy(o.at[:, HALF:], wo.at[which], sems.at[which * 3 + 2]))
    for copy in s_copies + q_copies + out_copies:
        copy.start()

    def put_mixed(half, lanes, first, value):
        for k in range(value.shape[0] // ROWS):
            b = first + k
            to = (b % YS * ZS + b // YS) * ROWS
            mix_t[half, to : to + ROWS, lanes] = value[k * ROWS : k * ROWS + ROWS]

    for source in range(8):
        sx, sc = source // 2, source % 2
        both = jnp.concatenate([mixed_in[source, 0], mixed_in[source, 1]], axis=1).astype(F32)
        if sx:
            both = pltpu.roll(both, sx * 64, 1)
        put_mixed(sc, slice(0, TOKENS), sx * GROUP // ROWS, both)
    key = lax.broadcasted_iota(jnp.int32, (128, 128), 0)
    query = lax.broadcasted_iota(jnp.int32, (128, 128), 1)
    bias[...] = jnp.where(key % 8 == query % 8, 0.0, -1e30)

    def project(half, weights):
        mixed = mix_t[half].astype(BF16)
        rows = slice(half * TOKENS, half * TOKENS + TOKENS)
        dims = (((0,), (0,)), ((), ()))
        for which, w in zip((core, other), weights):
            to = pl.ds(pl.multiple_of(which * (HALF - 128), 128), HALF)
            proj[rows, to] = lax.dot_general(mixed, w[...], dims, preferred_element_type=F32)

    for copy in s_copies:
        copy.wait()
    for half in range(2):
        project(half, (ws.at[0], ws.at[1]))

    here = rays[pl.ds(pl.multiple_of(t * PATCHES, PATCHES), PATCHES), :]
    ray = ray_sum(here, ray_weight[...])
    gate, shift, scale = mod[2:3, :], mod[3:4, :], 1.0 + mod[4:5, :]

    def slab(j, which, video):
        pair = which * 4 + lax.rem(x + j, XS)
        middles, norms = [], []
        for f in range(2):
            h = video[2 * (j % 2) + f].astype(F32) + ray
            p = proj[pl.ds(pl.multiple_of(pair * 64 + f * PATCHES, PATCHES), PATCHES), :]
            middle = (h + gate * p).astype(BF16).astype(F32)
            middles.append(middle)
            norms.append(normalize(middle, scale, shift).astype(F32))
        for g in range(4):
            rows = pl.ds(pl.multiple_of(g * 128 + pair * 16, 16), 16)
            cut = slice(g * 8, g * 8 + 8)
            mid[rows, :] = jnp.concatenate([m[cut] for m in middles], axis=0).astype(BF16)
            normed[rows, :] = jnp.concatenate([m[cut] for m in norms], axis=0).astype(BF16)

    for j in range(4):
        slab(j, core, ve_own if j < 2 else vl_own)
        slab(j, other, ve_sib if j < 2 else vl_sib)
    for which, copy in ((core, q_copies[0]), (other, q_copies[1])):
        copy.wait()
        w = wq.at[0] if copy is q_copies[0] else wq.at[1]
        for n in range(TQ // 256):
            to = pl.ds(pl.multiple_of(which * TQ_STEP + n * 256, 128), 256)
            made = jnp.dot(normed[...], w[:, n * 256 : n * 256 + 256], preferred_element_type=F32)
            packed[:, to] = made.astype(BF16)
    for copy in out_copies:
        copy.wait()
    for half in range(2):
        for g in (2 * half, 2 * half + 1):
            rows = slice(g * 128, g * 128 + 128)
            vt[g] = jnp.transpose(packed[rows, 2 * D :])
            lanes = slice((g % 2) * 128, (g % 2) * 128 + 128)
            mixed = attend(
                lambda lo, hi: packed[rows, lo:hi],
                lambda lo, hi: packed[rows, D + lo : D + hi],
                lambda lo, hi: vt[g, lo:hi, :],
                HEADS,
                lambda s: s + bias[...],
                held.at[g],
                soft.at[g],
                inverse.at[g],
            )
            put_mixed(half, lanes, 0, mixed)
        project(half, (wo.at[0], wo.at[1]))
    alive = jnp.where(t < cameras, 1.0, 0.0)
    last_gate = mod[5:6, :]
    for target in range(8):
        pair = target % 2 * 4 + target // 2
        for g in range(4):
            rows = slice(g * 128 + pair * 16, g * 128 + pair * 16 + 16)
            done = (mid[rows, :].astype(F32) + last_gate * proj[rows, :]) * alive
            for f in range(2):
                out[target, f, g * 8 : g * 8 + 8, :] = done[f * 8 : f * 8 + 8].astype(BF16)


def temporal(info, rays, ray_weight, mod, ve_own, ve_sib, vl_own, vl_sib, mixed_in, g_own, g_sib, o_own, o_sib):
    vmem = pl.BlockSpec(memory_space=pltpu.VMEM)
    far = pl.BlockSpec(memory_space=pl.ANY)
    return pl.pallas_call(
        temporal_kernel,
        out_shape=jax.ShapeDtypeStruct((8, 2, PATCHES, D), BF16),
        in_specs=[pl.BlockSpec(memory_space=pltpu.SMEM)] + [vmem] * 8 + [far] * 4,
        out_specs=vmem,
        scratch_shapes=[
            pltpu.VMEM((2, D, TQ), BF16),
            pltpu.VMEM((2, D, HALF), BF16),
            pltpu.VMEM((2, D, HALF), BF16),
            pltpu.VMEM((2, D, TOKENS), F32),
            pltpu.VMEM((2 * TOKENS, D), F32),
            pltpu.VMEM((2 * TOKENS, D), BF16),
            pltpu.VMEM((2 * TOKENS, D), BF16),
            pltpu.VMEM((2 * TOKENS, 3 * D), BF16),
            pltpu.VMEM((4, D, 128), BF16),
            pltpu.VMEM((128, 128), F32),
            pltpu.VMEM((4, HEADS, 128, 128), F32),
            pltpu.VMEM((4, HEADS, 128, 128), BF16),
            pltpu.VMEM((4, HEADS, 1, 128), F32),
            pltpu.SemaphoreType.DMA((6,)),
        ],
        compiler_params=pltpu.CompilerParams(vmem_limit_bytes=VMEM_LIMIT),
        cost_estimate=SMALL,
    )(info, rays, ray_weight, mod, ve_own, ve_sib, vl_own, vl_sib, mixed_in, g_own, g_sib, o_own, o_sib)


def on_device(
    video,
    cameras,
    rays,
    ray_weight,
    modulation,
    spatial_qkv,
    spatial_out,
    temporal_qkv,
    temporal_out,
):
    t = lax.axis_index("tm")
    clip = lax.axis_index("clip")
    x, core = t // 2, t % 2
    z, y = clip // YS, clip % YS
    info = jnp.stack([t, core, x, cameras[0], z, y]).astype(jnp.int32)
    mod = modulation[0].astype(F32)
    rays_t = rays.T
    zgroups = [[zz * YS + yy for zz in range(ZS)] for yy in range(YS)]

    def columns(a, start, size):
        return lax.dynamic_slice_in_dim(a, start, size, axis=1)

    zgroups = [[zz * YS + yy for zz in range(ZS)] for yy in range(YS)]
    ygroups = [[zz * YS + yy for yy in range(YS)] for zz in range(ZS)]

    def spread(a, groups):
        copies = jnp.broadcast_to(a[None], (len(groups[0]),) + a.shape)
        return lax.all_to_all(copies, "clip", 0, 0, axis_index_groups=groups, tiled=True).reshape(-1, a.shape[1])

    k = np.arange(D)
    goes = k // (ZS * ROWS) * ROWS + k // ROWS % ZS * (YS * ROWS) + k % ROWS
    order = jnp.asarray(k[:, None] == goes[None, :], BF16)
    low = core * (HALF - 128)

    x_up, x_down = x_send(video, 1), x_send(video, -1)

    g = columns(temporal_qkv, core * TQ_STEP, TQ)
    g = in_order([g, y_send(g, 1), y_send(g, 2), y_send(g, 3)], y)

    heads = [jnp.pad(columns(spatial_qkv, n * D + x * GROUP, GROUP), ((0, 0), (0, PAD - GROUP))) for n in range(3)]
    w = jnp.concatenate(
        [
            columns(jnp.concatenate(heads, axis=1), low, HALF),
            columns(spatial_out, low, HALF),
            columns(temporal_out, low, HALF),
        ],
        axis=1,
    )
    w = spread(w, zgroups)

    g, w, x_up, x_down = lax.optimization_barrier((g, w, x_up, x_down))
    g_own = lax.all_gather(g, "clip", axis=0, tiled=True, axis_index_groups=zgroups)
    w, o = w[:, :HALF], w[:, HALF:]
    w_up, w_down = y_send(w, 1), y_send(w, -1)
    far_0, far_1 = x_send(x_up[0:1], 1), x_send(x_down[1:2], -1)
    half = ZS * ROWS // 2
    w_up, w_down, o = lax.optimization_barrier((w_up, w_down, o))
    w_far_up = y_send(w_up[:half], 1)
    w_far_down = y_send(w_down[half:], -1)
    o_up, o_down = y_send(o, 1), y_send(o, -1)
    w_far_up, w_far_down, far_0, far_1 = lax.optimization_barrier((w_far_up, w_far_down, far_0, far_1))
    w_own = collect(info, [w, w_up, w_down, w_far_up, w_far_down], order)
    w_sib = core_swap(w_own)

    early, kept_e = spatial((2, 2), info, rays_t, ray_weight, mod, w_own, w_sib, [video, x_down])
    o_up, o_down, early = lax.optimization_barrier((o_up, o_down, early))
    o_far_up = y_send(o_up[:half], 1)
    o_far_down = y_send(o_down[half:], -1)
    ve_sib = core_swap(kept_e[1])
    mixed, kept_l = spatial(
        (1, 1, 2), info, rays_t, ray_weight, mod, w_own, w_sib, [far_0, far_1, x_up], [early]
    )
    g_own, mixed = lax.optimization_barrier((g_own, mixed))
    mixed = lax.all_to_all(mixed, "tm", split_axis=0, concat_axis=0, tiled=True)
    g_sib = core_swap(g_own)
    o_own = collect(info, [o, o_up, o_down, o_far_up, o_far_down])
    o_sib = core_swap(o_own)
    vl_sib = core_swap(kept_l[1])

    result = temporal(
        info, rays_t, ray_weight, mod, kept_e[0], ve_sib, kept_l[0], vl_sib, mixed, g_own, g_sib, o_own, o_sib
    )
    result = lax.all_to_all(result, "tm", split_axis=0, concat_axis=0, tiled=True)
    return jnp.transpose(result, (1, 0, 2, 3)).reshape(2, TOKENS, D)


def solution(mesh):
    placed = (
        P("tm", "clip", None),
        P("clip"),
        P(None, "clip"),
        P(),
        P("clip", None, None),
        P("clip", None),
        P("clip", None),
        P("clip", None),
        P("clip", None),
    )
    return jax.shard_map(
        on_device, mesh=mesh, in_specs=placed, out_specs=P("tm", "clip", None), check_vma=False
    )
```

```python
import functools

import jax
import jax.numpy as jnp
import numpy as np
from jax import lax
from jax.experimental import pallas as pl
from jax.experimental.pallas import tpu as pltpu
from jax.sharding import PartitionSpec as P

D = 1152
HEAD = 72
HEADS = 16
PATCHES = 32
TOKENS = 256
ROWS = 36
XS = 4
ZS = 8
YS = 4
GROUP_HEADS = HEADS // XS
GROUP = GROUP_HEADS * HEAD
PAD = 384
HALF = 512
MAIN = 2944
MAIN_STEP = 2816
EPS = 1e-6
SOFT = HEAD ** (-0.5) * 1.4426950408889634
F32 = jnp.float32
BF16 = jnp.bfloat16
VMEM_LIMIT = 52 * 1024 * 1024
SMALL = pl.CostEstimate(flops=1000, bytes_accessed=1000, transcendentals=0)


def z_send(a, s):
    pairs = [(z * YS + y, (z + s) % ZS * YS + y) for z in range(ZS) for y in range(YS)]
    return lax.ppermute(a, "clip", pairs)


def y_send(a, s):
    pairs = [(z * YS + y, z * YS + (y + s) % YS) for z in range(ZS) for y in range(YS)]
    return lax.ppermute(a, "clip", pairs)


def x_send(a, s):
    pairs = [(x * 2 + c, (x + s) % XS * 2 + c) for x in range(XS) for c in range(2)]
    return lax.ppermute(a, "tm", pairs)


def core_swap(a):
    return lax.ppermute(a, "tm", [(t, t ^ 1) for t in range(2 * XS)])


def in_order(pieces, me):
    n = len(pieces)
    back = pieces[::-1]
    both = jnp.stack(back + back[:-1])
    picked = lax.dynamic_slice_in_dim(both, n - 1 - me, n, axis=0)
    return picked.reshape(-1, pieces[0].shape[-1])


def spread(a, groups):
    copies = jnp.broadcast_to(a[None], (len(groups[0]),) + a.shape)
    return lax.all_to_all(copies, "clip", 0, 0, axis_index_groups=groups, tiled=True).reshape(-1, a.shape[1])


def attend(queries, keys, values_t, heads, masked, held, soft, inverse):
    for h in range(heads):
        first, last = h * HEAD, h * HEAD + HEAD - 1
        lo, hi = first // 128 * 128, last // 128 * 128 + 128
        lane = lax.broadcasted_iota(jnp.int32, (1, hi - lo), 1) + lo
        own = jnp.logical_and(lane >= first, lane <= last)
        q = jnp.where(own, queries(lo, hi), jnp.zeros((), BF16))
        held[h] = lax.dot_general(keys(lo, hi), q, (((1,), (1,)), ((), ())), preferred_element_type=F32)
    for h in range(heads):
        s = masked(held[h])
        m = jnp.max(s, axis=0, keepdims=True)
        e = jnp.exp2((s - m) * SOFT)
        inverse[h] = 1.0 / jnp.sum(e, axis=0, keepdims=True)
        soft[h] = e.astype(BF16)
    outs = []
    for h in range(heads):
        first = h * HEAD
        start = first // 16 * 16
        o = jnp.dot(values_t(start, start + 80), soft[h], preferred_element_type=F32) * inverse[h]
        outs.append(o[first - start : first - start + HEAD])
    return jnp.concatenate(outs, axis=0)


def normalize(h, scale, shift):
    center = jnp.mean(h, axis=-1, keepdims=True)
    d = h - center
    spread = jnp.mean(d * d, axis=-1, keepdims=True)
    return (d * lax.rsqrt(spread + EPS) * scale + shift).astype(BF16)


def ray_sum(rays, weight):
    total = rays[:, 0:1] * weight[0:1, :]
    for k in range(1, 6):
        total += rays[:, k : k + 1] * weight[k : k + 1, :]
    return total


def spatial_kernel(parts, before, *refs):
    info, rays, ray_weight, mod, w_own, w_sib = refs[:6]
    videos = refs[6 : 6 + len(parts)]
    refs = refs[6 + len(parts) :]
    if before:
        old, out, kept = refs[:3]
        refs = refs[3:]
        out[:, 0] = old[...]
    else:
        out, kept = refs[:2]
        refs = refs[2:]
    ray, wp, sems, normed, packed, vt, of, held, soft, inverse = refs
    t, core, cameras = info[0], info[1], info[3]

    def copies(left, right):
        return [
            pltpu.make_async_copy(left, wp.at[:, 0:HALF], sems.at[0]),
            pltpu.make_async_copy(right, wp.at[:, HALF:], sems.at[1]),
        ]

    @pl.when(core == 0)
    def _():
        for copy in copies(w_own, w_sib):
            copy.start()

    @pl.when(core == 1)
    def _():
        for copy in copies(w_sib, w_own):
            copy.start()

    ray[...] = ray_sum(rays[...], ray_weight[...])
    scale = 1.0 + mod[1:2, :]
    shift = mod[0:1, :]
    alive = lax.broadcasted_iota(jnp.int32, (TOKENS, TOKENS), 0) < cameras * PATCHES

    frames = [(v, f) for v, n in zip(videos, parts) for f in range(n)]

    def norm_frame(slot):
        video, frame = frames[slot]
        for r in range(TOKENS // 32):
            rows = slice(r * 32, r * 32 + 32)
            h = video[frame, rows, :].astype(F32) + ray[rows, :]
            normed[slot % 2, rows, :] = normalize(h, scale, shift)

    for who, owner in enumerate((t, t + 1 - 2 * core)):
        mine = pl.ds(pl.multiple_of(owner * PATCHES, PATCHES), PATCHES)
        for slot, (video, frame) in enumerate(frames):
            kept[who, slot] = video[frame, mine, :]
    norm_frame(0)
    for copy in copies(w_own, w_sib):
        copy.wait()
    for slot in range(4):
        turn = slot % 2
        made = jnp.dot(normed[turn], wp[...], preferred_element_type=F32)
        packed[turn] = made[:, : 2 * PAD].astype(BF16)
        vt[turn, 0:256] = jnp.transpose(made[:, 2 * PAD :]).astype(BF16)
        vt[turn, 256:GROUP] = jnp.transpose(made[:, 256:PAD])[32:64].astype(BF16)
        if slot < 3:
            norm_frame(slot + 1)
        of[slot] = attend(
            lambda lo, hi: packed[turn, :, lo:hi],
            lambda lo, hi: packed[turn, :, PAD + lo : PAD + hi],
            lambda lo, hi: vt[turn, lo:hi, :],
            GROUP_HEADS,
            lambda s: jnp.where(alive, s, -1e30),
            held.at[turn],
            soft.at[turn],
            inverse.at[turn],
        )

    block = lax.broadcasted_iota(jnp.int32, (GROUP, 128), 1) // PATCHES
    for i in range(8):
        unit, place = i // 4, i % 4
        made = None
        for f in range(4):
            a = of[f, :, unit * 128 : unit * 128 + 128]
            by = (f - place) * PATCHES % 128
            if by:
                a = pltpu.roll(a, by, 1)
            made = a if made is None else jnp.where(block == f, a, made)
        if before:
            out[i, 1] = made.astype(BF16)
        else:
            out[i] = made.astype(BF16)


def spatial(parts, info, rays, ray_weight, mod, w_own, w_sib, videos, before=()):
    vmem = pl.BlockSpec(memory_space=pltpu.VMEM)
    far = pl.BlockSpec(memory_space=pl.ANY)
    frames = sum(parts)
    return pl.pallas_call(
        functools.partial(spatial_kernel, parts, len(before)),
        out_shape=[
            jax.ShapeDtypeStruct((8, 2, GROUP, 128) if before else (8, GROUP, 128), BF16),
            jax.ShapeDtypeStruct((2, 4, PATCHES, D), BF16),
        ],
        in_specs=[pl.BlockSpec(memory_space=pltpu.SMEM)] + [vmem] * 3 + [far] * 2 + [vmem] * (len(parts) + len(before)),
        out_specs=[vmem, vmem],
        scratch_shapes=[
            pltpu.VMEM((TOKENS, D), F32),
            pltpu.VMEM((D, 2 * HALF), BF16),
            pltpu.SemaphoreType.DMA((2,)),
            pltpu.VMEM((2, TOKENS, D), BF16),
            pltpu.VMEM((2, TOKENS, 2 * PAD), BF16),
            pltpu.VMEM((2, GROUP, TOKENS), BF16),
            pltpu.VMEM((4, GROUP, TOKENS), F32),
            pltpu.VMEM((2, GROUP_HEADS, TOKENS, TOKENS), F32),
            pltpu.VMEM((2, GROUP_HEADS, TOKENS, TOKENS), BF16),
            pltpu.VMEM((2, GROUP_HEADS, 1, TOKENS), F32),
        ],
        compiler_params=pltpu.CompilerParams(vmem_limit_bytes=VMEM_LIMIT),
        cost_estimate=pl.CostEstimate(
            flops=frames * 2 * TOKENS * D * 3 * PAD, bytes_accessed=8_000_000, transcendentals=frames * 4 * 65536
        ),
    )(info, rays, ray_weight, mod, w_own, w_sib, *videos, *before)


def ring_rows(info):
    y = info[5]
    span = ZS * ROWS
    far = lax.rem(y + 2, YS) * span
    return [y * span, lax.rem(y + 3, YS) * span, lax.rem(y + 1, YS) * span, far, far + span // 2]


def turn_kernel(info, order, *refs):
    pieces, out, held = refs[:5], refs[6], refs[7]
    for start, piece in zip(ring_rows(info), pieces):
        held[pl.ds(pl.multiple_of(start, 16), piece.shape[0]), :] = piece[...]
    out[...] = jnp.dot(order[...], held[...], preferred_element_type=F32).astype(BF16)


def collect(info, pieces, order, token):
    vmem = pl.BlockSpec(memory_space=pltpu.VMEM)
    width = pieces[0].shape[1]
    return pl.pallas_call(
        turn_kernel,
        out_shape=jax.ShapeDtypeStruct((D, width), BF16),
        in_specs=[pl.BlockSpec(memory_space=pltpu.SMEM)] + [vmem] * 6 + [pl.BlockSpec(memory_space=pl.ANY)],
        out_specs=vmem,
        scratch_shapes=[pltpu.VMEM((D, width), BF16)],
        compiler_params=pltpu.CompilerParams(vmem_limit_bytes=VMEM_LIMIT),
        cost_estimate=SMALL,
    )(info, order, *pieces, token)


def temporal_kernel(
    info, rays, ray_weight, mod, ve_own, ve_sib, vl_own, vl_sib, mixed_in, g_own, g_sib,
    out, wa, wb, mix_t, proj, mid, normed, packed, vt, bias, held, soft, inverse, sems,
):
    t, core, x, cameras = info[0], info[1], info[2], info[3]
    other = 1 - core

    def copies(left, right):
        cut = 640
        return [
            pltpu.make_async_copy(right.at[:, cut : cut + D], wb.at[:, cut : cut + D], sems.at[0]),
            pltpu.make_async_copy(left, wa, sems.at[1]),
            pltpu.make_async_copy(right.at[:, 0:cut], wb.at[:, 0:cut], sems.at[2]),
            pltpu.make_async_copy(right.at[:, cut + D :], wb.at[:, cut + D :], sems.at[3]),
        ]

    @pl.when(core == 0)
    def _():
        for copy in copies(g_own, g_sib):
            copy.start()

    @pl.when(core == 1)
    def _():
        for copy in copies(g_sib, g_own):
            copy.start()

    arrived = copies(g_own, g_sib)

    for source in range(8):
        sx, sc = source // 2, source % 2
        both = jnp.concatenate([mixed_in[source, 0], mixed_in[source, 1]], axis=1).astype(F32)
        if sx:
            both = pltpu.roll(both, sx * 64, 1)
        mix_t[sc, sx * GROUP : sx * GROUP + GROUP, :] = both.astype(BF16)
    key = lax.broadcasted_iota(jnp.int32, (128, 128), 0)
    query = lax.broadcasted_iota(jnp.int32, (128, 128), 1)
    bias[...] = jnp.where(key % 8 == query % 8, 0.0, -1e30)

    def project(half, first):
        rows = slice(half * TOKENS, half * TOKENS + TOKENS)
        dims = (((0,), (0,)), ((), ()))
        w = wb[:, first : first + D]
        proj[rows, :] = lax.dot_general(mix_t[half], w, dims, preferred_element_type=F32)

    arrived[0].wait()
    for half in range(2):
        project(half, 640)

    here = rays[pl.ds(pl.multiple_of(t * PATCHES, PATCHES), PATCHES), :]
    ray = ray_sum(here, ray_weight[...])
    gate, shift, scale = mod[2:3, :], mod[3:4, :], 1.0 + mod[4:5, :]

    def slab(j, which, video):
        pair = which * 4 + lax.rem(x + j, XS)
        middles, norms = [], []
        for f in range(2):
            h = video[2 * (j % 2) + f].astype(F32) + ray
            p = proj[pl.ds(pl.multiple_of(pair * 64 + f * PATCHES, PATCHES), PATCHES), :]
            middle = (h + gate * p).astype(BF16).astype(F32)
            middles.append(middle)
            norms.append(normalize(middle, scale, shift).astype(F32))
        for g in range(4):
            rows = pl.ds(pl.multiple_of(g * 128 + pair * 16, 16), 16)
            cut = slice(g * 8, g * 8 + 8)
            mid[rows, :] = jnp.concatenate([m[cut] for m in middles], axis=0).astype(BF16)
            normed[rows, :] = jnp.concatenate([m[cut] for m in norms], axis=0).astype(BF16)

    for j in range(4):
        slab(j, core, ve_own if j < 2 else vl_own)
        slab(j, other, ve_sib if j < 2 else vl_sib)
    arrived[1].wait()
    tiles = [(wa, n * 256, min(256, MAIN - n * 256), n * 256) for n in range(-(-MAIN // 256))]
    tiles += [(wb, 128 + n * 256, 256, MAIN + n * 256) for n in range((3 * D - MAIN) // 256)]
    for w, at, width, to in tiles:
        if to == MAIN:
            arrived[2].wait()
        made = jnp.dot(normed[...], w[:, at : at + width], preferred_element_type=F32)
        packed[:, to : to + width] = made.astype(BF16)
    arrived[3].wait()
    for half in range(2):
        for g in (2 * half, 2 * half + 1):
            rows = slice(g * 128, g * 128 + 128)
            vt[g] = jnp.transpose(packed[rows, 2 * D :])
            lanes = slice((g % 2) * 128, (g % 2) * 128 + 128)
            mix_t[half, :, lanes] = attend(
                lambda lo, hi: packed[rows, lo:hi],
                lambda lo, hi: packed[rows, D + lo : D + hi],
                lambda lo, hi: vt[g, lo:hi, :],
                HEADS,
                lambda s: s + bias[...],
                held.at[g],
                soft.at[g],
                inverse.at[g],
            ).astype(BF16)
        project(half, 640 + D)
    alive = jnp.where(t < cameras, 1.0, 0.0)
    last_gate = mod[5:6, :]
    for target in range(8):
        pair = target % 2 * 4 + target // 2
        for g in range(4):
            rows = slice(g * 128 + pair * 16, g * 128 + pair * 16 + 16)
            done = (mid[rows, :].astype(F32) + last_gate * proj[rows, :]) * alive
            for f in range(2):
                out[target, f, g * 8 : g * 8 + 8, :] = done[f * 8 : f * 8 + 8].astype(BF16)


def temporal(info, rays, ray_weight, mod, ve_own, ve_sib, vl_own, vl_sib, mixed_in, g_own, g_sib):
    vmem = pl.BlockSpec(memory_space=pltpu.VMEM)
    far = pl.BlockSpec(memory_space=pl.ANY)
    return pl.pallas_call(
        temporal_kernel,
        out_shape=jax.ShapeDtypeStruct((8, 2, PATCHES, D), BF16),
        in_specs=[pl.BlockSpec(memory_space=pltpu.SMEM)] + [vmem] * 8 + [far] * 2,
        out_specs=vmem,
        scratch_shapes=[
            pltpu.VMEM((D, MAIN), BF16),
            pltpu.VMEM((D, MAIN), BF16),
            pltpu.VMEM((2, D, TOKENS), BF16),
            pltpu.VMEM((2 * TOKENS, D), F32),
            pltpu.VMEM((2 * TOKENS, D), BF16),
            pltpu.VMEM((2 * TOKENS, D), BF16),
            pltpu.VMEM((2 * TOKENS, 3 * D), BF16),
            pltpu.VMEM((4, D, 128), BF16),
            pltpu.VMEM((128, 128), F32),
            pltpu.VMEM((4, HEADS, 128, 128), F32),
            pltpu.VMEM((4, HEADS, 128, 128), BF16),
            pltpu.VMEM((4, HEADS, 1, 128), F32),
            pltpu.SemaphoreType.DMA((4,)),
        ],
        compiler_params=pltpu.CompilerParams(vmem_limit_bytes=VMEM_LIMIT),
        cost_estimate=SMALL,
    )(info, rays, ray_weight, mod, ve_own, ve_sib, vl_own, vl_sib, mixed_in, g_own, g_sib)


def on_device(
    video,
    cameras,
    rays,
    ray_weight,
    modulation,
    spatial_qkv,
    spatial_out,
    temporal_qkv,
    temporal_out,
):
    t = lax.axis_index("tm")
    clip = lax.axis_index("clip")
    x, core = t // 2, t % 2
    z, y = clip // YS, clip % YS
    info = jnp.stack([t, core, x, cameras[0], z, y]).astype(jnp.int32)
    mod = modulation[0].astype(F32)
    rays_t = rays.T
    zgroups = [[zz * YS + yy for zz in range(ZS)] for yy in range(YS)]

    def columns(a, start, size):
        return lax.dynamic_slice_in_dim(a, start, size, axis=1)

    zgroups = [[zz * YS + yy for zz in range(ZS)] for yy in range(YS)]
    ygroups = [[zz * YS + yy for yy in range(YS)] for zz in range(ZS)]

    def spread(a, groups):
        copies = jnp.broadcast_to(a[None], (len(groups[0]),) + a.shape)
        return lax.all_to_all(copies, "clip", 0, 0, axis_index_groups=groups, tiled=True).reshape(-1, a.shape[1])

    k = np.arange(D)
    goes = k // (ZS * ROWS) * ROWS + k // ROWS % ZS * (YS * ROWS) + k % ROWS
    order = jnp.asarray(k[:, None] == goes[None, :], BF16)

    x_up, x_down = x_send(video, 1), x_send(video, -1)

    g = columns(jnp.concatenate([temporal_qkv, spatial_out, temporal_out], axis=1), core * MAIN_STEP, MAIN)
    g = in_order([g, y_send(g, 1), y_send(g, 2), y_send(g, 3)], y)
    g_own = lax.all_gather(g, "clip", axis=0, tiled=True, axis_index_groups=zgroups)
    token = g[0:16, 0:128]

    q, k, v = (columns(spatial_qkv, n * D + x * GROUP, GROUP) for n in range(3))
    gap = jnp.zeros((ROWS, 96), BF16)
    w = jnp.concatenate([q, v[:, 256:], gap[:, :64], k, gap, v[:, :256]], axis=1)
    w = spread(columns(w, core * HALF, HALF), zgroups)

    token, w, x_up, x_down = lax.optimization_barrier((token, w, x_up, x_down))
    w_up, w_down = y_send(w, 1), y_send(w, -1)
    far_0, far_1 = x_send(x_up[0:1], 1), x_send(x_down[1:2], -1)
    half = ZS * ROWS // 2
    w_far_up = y_send(w_up[:half], 1)
    w_far_down = y_send(w_down[half:], -1)
    w_far_up, w_far_down, far_0, far_1 = lax.optimization_barrier((w_far_up, w_far_down, far_0, far_1))
    w_own = collect(info, [w, w_up, w_down, w_far_up, w_far_down], order, token)
    w_sib = core_swap(w_own)

    early, kept_e = spatial((2, 2), info, rays_t, ray_weight, mod, w_own, w_sib, [video, x_down])
    ve_sib = core_swap(kept_e[1])
    mixed, kept_l = spatial(
        (1, 1, 2), info, rays_t, ray_weight, mod, w_own, w_sib, [far_0, far_1, x_up], [early]
    )
    mixed = lax.all_to_all(mixed, "tm", split_axis=0, concat_axis=0, tiled=True)
    vl_sib = core_swap(kept_l[1])
    g_own, vl_sib = lax.optimization_barrier((g_own, vl_sib))
    g_sib = core_swap(g_own)

    result = temporal(
        info, rays_t, ray_weight, mod, kept_e[0], ve_sib, kept_l[0], vl_sib, mixed, g_own, g_sib
    )
    result = lax.all_to_all(result, "tm", split_axis=0, concat_axis=0, tiled=True)
    return jnp.transpose(result, (1, 0, 2, 3)).reshape(2, TOKENS, D)


def solution(mesh):
    placed = (
        P("tm", "clip", None),
        P("clip"),
        P(None, "clip"),
        P(),
        P("clip", None, None),
        P("clip", None),
        P("clip", None),
        P("clip", None),
        P("clip", None),
    )
    return jax.shard_map(
        on_device, mesh=mesh, in_specs=placed, out_specs=P("tm", "clip", None), check_vma=False
    )
```

```python
import functools

import jax
import jax.numpy as jnp
import numpy as np
from jax import lax
from jax.experimental import pallas as pl
from jax.experimental.pallas import tpu as pltpu
from jax.sharding import PartitionSpec as P

D = 1152
HEAD = 72
HEADS = 16
PATCHES = 32
TOKENS = 256
ROWS = 36
XS = 4
ZS = 8
YS = 4
GROUP_HEADS = HEADS // XS
GROUP = GROUP_HEADS * HEAD
PAD = 384
HALF = 512
MAIN = 2944
MAIN_STEP = 2816
EPS = 1e-6
SOFT = HEAD ** (-0.5) * 1.4426950408889634
F32 = jnp.float32
BF16 = jnp.bfloat16
VMEM_LIMIT = 52 * 1024 * 1024
SMALL = pl.CostEstimate(flops=1000, bytes_accessed=1000, transcendentals=0)


def z_send(a, s):
    pairs = [(z * YS + y, (z + s) % ZS * YS + y) for z in range(ZS) for y in range(YS)]
    return lax.ppermute(a, "clip", pairs)


def y_send(a, s):
    pairs = [(z * YS + y, z * YS + (y + s) % YS) for z in range(ZS) for y in range(YS)]
    return lax.ppermute(a, "clip", pairs)


def x_send(a, s):
    pairs = [(x * 2 + c, (x + s) % XS * 2 + c) for x in range(XS) for c in range(2)]
    return lax.ppermute(a, "tm", pairs)


def core_swap(a):
    return lax.ppermute(a, "tm", [(t, t ^ 1) for t in range(2 * XS)])


def tm_send(a, s):
    return lax.ppermute(a, "tm", [(t, (t + s) % (2 * XS)) for t in range(2 * XS)])


def in_order(pieces, me):
    n = len(pieces)
    back = pieces[::-1]
    both = jnp.stack(back + back[:-1])
    picked = lax.dynamic_slice_in_dim(both, n - 1 - me, n, axis=0)
    return picked.reshape(-1, pieces[0].shape[-1])


def attend(queries, keys, values_t, heads, masked, held, soft, inverse):
    for h in range(heads):
        first, last = h * HEAD, h * HEAD + HEAD - 1
        lo, hi = first // 128 * 128, last // 128 * 128 + 128
        lane = lax.broadcasted_iota(jnp.int32, (1, hi - lo), 1) + lo
        own = jnp.logical_and(lane >= first, lane <= last)
        q = jnp.where(own, queries(lo, hi), jnp.zeros((), BF16))
        held[h] = lax.dot_general(keys(lo, hi), q, (((1,), (1,)), ((), ())), preferred_element_type=F32)
    for h in range(heads):
        s = masked(held[h])
        m = jnp.max(s, axis=0, keepdims=True)
        e = jnp.exp2((s - m) * SOFT)
        inverse[h] = 1.0 / jnp.sum(e, axis=0, keepdims=True)
        soft[h] = e.astype(BF16)
    outs = []
    for h in range(heads):
        first = h * HEAD
        start = first // 16 * 16
        o = jnp.dot(values_t(start, start + 80), soft[h], preferred_element_type=F32) * inverse[h]
        outs.append(o[first - start : first - start + HEAD])
    return jnp.concatenate(outs, axis=0)


def normalize(h, scale, shift):
    center = jnp.mean(h, axis=-1, keepdims=True)
    d = h - center
    spread = jnp.mean(d * d, axis=-1, keepdims=True)
    return (d * lax.rsqrt(spread + EPS) * scale + shift).astype(BF16)


def ray_sum(rays, weight):
    total = rays[:, 0:1] * weight[0:1, :]
    for k in range(1, 6):
        total += rays[:, k : k + 1] * weight[k : k + 1, :]
    return total


def spatial_kernel(parts, before, *refs):
    info, rays, ray_weight, mod, w_own, w_sib = refs[:6]
    videos = refs[6 : 6 + len(parts)]
    refs = refs[6 + len(parts) :]
    if before:
        old, outs, kept = refs[0], refs[1:9], refs[9]
        out, refs = refs[-1], refs[10:-1]
        out[:, 0] = old[...]
    else:
        out, kept = refs[:2]
        refs = refs[2:]
    ray, wp, sems, normed, packed, vt, of, held, soft, inverse = refs
    t, core, cameras = info[0], info[1], info[3]

    def copies(left, right):
        return [
            pltpu.make_async_copy(left, wp.at[:, 0:HALF], sems.at[0]),
            pltpu.make_async_copy(right, wp.at[:, HALF:], sems.at[1]),
        ]

    @pl.when(core == 0)
    def _():
        for copy in copies(w_own, w_sib):
            copy.start()

    @pl.when(core == 1)
    def _():
        for copy in copies(w_sib, w_own):
            copy.start()

    ray[...] = ray_sum(rays[...], ray_weight[...])
    scale = 1.0 + mod[1:2, :]
    shift = mod[0:1, :]
    alive = lax.broadcasted_iota(jnp.int32, (TOKENS, TOKENS), 0) < cameras * PATCHES

    frames = [(v, f) for v, n in zip(videos, parts) for f in range(n)]

    def norm_frame(slot):
        video, frame = frames[slot]
        for r in range(TOKENS // 32):
            rows = slice(r * 32, r * 32 + 32)
            h = video[frame, rows, :].astype(F32) + ray[rows, :]
            normed[slot % 2, rows, :] = normalize(h, scale, shift)

    for who, owner in enumerate((t, t + 1 - 2 * core)):
        mine = pl.ds(pl.multiple_of(owner * PATCHES, PATCHES), PATCHES)
        for slot, (video, frame) in enumerate(frames):
            kept[who, slot] = video[frame, mine, :]
    norm_frame(0)
    for copy in copies(w_own, w_sib):
        copy.wait()
    for slot in range(4):
        turn = slot % 2
        made = jnp.dot(normed[turn], wp[...], preferred_element_type=F32)
        packed[turn] = made[:, : 2 * PAD].astype(BF16)
        vt[turn, 0:256] = jnp.transpose(made[:, 2 * PAD :]).astype(BF16)
        vt[turn, 256:GROUP] = jnp.transpose(made[:, 256:PAD])[32:64].astype(BF16)
        if slot < 3:
            norm_frame(slot + 1)
        of[slot] = attend(
            lambda lo, hi: packed[turn, :, lo:hi],
            lambda lo, hi: packed[turn, :, PAD + lo : PAD + hi],
            lambda lo, hi: vt[turn, lo:hi, :],
            GROUP_HEADS,
            lambda s: jnp.where(alive, s, -1e30),
            held.at[turn],
            soft.at[turn],
            inverse.at[turn],
        )

    block = lax.broadcasted_iota(jnp.int32, (GROUP, 128), 1) // PATCHES
    for i in range(8):
        unit, place = i // 4, i % 4
        made = None
        for f in range(4):
            a = of[f, :, unit * 128 : unit * 128 + 128]
            by = (f - place) * PATCHES % 128
            if by:
                a = pltpu.roll(a, by, 1)
            made = a if made is None else jnp.where(block == f, a, made)
        if before:
            out[i, 1] = made.astype(BF16)
        else:
            out[i] = made.astype(BF16)
    if before:
        for i in range(8):
            outs[i][...] = out[lax.rem(t + i, 8)]


def spatial(parts, info, rays, ray_weight, mod, w_own, w_sib, videos, before=()):
    vmem = pl.BlockSpec(memory_space=pltpu.VMEM)
    far = pl.BlockSpec(memory_space=pl.ANY)
    frames = sum(parts)
    return pl.pallas_call(
        functools.partial(spatial_kernel, parts, len(before)),
        out_shape=(
            [jax.ShapeDtypeStruct((2, GROUP, 128), BF16)] * 8
            if before
            else [jax.ShapeDtypeStruct((8, GROUP, 128), BF16)]
        )
        + [jax.ShapeDtypeStruct((2, 4, PATCHES, D), BF16)],
        in_specs=[pl.BlockSpec(memory_space=pltpu.SMEM)] + [vmem] * 3 + [far] * 2 + [vmem] * (len(parts) + len(before)),
        out_specs=[vmem] * (9 if before else 2),
        scratch_shapes=[
            pltpu.VMEM((TOKENS, D), F32),
            pltpu.VMEM((D, 2 * HALF), BF16),
            pltpu.SemaphoreType.DMA((2,)),
            pltpu.VMEM((2, TOKENS, D), BF16),
            pltpu.VMEM((2, TOKENS, 2 * PAD), BF16),
            pltpu.VMEM((2, GROUP, TOKENS), BF16),
            pltpu.VMEM((4, GROUP, TOKENS), F32),
            pltpu.VMEM((2, GROUP_HEADS, TOKENS, TOKENS), F32),
            pltpu.VMEM((2, GROUP_HEADS, TOKENS, TOKENS), BF16),
            pltpu.VMEM((2, GROUP_HEADS, 1, TOKENS), F32),
        ]
        + ([pltpu.VMEM((8, 2, GROUP, 128), BF16)] if before else []),
        compiler_params=pltpu.CompilerParams(vmem_limit_bytes=VMEM_LIMIT),
        cost_estimate=pl.CostEstimate(
            flops=frames * 2 * TOKENS * D * 3 * PAD, bytes_accessed=8_000_000, transcendentals=frames * 4 * 65536
        ),
    )(info, rays, ray_weight, mod, w_own, w_sib, *videos, *before)


def ring_rows(info):
    y = info[5]
    span = ZS * ROWS
    far = lax.rem(y + 2, YS) * span
    return [y * span, lax.rem(y + 3, YS) * span, lax.rem(y + 1, YS) * span, far, far + span // 2]


def turn_kernel(info, order, *refs):
    pieces, out, held = refs[:5], refs[6], refs[7]
    for start, piece in zip(ring_rows(info), pieces):
        held[pl.ds(pl.multiple_of(start, 16), piece.shape[0]), :] = piece[...]
    out[...] = jnp.dot(order[...], held[...], preferred_element_type=F32).astype(BF16)


def collect(info, pieces, order, token):
    vmem = pl.BlockSpec(memory_space=pltpu.VMEM)
    width = pieces[0].shape[1]
    return pl.pallas_call(
        turn_kernel,
        out_shape=jax.ShapeDtypeStruct((D, width), BF16),
        in_specs=[pl.BlockSpec(memory_space=pltpu.SMEM)] + [vmem] * 6 + [pl.BlockSpec(memory_space=pl.ANY)],
        out_specs=vmem,
        scratch_shapes=[pltpu.VMEM((D, width), BF16)],
        compiler_params=pltpu.CompilerParams(vmem_limit_bytes=VMEM_LIMIT),
        cost_estimate=SMALL,
    )(info, order, *pieces, token)


def temporal_kernel(*refs):
    info, rays, ray_weight, mod, ve_own, ve_sib, vl_own, vl_sib = refs[:8]
    mixed_in, g_own, g_sib, outs = refs[8:16], refs[16], refs[17], refs[18:26]
    wa, wb, mix_t, proj, mid, normed, packed, vt, bias, held, soft, inverse, sems = refs[26:]
    t, core, x, cameras = info[0], info[1], info[2], info[3]
    other = 1 - core

    def copies(left, right):
        cut = 640
        return [
            pltpu.make_async_copy(right.at[:, cut : cut + D], wb.at[:, cut : cut + D], sems.at[0]),
            pltpu.make_async_copy(left, wa, sems.at[1]),
            pltpu.make_async_copy(right.at[:, 0:cut], wb.at[:, 0:cut], sems.at[2]),
            pltpu.make_async_copy(right.at[:, cut + D :], wb.at[:, cut + D :], sems.at[3]),
        ]

    @pl.when(core == 0)
    def _():
        for copy in copies(g_own, g_sib):
            copy.start()

    @pl.when(core == 1)
    def _():
        for copy in copies(g_sib, g_own):
            copy.start()

    arrived = copies(g_own, g_sib)

    for i in range(8):
        source = lax.rem(t + 8 - i, 8)
        sx, sc = source // 2, lax.rem(source, 2)
        both = jnp.concatenate([mixed_in[i][0], mixed_in[i][1]], axis=1).astype(F32)
        both = pltpu.roll(both, sx * 64, 1)
        mix_t[sc, pl.ds(pl.multiple_of(sx * GROUP, 16), GROUP), :] = both.astype(BF16)
    key = lax.broadcasted_iota(jnp.int32, (128, 128), 0)
    query = lax.broadcasted_iota(jnp.int32, (128, 128), 1)
    bias[...] = jnp.where(key % 8 == query % 8, 0.0, -1e30)

    def project(half, first):
        rows = slice(half * TOKENS, half * TOKENS + TOKENS)
        dims = (((0,), (0,)), ((), ()))
        w = wb[:, first : first + D]
        proj[rows, :] = lax.dot_general(mix_t[half], w, dims, preferred_element_type=F32)

    arrived[0].wait()
    for half in range(2):
        project(half, 640)

    here = rays[pl.ds(pl.multiple_of(t * PATCHES, PATCHES), PATCHES), :]
    ray = ray_sum(here, ray_weight[...])
    gate, shift, scale = mod[2:3, :], mod[3:4, :], 1.0 + mod[4:5, :]

    def slab(j, which, video):
        pair = which * 4 + lax.rem(x + j, XS)
        middles, norms = [], []
        for f in range(2):
            h = video[2 * (j % 2) + f].astype(F32) + ray
            p = proj[pl.ds(pl.multiple_of(pair * 64 + f * PATCHES, PATCHES), PATCHES), :]
            middle = (h + gate * p).astype(BF16).astype(F32)
            middles.append(middle)
            norms.append(normalize(middle, scale, shift).astype(F32))
        for g in range(4):
            rows = pl.ds(pl.multiple_of(g * 128 + pair * 16, 16), 16)
            cut = slice(g * 8, g * 8 + 8)
            mid[rows, :] = jnp.concatenate([m[cut] for m in middles], axis=0).astype(BF16)
            normed[rows, :] = jnp.concatenate([m[cut] for m in norms], axis=0).astype(BF16)

    for j in range(4):
        slab(j, core, ve_own if j < 2 else vl_own)
        slab(j, other, ve_sib if j < 2 else vl_sib)
    arrived[1].wait()
    tiles = [(wa, n * 256, min(256, MAIN - n * 256), n * 256) for n in range(-(-MAIN // 256))]
    tiles += [(wb, 128 + n * 256, 256, MAIN + n * 256) for n in range((3 * D - MAIN) // 256)]
    for w, at, width, to in tiles:
        if to == MAIN:
            arrived[2].wait()
        made = jnp.dot(normed[...], w[:, at : at + width], preferred_element_type=F32)
        packed[:, to : to + width] = made.astype(BF16)
    arrived[3].wait()
    for half in range(2):
        for g in (2 * half, 2 * half + 1):
            rows = slice(g * 128, g * 128 + 128)
            vt[g] = jnp.transpose(packed[rows, 2 * D :])
            lanes = slice((g % 2) * 128, (g % 2) * 128 + 128)
            mix_t[half, :, lanes] = attend(
                lambda lo, hi: packed[rows, lo:hi],
                lambda lo, hi: packed[rows, D + lo : D + hi],
                lambda lo, hi: vt[g, lo:hi, :],
                HEADS,
                lambda s: s + bias[...],
                held.at[g],
                soft.at[g],
                inverse.at[g],
            ).astype(BF16)
        project(half, 640 + D)
    alive = jnp.where(t < cameras, 1.0, 0.0)
    last_gate = mod[5:6, :]
    for i in range(8):
        target = lax.rem(t + i, 8)
        pair = lax.rem(target, 2) * 4 + target // 2
        for g in range(4):
            rows = pl.ds(pl.multiple_of(g * 128 + pair * 16, 16), 16)
            done = (mid[rows, :].astype(F32) + last_gate * proj[rows, :]) * alive
            for f in range(2):
                outs[i][f, g * 8 : g * 8 + 8, :] = done[f * 8 : f * 8 + 8].astype(BF16)


def temporal(info, rays, ray_weight, mod, ve_own, ve_sib, vl_own, vl_sib, mixed_in, g_own, g_sib):
    vmem = pl.BlockSpec(memory_space=pltpu.VMEM)
    far = pl.BlockSpec(memory_space=pl.ANY)
    return pl.pallas_call(
        temporal_kernel,
        out_shape=[jax.ShapeDtypeStruct((2, PATCHES, D), BF16)] * 8,
        in_specs=[pl.BlockSpec(memory_space=pltpu.SMEM)] + [vmem] * 15 + [far] * 2,
        out_specs=[vmem] * 8,
        scratch_shapes=[
            pltpu.VMEM((D, MAIN), BF16),
            pltpu.VMEM((D, MAIN), BF16),
            pltpu.VMEM((2, D, TOKENS), BF16),
            pltpu.VMEM((2 * TOKENS, D), F32),
            pltpu.VMEM((2 * TOKENS, D), BF16),
            pltpu.VMEM((2 * TOKENS, D), BF16),
            pltpu.VMEM((2 * TOKENS, 3 * D), BF16),
            pltpu.VMEM((4, D, 128), BF16),
            pltpu.VMEM((128, 128), F32),
            pltpu.VMEM((4, HEADS, 128, 128), F32),
            pltpu.VMEM((4, HEADS, 128, 128), BF16),
            pltpu.VMEM((4, HEADS, 1, 128), F32),
            pltpu.SemaphoreType.DMA((4,)),
        ],
        compiler_params=pltpu.CompilerParams(vmem_limit_bytes=VMEM_LIMIT),
        cost_estimate=SMALL,
    )(info, rays, ray_weight, mod, ve_own, ve_sib, vl_own, vl_sib, *mixed_in, g_own, g_sib)


def join_kernel(info, *refs):
    pieces, out = refs[:8], refs[8]
    t = info[0]
    for i, piece in enumerate(pieces):
        source = lax.rem(t + 8 - i, 8)
        out[:, pl.ds(pl.multiple_of(source * PATCHES, PATCHES), PATCHES), :] = piece[...]


def join(info, pieces):
    vmem = pl.BlockSpec(memory_space=pltpu.VMEM)
    return pl.pallas_call(
        join_kernel,
        out_shape=jax.ShapeDtypeStruct((2, TOKENS, D), BF16),
        in_specs=[pl.BlockSpec(memory_space=pltpu.SMEM)] + [vmem] * 8,
        out_specs=vmem,
        compiler_params=pltpu.CompilerParams(vmem_limit_bytes=VMEM_LIMIT),
        cost_estimate=SMALL,
    )(info, *pieces)


def on_device(
    video,
    cameras,
    rays,
    ray_weight,
    modulation,
    spatial_qkv,
    spatial_out,
    temporal_qkv,
    temporal_out,
):
    t = lax.axis_index("tm")
    clip = lax.axis_index("clip")
    x, core = t // 2, t % 2
    z, y = clip // YS, clip % YS
    info = jnp.stack([t, core, x, cameras[0], z, y]).astype(jnp.int32)
    mod = modulation[0].astype(F32)
    rays_t = rays.T
    zgroups = [[zz * YS + yy for zz in range(ZS)] for yy in range(YS)]

    def columns(a, start, size):
        return lax.dynamic_slice_in_dim(a, start, size, axis=1)

    zgroups = [[zz * YS + yy for zz in range(ZS)] for yy in range(YS)]
    ygroups = [[zz * YS + yy for yy in range(YS)] for zz in range(ZS)]

    def spread(a, groups):
        copies = jnp.broadcast_to(a[None], (len(groups[0]),) + a.shape)
        return lax.all_to_all(copies, "clip", 0, 0, axis_index_groups=groups, tiled=True).reshape(-1, a.shape[1])

    k = np.arange(D)
    goes = k // (ZS * ROWS) * ROWS + k // ROWS % ZS * (YS * ROWS) + k % ROWS
    order = jnp.asarray(k[:, None] == goes[None, :], BF16)

    x_up, x_down = x_send(video, 1), x_send(video, -1)

    g = columns(jnp.concatenate([temporal_qkv, spatial_out, temporal_out], axis=1), core * MAIN_STEP, MAIN)
    g = [g] + [y_send(g, s) for s in range(1, YS)]

    q, k, v = (columns(spatial_qkv, n * D + x * GROUP, GROUP) for n in range(3))
    gap = jnp.zeros((ROWS, 96), BF16)
    w = jnp.concatenate([q, v[:, 256:], gap[:, :64], k, gap, v[:, :256]], axis=1)
    w = jnp.broadcast_to(columns(w, core * HALF, HALF)[None], (ZS, ROWS, HALF))
    g[1], g[2], g[3], w = lax.optimization_barrier((g[1], g[2], g[3], w))
    g = in_order(g, y)
    g_own = lax.all_gather(g, "clip", axis=0, tiled=True, axis_index_groups=zgroups)
    token = g[0:16, 0:128]
    w = lax.all_to_all(w, "clip", 0, 0, axis_index_groups=zgroups, tiled=True).reshape(-1, HALF)

    token, w, x_up, x_down = lax.optimization_barrier((token, w, x_up, x_down))
    w_up, w_down = y_send(w, 1), y_send(w, -1)
    far_0, far_1 = x_send(x_up[0:1], 1), x_send(x_down[1:2], -1)
    half = ZS * ROWS // 2
    w_far_up = y_send(w_up[:half], 1)
    w_far_down = y_send(w_down[half:], -1)
    w_far_up, w_far_down, far_0, far_1 = lax.optimization_barrier((w_far_up, w_far_down, far_0, far_1))
    w_own = collect(info, [w, w_up, w_down, w_far_up, w_far_down], order, token)
    w_sib = core_swap(w_own)

    early, kept_e = spatial((2, 2), info, rays_t, ray_weight, mod, w_own, w_sib, [video, x_down])
    ve_sib = core_swap(kept_e[1])
    *mixed, kept_l = spatial(
        (1, 1, 2), info, rays_t, ray_weight, mod, w_own, w_sib, [far_0, far_1, x_up], [early]
    )
    mixed = [mixed[0]] + [tm_send(mixed[i], i) for i in range(1, 8)]
    vl_sib = core_swap(kept_l[1])
    g_own, vl_sib, mixed[1:5] = lax.optimization_barrier((g_own, vl_sib, mixed[1:5]))
    g_sib = core_swap(g_own)

    result = temporal(
        info, rays_t, ray_weight, mod, kept_e[0], ve_sib, kept_l[0], vl_sib, mixed, g_own, g_sib
    )
    return join(info, [result[0]] + [tm_send(result[i], i) for i in range(1, 8)])


def solution(mesh):
    placed = (
        P("tm", "clip", None),
        P("clip"),
        P(None, "clip"),
        P(),
        P("clip", None, None),
        P("clip", None),
        P("clip", None),
        P("clip", None),
        P("clip", None),
    )
    return jax.shard_map(
        on_device, mesh=mesh, in_specs=placed, out_specs=P("tm", "clip", None), check_vma=False
    )
```

```python
import functools

import jax
import jax.numpy as jnp
import numpy as np
from jax import lax
from jax.experimental import pallas as pl
from jax.experimental.pallas import tpu as pltpu
from jax.sharding import PartitionSpec as P

D = 1152
HEAD = 72
HEADS = 16
PATCHES = 32
TOKENS = 256
ROWS = 36
XS = 4
ZS = 8
YS = 4
GROUP_HEADS = HEADS // XS
GROUP = GROUP_HEADS * HEAD
PAD = 384
HALF = 512
MAIN = 2944
MAIN_STEP = 2816
EPS = 1e-6
SOFT = HEAD ** (-0.5) * 1.4426950408889634
F32 = jnp.float32
BF16 = jnp.bfloat16
VMEM_LIMIT = 52 * 1024 * 1024
SMALL = pl.CostEstimate(flops=1000, bytes_accessed=1000, transcendentals=0)


def z_send(a, s):
    pairs = [(z * YS + y, (z + s) % ZS * YS + y) for z in range(ZS) for y in range(YS)]
    return lax.ppermute(a, "clip", pairs)


def y_send(a, s):
    pairs = [(z * YS + y, z * YS + (y + s) % YS) for z in range(ZS) for y in range(YS)]
    return lax.ppermute(a, "clip", pairs)


def x_send(a, s):
    pairs = [(x * 2 + c, (x + s) % XS * 2 + c) for x in range(XS) for c in range(2)]
    return lax.ppermute(a, "tm", pairs)


def core_swap(a):
    return lax.ppermute(a, "tm", [(t, t ^ 1) for t in range(2 * XS)])


def tm_send(a, s):
    return lax.ppermute(a, "tm", [(t, (t + s) % (2 * XS)) for t in range(2 * XS)])


def in_order(pieces, me):
    n = len(pieces)
    back = pieces[::-1]
    both = jnp.stack(back + back[:-1])
    picked = lax.dynamic_slice_in_dim(both, n - 1 - me, n, axis=0)
    return picked.reshape(-1, pieces[0].shape[-1])


def attend(queries, keys, values_t, heads, masked, held, soft, inverse):
    for h in range(heads):
        first, last = h * HEAD, h * HEAD + HEAD - 1
        lo, hi = first // 128 * 128, last // 128 * 128 + 128
        lane = lax.broadcasted_iota(jnp.int32, (1, hi - lo), 1) + lo
        own = jnp.logical_and(lane >= first, lane <= last)
        q = jnp.where(own, queries(lo, hi), jnp.zeros((), BF16))
        held[h] = lax.dot_general(keys(lo, hi), q, (((1,), (1,)), ((), ())), preferred_element_type=F32)
    for h in range(heads):
        s = masked(held[h])
        m = jnp.max(s, axis=0, keepdims=True)
        e = jnp.exp2((s - m) * SOFT)
        inverse[h] = 1.0 / jnp.sum(e, axis=0, keepdims=True)
        soft[h] = e.astype(BF16)
    outs = []
    for h in range(heads):
        first = h * HEAD
        start = first // 16 * 16
        o = jnp.dot(values_t(start, start + 80), soft[h], preferred_element_type=F32) * inverse[h]
        outs.append(o[first - start : first - start + HEAD])
    return jnp.concatenate(outs, axis=0)


def normalize(h, scale, shift):
    center = jnp.mean(h, axis=-1, keepdims=True)
    d = h - center
    spread = jnp.mean(d * d, axis=-1, keepdims=True)
    return (d * lax.rsqrt(spread + EPS) * scale + shift).astype(BF16)


def ray_sum(rays, weight):
    total = rays[:, 0:1] * weight[0:1, :]
    for k in range(1, 6):
        total += rays[:, k : k + 1] * weight[k : k + 1, :]
    return total


def spatial_kernel(parts, *refs):
    info, rays, ray_weight, mod, w_own, w_sib = refs[:6]
    videos = refs[6 : 6 + len(parts)]
    refs = refs[6 + len(parts) :]
    out, kept = refs[:2]
    refs = refs[2:]
    ray, wp, sems, normed, packed, vt, of, held, soft, inverse = refs
    t, core, cameras = info[0], info[1], info[3]

    def copies(left, right):
        return [
            pltpu.make_async_copy(left, wp.at[:, 0:HALF], sems.at[0]),
            pltpu.make_async_copy(right, wp.at[:, HALF:], sems.at[1]),
        ]

    @pl.when(core == 0)
    def _():
        for copy in copies(w_own, w_sib):
            copy.start()

    @pl.when(core == 1)
    def _():
        for copy in copies(w_sib, w_own):
            copy.start()

    ray[...] = ray_sum(rays[...], ray_weight[...])
    scale = 1.0 + mod[1:2, :]
    shift = mod[0:1, :]
    alive = lax.broadcasted_iota(jnp.int32, (TOKENS, TOKENS), 0) < cameras * PATCHES

    frames = [(v, f) for v, n in zip(videos, parts) for f in range(n)]

    def norm_frame(slot):
        video, frame = frames[slot]
        for r in range(TOKENS // 32):
            rows = slice(r * 32, r * 32 + 32)
            h = video[frame, rows, :].astype(F32) + ray[rows, :]
            normed[slot % 2, rows, :] = normalize(h, scale, shift)

    for who, owner in enumerate((t, t + 1 - 2 * core)):
        mine = pl.ds(pl.multiple_of(owner * PATCHES, PATCHES), PATCHES)
        for slot, (video, frame) in enumerate(frames):
            kept[who, slot] = video[frame, mine, :]
    norm_frame(0)
    for copy in copies(w_own, w_sib):
        copy.wait()
    for slot in range(4):
        turn = slot % 2
        made = jnp.dot(normed[turn], wp[...], preferred_element_type=F32)
        packed[turn] = made[:, : 2 * PAD].astype(BF16)
        vt[turn, 0:256] = jnp.transpose(made[:, 2 * PAD :]).astype(BF16)
        vt[turn, 256:GROUP] = jnp.transpose(made[:, 256:PAD])[32:64].astype(BF16)
        if slot < 3:
            norm_frame(slot + 1)
        of[slot] = attend(
            lambda lo, hi: packed[turn, :, lo:hi],
            lambda lo, hi: packed[turn, :, PAD + lo : PAD + hi],
            lambda lo, hi: vt[turn, lo:hi, :],
            GROUP_HEADS,
            lambda s: jnp.where(alive, s, -1e30),
            held.at[turn],
            soft.at[turn],
            inverse.at[turn],
        )

    block = lax.broadcasted_iota(jnp.int32, (GROUP, 128), 1) // PATCHES
    for i in range(8):
        unit, place = i // 4, i % 4
        made = None
        for f in range(4):
            a = of[f, :, unit * 128 : unit * 128 + 128]
            by = (f - place) * PATCHES % 128
            if by:
                a = pltpu.roll(a, by, 1)
            made = a if made is None else jnp.where(block == f, a, made)
        out[i] = made.astype(BF16)


def spatial(parts, info, rays, ray_weight, mod, w_own, w_sib, videos):
    vmem = pl.BlockSpec(memory_space=pltpu.VMEM)
    far = pl.BlockSpec(memory_space=pl.ANY)
    frames = sum(parts)
    return pl.pallas_call(
        functools.partial(spatial_kernel, parts),
        out_shape=[
            jax.ShapeDtypeStruct((8, GROUP, 128), BF16),
            jax.ShapeDtypeStruct((2, 4, PATCHES, D), BF16),
        ],
        in_specs=[pl.BlockSpec(memory_space=pltpu.SMEM)] + [vmem] * 3 + [far] * 2 + [vmem] * len(parts),
        out_specs=[vmem, vmem],
        scratch_shapes=[
            pltpu.VMEM((TOKENS, D), F32),
            pltpu.VMEM((D, 2 * HALF), BF16),
            pltpu.SemaphoreType.DMA((2,)),
            pltpu.VMEM((2, TOKENS, D), BF16),
            pltpu.VMEM((2, TOKENS, 2 * PAD), BF16),
            pltpu.VMEM((2, GROUP, TOKENS), BF16),
            pltpu.VMEM((4, GROUP, TOKENS), F32),
            pltpu.VMEM((2, GROUP_HEADS, TOKENS, TOKENS), F32),
            pltpu.VMEM((2, GROUP_HEADS, TOKENS, TOKENS), BF16),
            pltpu.VMEM((2, GROUP_HEADS, 1, TOKENS), F32),
        ],
        compiler_params=pltpu.CompilerParams(vmem_limit_bytes=VMEM_LIMIT),
        cost_estimate=pl.CostEstimate(
            flops=frames * 2 * TOKENS * D * 3 * PAD, bytes_accessed=8_000_000, transcendentals=frames * 4 * 65536
        ),
    )(info, rays, ray_weight, mod, w_own, w_sib, *videos)


def ring_rows(info):
    y = info[5]
    span = ZS * ROWS
    far = lax.rem(y + 2, YS) * span
    return [y * span, lax.rem(y + 3, YS) * span, lax.rem(y + 1, YS) * span, far, far + span // 2]


def turn_kernel(info, order, *refs):
    pieces, out, held = refs[:5], refs[6], refs[7]
    for start, piece in zip(ring_rows(info), pieces):
        held[pl.ds(pl.multiple_of(start, 16), piece.shape[0]), :] = piece[...]
    out[...] = jnp.dot(order[...], held[...], preferred_element_type=F32).astype(BF16)


def collect(info, pieces, order, token):
    vmem = pl.BlockSpec(memory_space=pltpu.VMEM)
    width = pieces[0].shape[1]
    return pl.pallas_call(
        turn_kernel,
        out_shape=jax.ShapeDtypeStruct((D, width), BF16),
        in_specs=[pl.BlockSpec(memory_space=pltpu.SMEM)] + [vmem] * 6 + [pl.BlockSpec(memory_space=pl.ANY)],
        out_specs=vmem,
        scratch_shapes=[pltpu.VMEM((D, width), BF16)],
        compiler_params=pltpu.CompilerParams(vmem_limit_bytes=VMEM_LIMIT),
        cost_estimate=SMALL,
    )(info, order, *pieces, token)


def temporal_kernel(*refs):
    info, rays, ray_weight, mod, ve_own, ve_sib, vl_own, vl_sib = refs[:8]
    early, late, g_own, g_sib, outs = refs[8], refs[9], refs[10], refs[11], refs[12:20]
    wa, wb, mix_t, proj, mid, normed, packed, vt, bias, held, soft, inverse, sems = refs[20:]
    t, core, x, cameras = info[0], info[1], info[2], info[3]
    other = 1 - core

    def copies(left, right):
        cut = 640
        return [
            pltpu.make_async_copy(right.at[:, cut : cut + D], wb.at[:, cut : cut + D], sems.at[0]),
            pltpu.make_async_copy(left, wa, sems.at[1]),
            pltpu.make_async_copy(right.at[:, 0:cut], wb.at[:, 0:cut], sems.at[2]),
            pltpu.make_async_copy(right.at[:, cut + D :], wb.at[:, cut + D :], sems.at[3]),
        ]

    @pl.when(core == 0)
    def _():
        for copy in copies(g_own, g_sib):
            copy.start()

    @pl.when(core == 1)
    def _():
        for copy in copies(g_sib, g_own):
            copy.start()

    arrived = copies(g_own, g_sib)

    for source in range(8):
        sx, sc = source // 2, source % 2
        both = jnp.concatenate([early[source], late[source]], axis=1).astype(F32)
        if sx:
            both = pltpu.roll(both, sx * 64, 1)
        mix_t[sc, sx * GROUP : sx * GROUP + GROUP, :] = both.astype(BF16)
    key = lax.broadcasted_iota(jnp.int32, (128, 128), 0)
    query = lax.broadcasted_iota(jnp.int32, (128, 128), 1)
    bias[...] = jnp.where(key % 8 == query % 8, 0.0, -1e30)

    def project(half, first):
        rows = slice(half * TOKENS, half * TOKENS + TOKENS)
        dims = (((0,), (0,)), ((), ()))
        w = wb[:, first : first + D]
        proj[rows, :] = lax.dot_general(mix_t[half], w, dims, preferred_element_type=F32)

    arrived[0].wait()
    for half in range(2):
        project(half, 640)

    here = rays[pl.ds(pl.multiple_of(t * PATCHES, PATCHES), PATCHES), :]
    ray = ray_sum(here, ray_weight[...])
    gate, shift, scale = mod[2:3, :], mod[3:4, :], 1.0 + mod[4:5, :]

    def slab(j, which, video):
        pair = which * 4 + lax.rem(x + j, XS)
        middles, norms = [], []
        for f in range(2):
            h = video[2 * (j % 2) + f].astype(F32) + ray
            p = proj[pl.ds(pl.multiple_of(pair * 64 + f * PATCHES, PATCHES), PATCHES), :]
            middle = (h + gate * p).astype(BF16).astype(F32)
            middles.append(middle)
            norms.append(normalize(middle, scale, shift).astype(F32))
        for g in range(4):
            rows = pl.ds(pl.multiple_of(g * 128 + pair * 16, 16), 16)
            cut = slice(g * 8, g * 8 + 8)
            mid[rows, :] = jnp.concatenate([m[cut] for m in middles], axis=0).astype(BF16)
            normed[rows, :] = jnp.concatenate([m[cut] for m in norms], axis=0).astype(BF16)

    for j in range(4):
        slab(j, core, ve_own if j < 2 else vl_own)
        slab(j, other, ve_sib if j < 2 else vl_sib)
    arrived[1].wait()
    tiles = [(wa, n * 256, min(256, MAIN - n * 256), n * 256) for n in range(-(-MAIN // 256))]
    tiles += [(wb, 128 + n * 256, 256, MAIN + n * 256) for n in range((3 * D - MAIN) // 256)]
    for w, at, width, to in tiles:
        if to == MAIN:
            arrived[2].wait()
        made = jnp.dot(normed[...], w[:, at : at + width], preferred_element_type=F32)
        packed[:, to : to + width] = made.astype(BF16)
    arrived[3].wait()
    for half in range(2):
        for g in (2 * half, 2 * half + 1):
            rows = slice(g * 128, g * 128 + 128)
            vt[g] = jnp.transpose(packed[rows, 2 * D :])
            lanes = slice((g % 2) * 128, (g % 2) * 128 + 128)
            mix_t[half, :, lanes] = attend(
                lambda lo, hi: packed[rows, lo:hi],
                lambda lo, hi: packed[rows, D + lo : D + hi],
                lambda lo, hi: vt[g, lo:hi, :],
                HEADS,
                lambda s: s + bias[...],
                held.at[g],
                soft.at[g],
                inverse.at[g],
            ).astype(BF16)
        project(half, 640 + D)
    alive = jnp.where(t < cameras, 1.0, 0.0)
    last_gate = mod[5:6, :]
    for i in range(8):
        target = lax.rem(t + i, 8)
        pair = lax.rem(target, 2) * 4 + target // 2
        for g in range(4):
            rows = pl.ds(pl.multiple_of(g * 128 + pair * 16, 16), 16)
            done = (mid[rows, :].astype(F32) + last_gate * proj[rows, :]) * alive
            for f in range(2):
                outs[i][f, g * 8 : g * 8 + 8, :] = done[f * 8 : f * 8 + 8].astype(BF16)


def temporal(info, rays, ray_weight, mod, ve_own, ve_sib, vl_own, vl_sib, early, late, g_own, g_sib):
    vmem = pl.BlockSpec(memory_space=pltpu.VMEM)
    far = pl.BlockSpec(memory_space=pl.ANY)
    return pl.pallas_call(
        temporal_kernel,
        out_shape=[jax.ShapeDtypeStruct((2, PATCHES, D), BF16)] * 8,
        in_specs=[pl.BlockSpec(memory_space=pltpu.SMEM)] + [vmem] * 9 + [far] * 2,
        out_specs=[vmem] * 8,
        scratch_shapes=[
            pltpu.VMEM((D, MAIN), BF16),
            pltpu.VMEM((D, MAIN), BF16),
            pltpu.VMEM((2, D, TOKENS), BF16),
            pltpu.VMEM((2 * TOKENS, D), F32),
            pltpu.VMEM((2 * TOKENS, D), BF16),
            pltpu.VMEM((2 * TOKENS, D), BF16),
            pltpu.VMEM((2 * TOKENS, 3 * D), BF16),
            pltpu.VMEM((4, D, 128), BF16),
            pltpu.VMEM((128, 128), F32),
            pltpu.VMEM((4, HEADS, 128, 128), F32),
            pltpu.VMEM((4, HEADS, 128, 128), BF16),
            pltpu.VMEM((4, HEADS, 1, 128), F32),
            pltpu.SemaphoreType.DMA((4,)),
        ],
        compiler_params=pltpu.CompilerParams(vmem_limit_bytes=VMEM_LIMIT),
        cost_estimate=SMALL,
    )(info, rays, ray_weight, mod, ve_own, ve_sib, vl_own, vl_sib, early, late, g_own, g_sib)


def join_kernel(info, *refs):
    pieces, out = refs[:8], refs[8]
    t = info[0]
    for i, piece in enumerate(pieces):
        source = lax.rem(t + 8 - i, 8)
        out[:, pl.ds(pl.multiple_of(source * PATCHES, PATCHES), PATCHES), :] = piece[...]


def join(info, pieces):
    vmem = pl.BlockSpec(memory_space=pltpu.VMEM)
    return pl.pallas_call(
        join_kernel,
        out_shape=jax.ShapeDtypeStruct((2, TOKENS, D), BF16),
        in_specs=[pl.BlockSpec(memory_space=pltpu.SMEM)] + [vmem] * 8,
        out_specs=vmem,
        compiler_params=pltpu.CompilerParams(vmem_limit_bytes=VMEM_LIMIT),
        cost_estimate=SMALL,
    )(info, *pieces)


def on_device(
    video,
    cameras,
    rays,
    ray_weight,
    modulation,
    spatial_qkv,
    spatial_out,
    temporal_qkv,
    temporal_out,
):
    t = lax.axis_index("tm")
    clip = lax.axis_index("clip")
    x, core = t // 2, t % 2
    z, y = clip // YS, clip % YS
    info = jnp.stack([t, core, x, cameras[0], z, y]).astype(jnp.int32)
    mod = modulation[0].astype(F32)
    rays_t = rays.T
    zgroups = [[zz * YS + yy for zz in range(ZS)] for yy in range(YS)]

    def columns(a, start, size):
        return lax.dynamic_slice_in_dim(a, start, size, axis=1)

    zgroups = [[zz * YS + yy for zz in range(ZS)] for yy in range(YS)]
    ygroups = [[zz * YS + yy for yy in range(YS)] for zz in range(ZS)]

    def spread(a, groups):
        copies = jnp.broadcast_to(a[None], (len(groups[0]),) + a.shape)
        return lax.all_to_all(copies, "clip", 0, 0, axis_index_groups=groups, tiled=True).reshape(-1, a.shape[1])

    k = np.arange(D)
    goes = k // (ZS * ROWS) * ROWS + k // ROWS % ZS * (YS * ROWS) + k % ROWS
    order = jnp.asarray(k[:, None] == goes[None, :], BF16)

    x_up, x_down = x_send(video, 1), x_send(video, -1)

    g = columns(jnp.concatenate([temporal_qkv, spatial_out, temporal_out], axis=1), core * MAIN_STEP, MAIN)
    g = [g] + [y_send(g, s) for s in range(1, YS)]

    q, k, v = (columns(spatial_qkv, n * D + x * GROUP, GROUP) for n in range(3))
    gap = jnp.zeros((ROWS, 96), BF16)
    w = jnp.concatenate([q, v[:, 256:], gap[:, :64], k, gap, v[:, :256]], axis=1)
    w = jnp.broadcast_to(columns(w, core * HALF, HALF)[None], (ZS, ROWS, HALF))
    g[1], g[2], g[3], w = lax.optimization_barrier((g[1], g[2], g[3], w))
    g = in_order(g, y)
    g_own = lax.all_gather(g, "clip", axis=0, tiled=True, axis_index_groups=zgroups)
    token = g[0:16, 0:128]
    w = lax.all_to_all(w, "clip", 0, 0, axis_index_groups=zgroups, tiled=True).reshape(-1, HALF)

    token, w, x_up, x_down = lax.optimization_barrier((token, w, x_up, x_down))
    w_up, w_down = y_send(w, 1), y_send(w, -1)
    far_0, far_1 = x_send(x_up[0:1], 1), x_send(x_down[1:2], -1)
    half = ZS * ROWS // 2
    w_far_up = y_send(w_up[:half], 1)
    w_far_down = y_send(w_down[half:], -1)
    w_far_up, w_far_down, far_0, far_1 = lax.optimization_barrier((w_far_up, w_far_down, far_0, far_1))
    w_own = collect(info, [w, w_up, w_down, w_far_up, w_far_down], order, token)
    w_sib = core_swap(w_own)

    early, kept_e = spatial((2, 2), info, rays_t, ray_weight, mod, w_own, w_sib, [video, x_down])
    far_0, early = lax.optimization_barrier((far_0, early))
    early = lax.all_to_all(early, "tm", split_axis=0, concat_axis=0, tiled=True)
    ve_sib = core_swap(kept_e[1])
    late, kept_l = spatial((1, 1, 2), info, rays_t, ray_weight, mod, w_own, w_sib, [far_0, far_1, x_up])
    late = lax.all_to_all(late, "tm", split_axis=0, concat_axis=0, tiled=True)
    vl_sib = core_swap(kept_l[1])
    g_own, vl_sib, early = lax.optimization_barrier((g_own, vl_sib, early))
    g_sib = core_swap(g_own)

    result = temporal(
        info, rays_t, ray_weight, mod, kept_e[0], ve_sib, kept_l[0], vl_sib, early, late, g_own, g_sib
    )
    return join(info, [result[0]] + [tm_send(result[i], i) for i in range(1, 8)])


def solution(mesh):
    placed = (
        P("tm", "clip", None),
        P("clip"),
        P(None, "clip"),
        P(),
        P("clip", None, None),
        P("clip", None),
        P("clip", None),
        P("clip", None),
        P("clip", None),
    )
    return jax.shard_map(
        on_device, mesh=mesh, in_specs=placed, out_specs=P("tm", "clip", None), check_vma=False
    )
```

```python
import functools

import jax
import jax.numpy as jnp
import numpy as np
from jax import lax
from jax.experimental import pallas as pl
from jax.experimental.pallas import tpu as pltpu
from jax.sharding import PartitionSpec as P

D = 1152
HEAD = 72
HEADS = 16
PATCHES = 32
TOKENS = 256
ROWS = 36
XS = 4
ZS = 8
YS = 4
GROUP_HEADS = HEADS // XS
GROUP = GROUP_HEADS * HEAD
PAD = 384
HALF = 512
MAIN = 2944
MAIN_STEP = 2816
EPS = 1e-6
SOFT = HEAD ** (-0.5) * 1.4426950408889634
F32 = jnp.float32
BF16 = jnp.bfloat16
VMEM_LIMIT = 52 * 1024 * 1024
SMALL = pl.CostEstimate(flops=1000, bytes_accessed=1000, transcendentals=0)


def z_send(a, s):
    pairs = [(z * YS + y, (z + s) % ZS * YS + y) for z in range(ZS) for y in range(YS)]
    return lax.ppermute(a, "clip", pairs)


def y_send(a, s):
    pairs = [(z * YS + y, z * YS + (y + s) % YS) for z in range(ZS) for y in range(YS)]
    return lax.ppermute(a, "clip", pairs)


def x_send(a, s):
    pairs = [(x * 2 + c, (x + s) % XS * 2 + c) for x in range(XS) for c in range(2)]
    return lax.ppermute(a, "tm", pairs)


def core_swap(a):
    return lax.ppermute(a, "tm", [(t, t ^ 1) for t in range(2 * XS)])


def tm_send(a, s):
    return lax.ppermute(a, "tm", [(t, (t + s) % (2 * XS)) for t in range(2 * XS)])


def in_order(pieces, me):
    n = len(pieces)
    back = pieces[::-1]
    both = jnp.stack(back + back[:-1])
    picked = lax.dynamic_slice_in_dim(both, n - 1 - me, n, axis=0)
    return picked.reshape(-1, pieces[0].shape[-1])


def spread(a, groups):
    copies = jnp.broadcast_to(a[None], (len(groups[0]),) + a.shape)
    return lax.all_to_all(copies, "clip", 0, 0, axis_index_groups=groups, tiled=True).reshape(-1, a.shape[1])


def attend(queries, keys, values_t, heads, masked, held, soft, inverse):
    for h in range(heads):
        first, last = h * HEAD, h * HEAD + HEAD - 1
        lo, hi = first // 128 * 128, last // 128 * 128 + 128
        lane = lax.broadcasted_iota(jnp.int32, (1, hi - lo), 1) + lo
        own = jnp.logical_and(lane >= first, lane <= last)
        q = jnp.where(own, queries(lo, hi), jnp.zeros((), BF16))
        held[h] = lax.dot_general(keys(lo, hi), q, (((1,), (1,)), ((), ())), preferred_element_type=F32)
    for h in range(heads):
        s = masked(held[h])
        m = jnp.max(s, axis=0, keepdims=True)
        e = jnp.exp2((s - m) * SOFT)
        inverse[h] = 1.0 / jnp.sum(e, axis=0, keepdims=True)
        soft[h] = e.astype(BF16)
    outs = []
    for h in range(heads):
        first = h * HEAD
        start = first // 16 * 16
        o = jnp.dot(values_t(start, start + 80), soft[h], preferred_element_type=F32) * inverse[h]
        outs.append(o[first - start : first - start + HEAD])
    return jnp.concatenate(outs, axis=0)


def normalize(h, scale, shift):
    center = jnp.mean(h, axis=-1, keepdims=True)
    d = h - center
    spread = jnp.mean(d * d, axis=-1, keepdims=True)
    return (d * lax.rsqrt(spread + EPS) * scale + shift).astype(BF16)


def ray_sum(rays, weight):
    total = rays[:, 0:1] * weight[0:1, :]
    for k in range(1, 6):
        total += rays[:, k : k + 1] * weight[k : k + 1, :]
    return total


def spatial_kernel(parts, *refs):
    info, rays, ray_weight, mod, w_own, w_sib = refs[:6]
    videos = refs[6 : 6 + len(parts)]
    refs = refs[6 + len(parts) :]
    out, kept = refs[:2]
    refs = refs[2:]
    ray, wp, sems, normed, packed, vt, of, held, soft, inverse = refs
    t, core, cameras = info[0], info[1], info[3]

    def copies(left, right):
        return [
            pltpu.make_async_copy(left, wp.at[:, 0:HALF], sems.at[0]),
            pltpu.make_async_copy(right, wp.at[:, HALF:], sems.at[1]),
        ]

    @pl.when(core == 0)
    def _():
        for copy in copies(w_own, w_sib):
            copy.start()

    @pl.when(core == 1)
    def _():
        for copy in copies(w_sib, w_own):
            copy.start()

    ray[...] = ray_sum(rays[...], ray_weight[...])
    scale = 1.0 + mod[1:2, :]
    shift = mod[0:1, :]
    alive = lax.broadcasted_iota(jnp.int32, (TOKENS, TOKENS), 0) < cameras * PATCHES

    frames = [(v, f) for v, n in zip(videos, parts) for f in range(n)]

    def norm_frame(slot):
        video, frame = frames[slot]
        for r in range(TOKENS // 32):
            rows = slice(r * 32, r * 32 + 32)
            h = video[frame, rows, :].astype(F32) + ray[rows, :]
            normed[slot % 2, rows, :] = normalize(h, scale, shift)

    for who, owner in enumerate((t, t + 1 - 2 * core)):
        mine = pl.ds(pl.multiple_of(owner * PATCHES, PATCHES), PATCHES)
        for slot, (video, frame) in enumerate(frames):
            kept[who, slot] = video[frame, mine, :]
    norm_frame(0)
    for copy in copies(w_own, w_sib):
        copy.wait()
    for slot in range(4):
        turn = slot % 2
        made = jnp.dot(normed[turn], wp[...], preferred_element_type=F32)
        packed[turn] = made[:, : 2 * PAD].astype(BF16)
        vt[turn, 0:256] = jnp.transpose(made[:, 2 * PAD :]).astype(BF16)
        vt[turn, 256:GROUP] = jnp.transpose(made[:, 256:PAD])[32:64].astype(BF16)
        if slot < 3:
            norm_frame(slot + 1)
        of[slot] = attend(
            lambda lo, hi: packed[turn, :, lo:hi],
            lambda lo, hi: packed[turn, :, PAD + lo : PAD + hi],
            lambda lo, hi: vt[turn, lo:hi, :],
            GROUP_HEADS,
            lambda s: jnp.where(alive, s, -1e30),
            held.at[turn],
            soft.at[turn],
            inverse.at[turn],
        )

    block = lax.broadcasted_iota(jnp.int32, (GROUP, 128), 1) // PATCHES
    for i in range(8):
        unit, place = i // 4, i % 4
        made = None
        for f in range(4):
            a = of[f, :, unit * 128 : unit * 128 + 128]
            by = (f - place) * PATCHES % 128
            if by:
                a = pltpu.roll(a, by, 1)
            made = a if made is None else jnp.where(block == f, a, made)
        out[i] = made.astype(BF16)


def spatial(parts, info, rays, ray_weight, mod, w_own, w_sib, videos):
    vmem = pl.BlockSpec(memory_space=pltpu.VMEM)
    far = pl.BlockSpec(memory_space=pl.ANY)
    frames = sum(parts)
    return pl.pallas_call(
        functools.partial(spatial_kernel, parts),
        out_shape=[
            jax.ShapeDtypeStruct((8, GROUP, 128), BF16),
            jax.ShapeDtypeStruct((2, 4, PATCHES, D), BF16),
        ],
        in_specs=[pl.BlockSpec(memory_space=pltpu.SMEM)] + [vmem] * 3 + [far] * 2 + [vmem] * len(parts),
        out_specs=[vmem, vmem],
        scratch_shapes=[
            pltpu.VMEM((TOKENS, D), F32),
            pltpu.VMEM((D, 2 * HALF), BF16),
            pltpu.SemaphoreType.DMA((2,)),
            pltpu.VMEM((2, TOKENS, D), BF16),
            pltpu.VMEM((2, TOKENS, 2 * PAD), BF16),
            pltpu.VMEM((2, GROUP, TOKENS), BF16),
            pltpu.VMEM((4, GROUP, TOKENS), F32),
            pltpu.VMEM((2, GROUP_HEADS, TOKENS, TOKENS), F32),
            pltpu.VMEM((2, GROUP_HEADS, TOKENS, TOKENS), BF16),
            pltpu.VMEM((2, GROUP_HEADS, 1, TOKENS), F32),
        ],
        compiler_params=pltpu.CompilerParams(vmem_limit_bytes=VMEM_LIMIT),
        cost_estimate=pl.CostEstimate(
            flops=frames * 2 * TOKENS * D * 3 * PAD, bytes_accessed=8_000_000, transcendentals=frames * 4 * 65536
        ),
    )(info, rays, ray_weight, mod, w_own, w_sib, *videos)


def ring_rows(info):
    y = info[5]
    span = ZS * ROWS
    far = lax.rem(y + 2, YS) * span
    return [y * span, lax.rem(y + 3, YS) * span, lax.rem(y + 1, YS) * span, far, far + span // 2]


def turn_kernel(info, order, *refs):
    pieces, out, held = refs[:5], refs[6], refs[7]
    for start, piece in zip(ring_rows(info), pieces):
        held[pl.ds(pl.multiple_of(start, 16), piece.shape[0]), :] = piece[...]
    out[...] = jnp.dot(order[...], held[...], preferred_element_type=F32).astype(BF16)


def collect(info, pieces, order, token):
    vmem = pl.BlockSpec(memory_space=pltpu.VMEM)
    width = pieces[0].shape[1]
    return pl.pallas_call(
        turn_kernel,
        out_shape=jax.ShapeDtypeStruct((D, width), BF16),
        in_specs=[pl.BlockSpec(memory_space=pltpu.SMEM)] + [vmem] * 6 + [pl.BlockSpec(memory_space=pl.ANY)],
        out_specs=vmem,
        scratch_shapes=[pltpu.VMEM((D, width), BF16)],
        compiler_params=pltpu.CompilerParams(vmem_limit_bytes=VMEM_LIMIT),
        cost_estimate=SMALL,
    )(info, order, *pieces, token)


def temporal_kernel(*refs):
    info, rays, ray_weight, mod, ve_own, ve_sib, vl_own, vl_sib = refs[:8]
    early, late, g_own, g_sib, outs = refs[8], refs[9], refs[10], refs[11], refs[12:20]
    wa, wb, mix_t, proj, mid, normed, packed, vt, bias, held, soft, inverse, sems = refs[20:]
    t, core, x, cameras = info[0], info[1], info[2], info[3]
    other = 1 - core

    def copies(left, right):
        cut = 640
        return [
            pltpu.make_async_copy(right.at[:, cut : cut + D], wb.at[:, cut : cut + D], sems.at[0]),
            pltpu.make_async_copy(left, wa, sems.at[1]),
            pltpu.make_async_copy(right.at[:, 0:cut], wb.at[:, 0:cut], sems.at[2]),
            pltpu.make_async_copy(right.at[:, cut + D :], wb.at[:, cut + D :], sems.at[3]),
        ]

    @pl.when(core == 0)
    def _():
        for copy in copies(g_own, g_sib):
            copy.start()

    @pl.when(core == 1)
    def _():
        for copy in copies(g_sib, g_own):
            copy.start()

    arrived = copies(g_own, g_sib)

    for source in range(8):
        sx, sc = source // 2, source % 2
        both = jnp.concatenate([early[source], late[source]], axis=1).astype(F32)
        if sx:
            both = pltpu.roll(both, sx * 64, 1)
        mix_t[sc, sx * GROUP : sx * GROUP + GROUP, :] = both.astype(BF16)
    key = lax.broadcasted_iota(jnp.int32, (128, 128), 0)
    query = lax.broadcasted_iota(jnp.int32, (128, 128), 1)
    bias[...] = jnp.where(key % 8 == query % 8, 0.0, -1e30)

    def project(half, first):
        rows = slice(half * TOKENS, half * TOKENS + TOKENS)
        dims = (((0,), (0,)), ((), ()))
        w = wb[:, first : first + D]
        proj[rows, :] = lax.dot_general(mix_t[half], w, dims, preferred_element_type=F32)

    arrived[0].wait()
    for half in range(2):
        project(half, 640)

    here = rays[pl.ds(pl.multiple_of(t * PATCHES, PATCHES), PATCHES), :]
    ray = ray_sum(here, ray_weight[...])
    gate, shift, scale = mod[2:3, :], mod[3:4, :], 1.0 + mod[4:5, :]

    def slab(j, which, video):
        pair = which * 4 + lax.rem(x + j, XS)
        middles, norms = [], []
        for f in range(2):
            h = video[2 * (j % 2) + f].astype(F32) + ray
            p = proj[pl.ds(pl.multiple_of(pair * 64 + f * PATCHES, PATCHES), PATCHES), :]
            middle = (h + gate * p).astype(BF16).astype(F32)
            middles.append(middle)
            norms.append(normalize(middle, scale, shift).astype(F32))
        for g in range(4):
            rows = pl.ds(pl.multiple_of(g * 128 + pair * 16, 16), 16)
            cut = slice(g * 8, g * 8 + 8)
            mid[rows, :] = jnp.concatenate([m[cut] for m in middles], axis=0).astype(BF16)
            normed[rows, :] = jnp.concatenate([m[cut] for m in norms], axis=0).astype(BF16)

    for j in range(4):
        slab(j, core, ve_own if j < 2 else vl_own)
        slab(j, other, ve_sib if j < 2 else vl_sib)
    arrived[1].wait()
    tiles = [(wa, n * 256, min(256, MAIN - n * 256), n * 256) for n in range(-(-MAIN // 256))]
    tiles += [(wb, 128 + n * 256, 256, MAIN + n * 256) for n in range((3 * D - MAIN) // 256)]
    for w, at, width, to in tiles:
        if to == MAIN:
            arrived[2].wait()
        made = jnp.dot(normed[...], w[:, at : at + width], preferred_element_type=F32)
        packed[:, to : to + width] = made.astype(BF16)
    arrived[3].wait()
    for half in range(2):
        for g in (2 * half, 2 * half + 1):
            rows = slice(g * 128, g * 128 + 128)
            vt[g] = jnp.transpose(packed[rows, 2 * D :])
            lanes = slice((g % 2) * 128, (g % 2) * 128 + 128)
            mix_t[half, :, lanes] = attend(
                lambda lo, hi: packed[rows, lo:hi],
                lambda lo, hi: packed[rows, D + lo : D + hi],
                lambda lo, hi: vt[g, lo:hi, :],
                HEADS,
                lambda s: s + bias[...],
                held.at[g],
                soft.at[g],
                inverse.at[g],
            ).astype(BF16)
        project(half, 640 + D)
    alive = jnp.where(t < cameras, 1.0, 0.0)
    last_gate = mod[5:6, :]
    for i in range(8):
        target = lax.rem(t + i, 8)
        pair = lax.rem(target, 2) * 4 + target // 2
        for g in range(4):
            rows = pl.ds(pl.multiple_of(g * 128 + pair * 16, 16), 16)
            done = (mid[rows, :].astype(F32) + last_gate * proj[rows, :]) * alive
            for f in range(2):
                outs[i][f, g * 8 : g * 8 + 8, :] = done[f * 8 : f * 8 + 8].astype(BF16)


def temporal(info, rays, ray_weight, mod, ve_own, ve_sib, vl_own, vl_sib, early, late, g_own, g_sib):
    vmem = pl.BlockSpec(memory_space=pltpu.VMEM)
    far = pl.BlockSpec(memory_space=pl.ANY)
    return pl.pallas_call(
        temporal_kernel,
        out_shape=[jax.ShapeDtypeStruct((2, PATCHES, D), BF16)] * 8,
        in_specs=[pl.BlockSpec(memory_space=pltpu.SMEM)] + [vmem] * 9 + [far] * 2,
        out_specs=[vmem] * 8,
        scratch_shapes=[
            pltpu.VMEM((D, MAIN), BF16),
            pltpu.VMEM((D, MAIN), BF16),
            pltpu.VMEM((2, D, TOKENS), BF16),
            pltpu.VMEM((2 * TOKENS, D), F32),
            pltpu.VMEM((2 * TOKENS, D), BF16),
            pltpu.VMEM((2 * TOKENS, D), BF16),
            pltpu.VMEM((2 * TOKENS, 3 * D), BF16),
            pltpu.VMEM((4, D, 128), BF16),
            pltpu.VMEM((128, 128), F32),
            pltpu.VMEM((4, HEADS, 128, 128), F32),
            pltpu.VMEM((4, HEADS, 128, 128), BF16),
            pltpu.VMEM((4, HEADS, 1, 128), F32),
            pltpu.SemaphoreType.DMA((4,)),
        ],
        compiler_params=pltpu.CompilerParams(vmem_limit_bytes=VMEM_LIMIT),
        cost_estimate=SMALL,
    )(info, rays, ray_weight, mod, ve_own, ve_sib, vl_own, vl_sib, early, late, g_own, g_sib)


def join_kernel(info, *refs):
    pieces, out = refs[:8], refs[8]
    t = info[0]
    for i, piece in enumerate(pieces):
        source = lax.rem(t + 8 - i, 8)
        out[:, pl.ds(pl.multiple_of(source * PATCHES, PATCHES), PATCHES), :] = piece[...]


def join(info, pieces):
    vmem = pl.BlockSpec(memory_space=pltpu.VMEM)
    return pl.pallas_call(
        join_kernel,
        out_shape=jax.ShapeDtypeStruct((2, TOKENS, D), BF16),
        in_specs=[pl.BlockSpec(memory_space=pltpu.SMEM)] + [vmem] * 8,
        out_specs=vmem,
        compiler_params=pltpu.CompilerParams(vmem_limit_bytes=VMEM_LIMIT),
        cost_estimate=SMALL,
    )(info, *pieces)


def on_device(
    video,
    cameras,
    rays,
    ray_weight,
    modulation,
    spatial_qkv,
    spatial_out,
    temporal_qkv,
    temporal_out,
):
    t = lax.axis_index("tm")
    clip = lax.axis_index("clip")
    x, core = t // 2, t % 2
    z, y = clip // YS, clip % YS
    info = jnp.stack([t, core, x, cameras[0], z, y]).astype(jnp.int32)
    mod = modulation[0].astype(F32)
    rays_t = rays.T
    zgroups = [[zz * YS + yy for zz in range(ZS)] for yy in range(YS)]

    def columns(a, start, size):
        return lax.dynamic_slice_in_dim(a, start, size, axis=1)

    zgroups = [[zz * YS + yy for zz in range(ZS)] for yy in range(YS)]
    ygroups = [[zz * YS + yy for yy in range(YS)] for zz in range(ZS)]

    def spread(a, groups):
        copies = jnp.broadcast_to(a[None], (len(groups[0]),) + a.shape)
        return lax.all_to_all(copies, "clip", 0, 0, axis_index_groups=groups, tiled=True).reshape(-1, a.shape[1])

    k = np.arange(D)
    goes = k // (ZS * ROWS) * ROWS + k // ROWS % ZS * (YS * ROWS) + k % ROWS
    order = jnp.asarray(k[:, None] == goes[None, :], BF16)

    x_up, x_down = x_send(video, 1), x_send(video, -1)

    g = columns(jnp.concatenate([temporal_qkv, spatial_out, temporal_out], axis=1), core * MAIN_STEP, MAIN)
    g = in_order([g, y_send(g, 1), y_send(g, 2), y_send(g, 3)], y)
    g_own = lax.all_gather(g, "clip", axis=0, tiled=True, axis_index_groups=zgroups)
    token = g[0:16, 0:128]

    q, k, v = (columns(spatial_qkv, n * D + x * GROUP, GROUP) for n in range(3))
    gap = jnp.zeros((ROWS, 96), BF16)
    w = jnp.concatenate([q, v[:, 256:], gap[:, :64], k, gap, v[:, :256]], axis=1)
    w = spread(columns(w, core * HALF, HALF), zgroups)

    token, w, x_up, x_down = lax.optimization_barrier((token, w, x_up, x_down))
    w_up, w_down = y_send(w, 1), y_send(w, -1)
    far_0, far_1 = x_send(x_up[0:1], 1), x_send(x_down[1:2], -1)
    half = ZS * ROWS // 2
    w_far_up = y_send(w_up[:half], 1)
    w_far_down = y_send(w_down[half:], -1)
    w_far_up, w_far_down, far_0, far_1 = lax.optimization_barrier((w_far_up, w_far_down, far_0, far_1))
    w_own = collect(info, [w, w_up, w_down, w_far_up, w_far_down], order, token)
    w_sib = core_swap(w_own)

    early, kept_e = spatial((2, 2), info, rays_t, ray_weight, mod, w_own, w_sib, [video, x_down])
    far_0, early = lax.optimization_barrier((far_0, early))
    early = lax.all_to_all(early, "tm", split_axis=0, concat_axis=0, tiled=True)
    ve_sib = core_swap(kept_e[1])
    late, kept_l = spatial((1, 1, 2), info, rays_t, ray_weight, mod, w_own, w_sib, [far_0, far_1, x_up])
    late = lax.all_to_all(late, "tm", split_axis=0, concat_axis=0, tiled=True)
    vl_sib = core_swap(kept_l[1])
    g_own, vl_sib, early = lax.optimization_barrier((g_own, vl_sib, early))
    g_sib = core_swap(g_own)

    result = temporal(
        info, rays_t, ray_weight, mod, kept_e[0], ve_sib, kept_l[0], vl_sib, early, late, g_own, g_sib
    )
    return join(info, [result[0]] + [tm_send(result[i], i) for i in range(1, 8)])


def solution(mesh):
    placed = (
        P("tm", "clip", None),
        P("clip"),
        P(None, "clip"),
        P(),
        P("clip", None, None),
        P("clip", None),
        P("clip", None),
        P("clip", None),
        P("clip", None),
    )
    return jax.shard_map(
        on_device, mesh=mesh, in_specs=placed, out_specs=P("tm", "clip", None), check_vma=False
    )
```

```python
import functools

import jax
import jax.numpy as jnp
import numpy as np
from jax import lax
from jax.experimental import pallas as pl
from jax.experimental.pallas import tpu as pltpu
from jax.sharding import PartitionSpec as P

D = 1152
HEAD = 72
HEADS = 16
PATCHES = 32
TOKENS = 256
ROWS = 36
XS = 4
ZS = 8
YS = 4
GROUP_HEADS = HEADS // XS
GROUP = GROUP_HEADS * HEAD
PAD = 384
HALF = 512
MAIN = 2944
MAIN_STEP = 2816
EPS = 1e-6
SOFT = HEAD ** (-0.5) * 1.4426950408889634
F32 = jnp.float32
BF16 = jnp.bfloat16
VMEM_LIMIT = 52 * 1024 * 1024
SMALL = pl.CostEstimate(flops=1000, bytes_accessed=1000, transcendentals=0)


def z_send(a, s):
    pairs = [(z * YS + y, (z + s) % ZS * YS + y) for z in range(ZS) for y in range(YS)]
    return lax.ppermute(a, "clip", pairs)


def y_send(a, s):
    pairs = [(z * YS + y, z * YS + (y + s) % YS) for z in range(ZS) for y in range(YS)]
    return lax.ppermute(a, "clip", pairs)


def x_send(a, s):
    pairs = [(x * 2 + c, (x + s) % XS * 2 + c) for x in range(XS) for c in range(2)]
    return lax.ppermute(a, "tm", pairs)


def core_swap(a):
    return lax.ppermute(a, "tm", [(t, t ^ 1) for t in range(2 * XS)])


def in_order(pieces, me):
    n = len(pieces)
    back = pieces[::-1]
    both = jnp.stack(back + back[:-1])
    picked = lax.dynamic_slice_in_dim(both, n - 1 - me, n, axis=0)
    return picked.reshape(-1, pieces[0].shape[-1])


def spread(a, groups):
    copies = jnp.broadcast_to(a[None], (len(groups[0]),) + a.shape)
    return lax.all_to_all(copies, "clip", 0, 0, axis_index_groups=groups, tiled=True).reshape(-1, a.shape[1])


def attend(queries, keys, values_t, heads, masked, held, soft, inverse):
    for h in range(heads):
        first, last = h * HEAD, h * HEAD + HEAD - 1
        lo, hi = first // 128 * 128, last // 128 * 128 + 128
        lane = lax.broadcasted_iota(jnp.int32, (1, hi - lo), 1) + lo
        own = jnp.logical_and(lane >= first, lane <= last)
        q = jnp.where(own, queries(lo, hi), jnp.zeros((), BF16))
        held[h] = lax.dot_general(keys(lo, hi), q, (((1,), (1,)), ((), ())), preferred_element_type=F32)
    for h in range(heads):
        s = masked(held[h])
        m = jnp.max(s, axis=0, keepdims=True)
        e = jnp.exp2((s - m) * SOFT)
        inverse[h] = 1.0 / jnp.sum(e, axis=0, keepdims=True)
        soft[h] = e.astype(BF16)
    outs = []
    for h in range(heads):
        first = h * HEAD
        start = first // 16 * 16
        o = jnp.dot(values_t(start, start + 80), soft[h], preferred_element_type=F32) * inverse[h]
        outs.append(o[first - start : first - start + HEAD])
    return jnp.concatenate(outs, axis=0)


def normalize(h, scale, shift):
    center = jnp.mean(h, axis=-1, keepdims=True)
    d = h - center
    spread = jnp.mean(d * d, axis=-1, keepdims=True)
    return (d * lax.rsqrt(spread + EPS) * scale + shift).astype(BF16)


def ray_sum(rays, weight):
    total = rays[:, 0:1] * weight[0:1, :]
    for k in range(1, 6):
        total += rays[:, k : k + 1] * weight[k : k + 1, :]
    return total


def spatial_kernel(parts, *refs):
    info, rays, ray_weight, mod, w_own, w_sib = refs[:6]
    videos = refs[6 : 6 + len(parts)]
    refs = refs[6 + len(parts) :]
    out, kept = refs[:2]
    refs = refs[2:]
    ray, wp, sems, normed, packed, vt, of, held, soft, inverse = refs
    t, core, cameras = info[0], info[1], info[3]

    def copies(left, right):
        return [
            pltpu.make_async_copy(left, wp.at[:, 0:HALF], sems.at[0]),
            pltpu.make_async_copy(right, wp.at[:, HALF:], sems.at[1]),
        ]

    @pl.when(core == 0)
    def _():
        for copy in copies(w_own, w_sib):
            copy.start()

    @pl.when(core == 1)
    def _():
        for copy in copies(w_sib, w_own):
            copy.start()

    ray[...] = ray_sum(rays[...], ray_weight[...])
    scale = 1.0 + mod[1:2, :]
    shift = mod[0:1, :]
    alive = lax.broadcasted_iota(jnp.int32, (TOKENS, TOKENS), 0) < cameras * PATCHES

    frames = [(v, f) for v, n in zip(videos, parts) for f in range(n)]

    def norm_frame(slot):
        video, frame = frames[slot]
        for r in range(TOKENS // 32):
            rows = slice(r * 32, r * 32 + 32)
            h = video[frame, rows, :].astype(F32) + ray[rows, :]
            normed[slot % 2, rows, :] = normalize(h, scale, shift)

    for who, owner in enumerate((t, t + 1 - 2 * core)):
        mine = pl.ds(pl.multiple_of(owner * PATCHES, PATCHES), PATCHES)
        for slot, (video, frame) in enumerate(frames):
            kept[who, slot] = video[frame, mine, :]
    norm_frame(0)
    for copy in copies(w_own, w_sib):
        copy.wait()
    for slot in range(4):
        turn = slot % 2
        made = jnp.dot(normed[turn], wp[...], preferred_element_type=F32)
        packed[turn] = made[:, : 2 * PAD].astype(BF16)
        vt[turn, 0:256] = jnp.transpose(made[:, 2 * PAD :]).astype(BF16)
        vt[turn, 256:GROUP] = jnp.transpose(made[:, 256:PAD])[32:64].astype(BF16)
        if slot < 3:
            norm_frame(slot + 1)
        of[slot] = attend(
            lambda lo, hi: packed[turn, :, lo:hi],
            lambda lo, hi: packed[turn, :, PAD + lo : PAD + hi],
            lambda lo, hi: vt[turn, lo:hi, :],
            GROUP_HEADS,
            lambda s: jnp.where(alive, s, -1e30),
            held.at[turn],
            soft.at[turn],
            inverse.at[turn],
        )

    block = lax.broadcasted_iota(jnp.int32, (GROUP, 128), 1) // PATCHES
    for i in range(8):
        unit, place = i // 4, i % 4
        made = None
        for f in range(4):
            a = of[f, :, unit * 128 : unit * 128 + 128]
            by = (f - place) * PATCHES % 128
            if by:
                a = pltpu.roll(a, by, 1)
            made = a if made is None else jnp.where(block == f, a, made)
        out[i] = made.astype(BF16)


def spatial(parts, info, rays, ray_weight, mod, w_own, w_sib, videos):
    vmem = pl.BlockSpec(memory_space=pltpu.VMEM)
    far = pl.BlockSpec(memory_space=pl.ANY)
    frames = sum(parts)
    return pl.pallas_call(
        functools.partial(spatial_kernel, parts),
        out_shape=[
            jax.ShapeDtypeStruct((8, GROUP, 128), BF16),
            jax.ShapeDtypeStruct((2, 4, PATCHES, D), BF16),
        ],
        in_specs=[pl.BlockSpec(memory_space=pltpu.SMEM)] + [vmem] * 3 + [far] * 2 + [vmem] * len(parts),
        out_specs=[vmem, vmem],
        scratch_shapes=[
            pltpu.VMEM((TOKENS, D), F32),
            pltpu.VMEM((D, 2 * HALF), BF16),
            pltpu.SemaphoreType.DMA((2,)),
            pltpu.VMEM((2, TOKENS, D), BF16),
            pltpu.VMEM((2, TOKENS, 2 * PAD), BF16),
            pltpu.VMEM((2, GROUP, TOKENS), BF16),
            pltpu.VMEM((4, GROUP, TOKENS), F32),
            pltpu.VMEM((2, GROUP_HEADS, TOKENS, TOKENS), F32),
            pltpu.VMEM((2, GROUP_HEADS, TOKENS, TOKENS), BF16),
            pltpu.VMEM((2, GROUP_HEADS, 1, TOKENS), F32),
        ],
        compiler_params=pltpu.CompilerParams(vmem_limit_bytes=VMEM_LIMIT),
        cost_estimate=pl.CostEstimate(
            flops=frames * 2 * TOKENS * D * 3 * PAD, bytes_accessed=8_000_000, transcendentals=frames * 4 * 65536
        ),
    )(info, rays, ray_weight, mod, w_own, w_sib, *videos)


def ring_rows(info):
    y = info[5]
    span = ZS * ROWS
    far = lax.rem(y + 2, YS) * span
    return [y * span, lax.rem(y + 3, YS) * span, lax.rem(y + 1, YS) * span, far, far + span // 2]


def turn_kernel(info, order, *refs):
    pieces, out, held = refs[:5], refs[6], refs[7]
    for start, piece in zip(ring_rows(info), pieces):
        held[pl.ds(pl.multiple_of(start, 16), piece.shape[0]), :] = piece[...]
    out[...] = jnp.dot(order[...], held[...], preferred_element_type=F32).astype(BF16)


def collect(info, pieces, order, token):
    vmem = pl.BlockSpec(memory_space=pltpu.VMEM)
    width = pieces[0].shape[1]
    return pl.pallas_call(
        turn_kernel,
        out_shape=jax.ShapeDtypeStruct((D, width), BF16),
        in_specs=[pl.BlockSpec(memory_space=pltpu.SMEM)] + [vmem] * 6 + [pl.BlockSpec(memory_space=pl.ANY)],
        out_specs=vmem,
        scratch_shapes=[pltpu.VMEM((D, width), BF16)],
        compiler_params=pltpu.CompilerParams(vmem_limit_bytes=VMEM_LIMIT),
        cost_estimate=SMALL,
    )(info, order, *pieces, token)


def temporal_kernel(*refs):
    info, rays, ray_weight, mod, ve_own, ve_sib, vl_own, vl_sib = refs[:8]
    early, late, g_own, g_sib, out = refs[8:13]
    wa, wb, mix_t, proj, mid, normed, packed, vt, bias, held, soft, inverse, sems = refs[13:]
    t, core, x, cameras = info[0], info[1], info[2], info[3]
    other = 1 - core

    def copies(left, right):
        cut = 640
        return [
            pltpu.make_async_copy(right.at[:, cut : cut + D], wb.at[:, cut : cut + D], sems.at[0]),
            pltpu.make_async_copy(left, wa, sems.at[1]),
            pltpu.make_async_copy(right.at[:, 0:cut], wb.at[:, 0:cut], sems.at[2]),
            pltpu.make_async_copy(right.at[:, cut + D :], wb.at[:, cut + D :], sems.at[3]),
        ]

    @pl.when(core == 0)
    def _():
        for copy in copies(g_own, g_sib):
            copy.start()

    @pl.when(core == 1)
    def _():
        for copy in copies(g_sib, g_own):
            copy.start()

    arrived = copies(g_own, g_sib)

    for source in range(8):
        sx, sc = source // 2, source % 2
        both = jnp.concatenate([early[source], late[source]], axis=1).astype(F32)
        if sx:
            both = pltpu.roll(both, sx * 64, 1)
        mix_t[sc, sx * GROUP : sx * GROUP + GROUP, :] = both.astype(BF16)
    key = lax.broadcasted_iota(jnp.int32, (128, 128), 0)
    query = lax.broadcasted_iota(jnp.int32, (128, 128), 1)
    bias[...] = jnp.where(key % 8 == query % 8, 0.0, -1e30)

    def project(half, first):
        rows = slice(half * TOKENS, half * TOKENS + TOKENS)
        dims = (((0,), (0,)), ((), ()))
        w = wb[:, first : first + D]
        proj[rows, :] = lax.dot_general(mix_t[half], w, dims, preferred_element_type=F32)

    arrived[0].wait()
    for half in range(2):
        project(half, 640)

    here = rays[pl.ds(pl.multiple_of(t * PATCHES, PATCHES), PATCHES), :]
    ray = ray_sum(here, ray_weight[...])
    gate, shift, scale = mod[2:3, :], mod[3:4, :], 1.0 + mod[4:5, :]

    def slab(j, which, video):
        pair = which * 4 + lax.rem(x + j, XS)
        middles, norms = [], []
        for f in range(2):
            h = video[2 * (j % 2) + f].astype(F32) + ray
            p = proj[pl.ds(pl.multiple_of(pair * 64 + f * PATCHES, PATCHES), PATCHES), :]
            middle = (h + gate * p).astype(BF16).astype(F32)
            middles.append(middle)
            norms.append(normalize(middle, scale, shift).astype(F32))
        for g in range(4):
            rows = pl.ds(pl.multiple_of(g * 128 + pair * 16, 16), 16)
            cut = slice(g * 8, g * 8 + 8)
            mid[rows, :] = jnp.concatenate([m[cut] for m in middles], axis=0).astype(BF16)
            normed[rows, :] = jnp.concatenate([m[cut] for m in norms], axis=0).astype(BF16)

    for j in range(4):
        slab(j, core, ve_own if j < 2 else vl_own)
        slab(j, other, ve_sib if j < 2 else vl_sib)
    arrived[1].wait()
    tiles = [(wa, n * 256, min(256, MAIN - n * 256), n * 256) for n in range(-(-MAIN // 256))]
    tiles += [(wb, 128 + n * 256, 256, MAIN + n * 256) for n in range((3 * D - MAIN) // 256)]
    for w, at, width, to in tiles:
        if to == MAIN:
            arrived[2].wait()
        made = jnp.dot(normed[...], w[:, at : at + width], preferred_element_type=F32)
        packed[:, to : to + width] = made.astype(BF16)
    arrived[3].wait()
    for half in range(2):
        for g in (2 * half, 2 * half + 1):
            rows = slice(g * 128, g * 128 + 128)
            vt[g] = jnp.transpose(packed[rows, 2 * D :])
            lanes = slice((g % 2) * 128, (g % 2) * 128 + 128)
            mix_t[half, :, lanes] = attend(
                lambda lo, hi: packed[rows, lo:hi],
                lambda lo, hi: packed[rows, D + lo : D + hi],
                lambda lo, hi: vt[g, lo:hi, :],
                HEADS,
                lambda s: s + bias[...],
                held.at[g],
                soft.at[g],
                inverse.at[g],
            ).astype(BF16)
        project(half, 640 + D)
    alive = jnp.where(t < cameras, 1.0, 0.0)
    last_gate = mod[5:6, :]
    for target in range(8):
        pair = target % 2 * 4 + target // 2
        for g in range(4):
            rows = slice(g * 128 + pair * 16, g * 128 + pair * 16 + 16)
            done = (mid[rows, :].astype(F32) + last_gate * proj[rows, :]) * alive
            for f in range(2):
                out[target, f, g * 8 : g * 8 + 8, :] = done[f * 8 : f * 8 + 8].astype(BF16)


def temporal(info, rays, ray_weight, mod, ve_own, ve_sib, vl_own, vl_sib, early, late, g_own, g_sib):
    vmem = pl.BlockSpec(memory_space=pltpu.VMEM)
    far = pl.BlockSpec(memory_space=pl.ANY)
    return pl.pallas_call(
        temporal_kernel,
        out_shape=jax.ShapeDtypeStruct((8, 2, PATCHES, D), BF16),
        in_specs=[pl.BlockSpec(memory_space=pltpu.SMEM)] + [vmem] * 9 + [far] * 2,
        out_specs=vmem,
        scratch_shapes=[
            pltpu.VMEM((D, MAIN), BF16),
            pltpu.VMEM((D, MAIN), BF16),
            pltpu.VMEM((2, D, TOKENS), BF16),
            pltpu.VMEM((2 * TOKENS, D), F32),
            pltpu.VMEM((2 * TOKENS, D), BF16),
            pltpu.VMEM((2 * TOKENS, D), BF16),
            pltpu.VMEM((2 * TOKENS, 3 * D), BF16),
            pltpu.VMEM((4, D, 128), BF16),
            pltpu.VMEM((128, 128), F32),
            pltpu.VMEM((4, HEADS, 128, 128), F32),
            pltpu.VMEM((4, HEADS, 128, 128), BF16),
            pltpu.VMEM((4, HEADS, 1, 128), F32),
            pltpu.SemaphoreType.DMA((4,)),
        ],
        compiler_params=pltpu.CompilerParams(vmem_limit_bytes=VMEM_LIMIT),
        cost_estimate=SMALL,
    )(info, rays, ray_weight, mod, ve_own, ve_sib, vl_own, vl_sib, early, late, g_own, g_sib)


def on_device(
    video,
    cameras,
    rays,
    ray_weight,
    modulation,
    spatial_qkv,
    spatial_out,
    temporal_qkv,
    temporal_out,
):
    t = lax.axis_index("tm")
    clip = lax.axis_index("clip")
    x, core = t // 2, t % 2
    z, y = clip // YS, clip % YS
    info = jnp.stack([t, core, x, cameras[0], z, y]).astype(jnp.int32)
    mod = modulation[0].astype(F32)
    rays_t = rays.T
    zgroups = [[zz * YS + yy for zz in range(ZS)] for yy in range(YS)]

    def columns(a, start, size):
        return lax.dynamic_slice_in_dim(a, start, size, axis=1)

    zgroups = [[zz * YS + yy for zz in range(ZS)] for yy in range(YS)]
    ygroups = [[zz * YS + yy for yy in range(YS)] for zz in range(ZS)]

    def spread(a, groups):
        copies = jnp.broadcast_to(a[None], (len(groups[0]),) + a.shape)
        return lax.all_to_all(copies, "clip", 0, 0, axis_index_groups=groups, tiled=True).reshape(-1, a.shape[1])

    k = np.arange(D)
    goes = k // (ZS * ROWS) * ROWS + k // ROWS % ZS * (YS * ROWS) + k % ROWS
    order = jnp.asarray(k[:, None] == goes[None, :], BF16)

    x_up, x_down = x_send(video, 1), x_send(video, -1)

    g = columns(jnp.concatenate([temporal_qkv, spatial_out, temporal_out], axis=1), core * MAIN_STEP, MAIN)
    g = in_order([g, y_send(g, 1), y_send(g, 2), y_send(g, 3)], y)
    g_own = lax.all_gather(g, "clip", axis=0, tiled=True, axis_index_groups=zgroups)
    token = g[0:16, 0:128]

    q, k, v = (columns(spatial_qkv, n * D + x * GROUP, GROUP) for n in range(3))
    gap = jnp.zeros((ROWS, 96), BF16)
    w = jnp.concatenate([q, v[:, 256:], gap[:, :64], k, gap, v[:, :256]], axis=1)
    w = spread(columns(w, core * HALF, HALF), zgroups)

    token, w, x_up, x_down = lax.optimization_barrier((token, w, x_up, x_down))
    w_up, w_down = y_send(w, 1), y_send(w, -1)
    far_0, far_1 = x_send(x_up[0:1], 1), x_send(x_down[1:2], -1)
    half = ZS * ROWS // 2
    w_far_up = y_send(w_up[:half], 1)
    w_far_down = y_send(w_down[half:], -1)
    w_far_up, w_far_down, far_0, far_1 = lax.optimization_barrier((w_far_up, w_far_down, far_0, far_1))
    w_own = collect(info, [w, w_up, w_down, w_far_up, w_far_down], order, token)
    w_sib = core_swap(w_own)

    early, kept_e = spatial((2, 2), info, rays_t, ray_weight, mod, w_own, w_sib, [video, x_down])
    far_0, early = lax.optimization_barrier((far_0, early))
    early = lax.all_to_all(early, "tm", split_axis=0, concat_axis=0, tiled=True)
    ve_sib = core_swap(kept_e[1])
    late, kept_l = spatial((1, 1, 2), info, rays_t, ray_weight, mod, w_own, w_sib, [far_0, far_1, x_up])
    late = lax.all_to_all(late, "tm", split_axis=0, concat_axis=0, tiled=True)
    vl_sib = core_swap(kept_l[1])
    g_own, vl_sib, early = lax.optimization_barrier((g_own, vl_sib, early))
    g_sib = core_swap(g_own)

    result = temporal(
        info, rays_t, ray_weight, mod, kept_e[0], ve_sib, kept_l[0], vl_sib, early, late, g_own, g_sib
    )
    result = lax.all_to_all(result, "tm", split_axis=0, concat_axis=0, tiled=True)
    return jnp.transpose(result, (1, 0, 2, 3)).reshape(2, TOKENS, D)


def solution(mesh):
    placed = (
        P("tm", "clip", None),
        P("clip"),
        P(None, "clip"),
        P(),
        P("clip", None, None),
        P("clip", None),
        P("clip", None),
        P("clip", None),
        P("clip", None),
    )
    return jax.shard_map(
        on_device, mesh=mesh, in_specs=placed, out_specs=P("tm", "clip", None), check_vma=False
    )
```
